32 devices in a mesh: batch: 16 (over z, y, x), tensor: 2 (over core).
Axes of the slice: x: 2, y: 2, z: 4, core: 2. Of those that a mesh axis runs over, the one named last changes fastest.
Arguments:
- inputs: bfloat16 [2, 8192, 768], P(None, ('batch', 'tensor')), may hold values from -6 to 6
- cotangent: bfloat16 [2, 8192, 768], P(None, ('batch', 'tensor')), may hold values from -6 to 6
- lengths: int32 [2, 16, 16], P(None, 'batch'), may hold values from 1 to 384, 512 in all within a row
- owners: int32 [256], replicated, may hold values from 0 to 15, as said below
- vectors: float32 [512, 28], P('batch'), may hold values from -4 to 4
- first_moment: float32 [512, 28], P('batch'), may hold values from -160 to 160
- second_moment: float32 [512, 28], P('batch'), may hold values from 737.28 to 2949.12
- weight_in: bfloat16 [2, 768, 3, 768], P(None, 'batch', None, 'tensor'), may hold values from -0.21875 to 0.21875
- weight_out: bfloat16 [2, 768, 768], P(None, 'tensor', 'batch'), may hold values from -0.875 to 0.875
- weight_up: bfloat16 [2, 768, 3072], P(None, 'batch', 'tensor'), may hold values from -0.21875 to 0.21875
- weight_down: bfloat16 [2, 3072, 768], P(None, 'tensor', 'batch'), may hold values from -0.109375 to 0.109375
- basis_a: bfloat16 [1024, 768], P('batch'), may hold values from -0.21875 to 0.21875
- basis_b: bfloat16 [768, 1024], P('tensor', 'batch'), may hold values from -0.1875 to 0.1875
- norm_gain: float32 [2, 2, 768], replicated, may hold values from 0.5 to 1.5
- norm_bias: float32 [2, 2, 768], replicated, may hold values from -2 to 2
Outputs:
- outputs: bfloat16 [2, 8192, 768], P(None, ('batch', 'tensor'))
- input_grads: float32 [2, 8192, 768], P(None, ('batch', 'tensor'))
- vector_grads: float32 [512, 28], P('batch')
- new_first_moment: float32 [512, 28], P('batch')
- new_second_moment: float32 [512, 28], P('batch')
- new_vectors: float32 [512, 28], P('batch')
- new_vectors_low: bfloat16 [512, 28], P('batch')
The draws below stay inside these ranges and needn't reach their ends.
Inputs may be any that keep to these rules, and one draw needn't show every extreme that they name: Batch index b owns the pieces c with owners[c] = b; none owns more than 32 pieces and some owns exactly 32.
All inputs are finite; a program needn't handle non-finite values.
Results may differ from the reference program's by a relative error of at most 0.039.
Values may be sent and summed in bfloat16 or wider, within the bound.
A program may use at most 192 MiB of HBM per device.

```python
import math
import jax
import jax.numpy as jnp
import numpy as np
from jax import lax

D = 768
HEADS = 12
HDIM = 64
FF = 3072
R = 1024
LAYERS = 2
MICRO = 2
ROW = 512
SEGS = 16
LONGEST = 384
SPANS = 256
STEP = 10
TOKENS = 8192
SPAN = 28
SLOTS = 32
N_BATCH = 16
N_TENSOR = 2


def draw_owners(key, part):
    key = jax.random.fold_in(key, 7)
    first_key, second_key, third_key = jax.random.split(key, 3)
    fullest = jax.random.randint(first_key, (), 0, N_BATCH)
    shuffled = jax.random.permutation(second_key, N_BATCH * SLOTS)
    behind = (shuffled // SLOTS != fullest).astype(jnp.int32)
    ordering = jnp.argsort(behind, stable=True)
    chosen = shuffled[ordering][:SPANS]
    chosen = jax.random.permutation(third_key, chosen)
    return (chosen // SLOTS).astype(jnp.int32)


def block_levels(rng, extent, pieces, low, largest):
    factor_of = 1.0
    for position, parts in pieces:
        heights = jax.random.uniform(jax.random.fold_in(jax.random.fold_in(rng, 6), position), (parts,), jnp.float32, low / len(pieces), largest / len(pieces))
        factor_of = factor_of * jnp.repeat(jnp.exp(heights), extent[position] // parts).reshape((-1,) + (1,) * (len(extent) - 1 - position))
    return factor_of


def split_up(amount, total, limit, slope):
    loads = [(1 << 20) // math.isqrt(rank ** slope) + 1 for rank in range(2, amount + 1)]
    spare, counts = total - limit - (amount - 1), [1] * (amount - 1)
    while spare > 0:
        free = [i for i in range(amount - 1) if counts[i] < limit]
        mass, left = sum([loads[i] for i in free]), spare
        for i in free:
            addition = min(limit - counts[i], max(1, left * loads[i] // mass), spare)
            counts[i] = counts[i] + addition
            spare = spare - addition
    return np.array([limit] + counts)


def ragged(own_key, count, total, most, slope):
    if count == 2:
        one = jax.random.randint(own_key, (), max(1, total - most), min(most, total - 1) + 1)
        return jnp.stack([one, total - one])
    sizes = jnp.asarray(split_up(count, total, most, slope), jnp.int32)
    pairs = (count - 1) // 2
    giver, taker = sizes[1:1 + 2 * pairs:2], sizes[2:2 + 2 * pairs:2]
    slack = jnp.minimum(giver - 1, most - taker)
    passed = jax.random.randint(jax.random.fold_in(own_key, 1), (pairs,), 0, 1 << 20) % (slack + 1)
    sizes = sizes.at[1:1 + 2 * pairs:2].set(giver - passed).at[2:2 + 2 * pairs:2].set(taker + passed)
    return sizes[jax.random.permutation(jax.random.fold_in(own_key, 2), count)]


def scatter_about(rng, shape, deviation, limit, pieces=(), kind=jnp.bfloat16):
    values = deviation * jax.random.normal(rng, shape, jnp.float32)
    if pieces:
        values = values * block_levels(rng, shape, pieces, -0.22, 0.18)
    return jnp.clip(values, -limit, limit).astype(kind)


def setup_inputs(seed: int = 0) -> dict:
    keys = jax.random.split(jax.random.key(seed), 16)
    return {
        "inputs": scatter_about(keys[0], (MICRO, N_BATCH * ROW, D), 1.0, 6.0, ((1, 32),)),
        "cotangent": scatter_about(keys[1], (MICRO, N_BATCH * ROW, D), 1.0, 6.0, ((1, 32),)),
        "lengths": jax.vmap(lambda own: ragged(own, SEGS, ROW, LONGEST, 2))(jax.random.split(keys[2], MICRO * N_BATCH)).reshape((MICRO, N_BATCH, SEGS)).astype(jnp.int32),
        "owners": draw_owners(jax.random.fold_in(keys[15], 71), 0),
        "vectors": scatter_about(keys[4], (N_BATCH * SLOTS, SPAN), 0.7, 4.0, ((0, 16),), jnp.float32),
        "first_moment": scatter_about(keys[5], (N_BATCH * SLOTS, SPAN), (0.3 * TOKENS ** 0.5), 160.0, ((0, 16),), jnp.float32),
        "second_moment": jnp.clip(jnp.exp(math.log(2949.12) - 1.3862944 * jax.random.uniform(keys[6], (N_BATCH * SLOTS, SPAN), jnp.float32) ** block_levels(keys[6], (N_BATCH * SLOTS, SPAN), ((0, 16),), -0.2, 0.2)), 737.28, 2949.12),
        "weight_in": scatter_about(keys[7], (LAYERS, D, 3, D), D ** -0.5, 0.21875, ((1, 16), (3, 2))),
        "weight_out": scatter_about(keys[8], (LAYERS, D, D), (D // 16) ** -0.5, 0.875, ((1, 2), (2, 16))),
        "weight_up": scatter_about(keys[9], (LAYERS, D, FF), D ** -0.5, 0.21875, ((1, 16), (2, 2))),
        "weight_down": scatter_about(keys[10], (LAYERS, FF, D), FF ** -0.5, 0.109375, ((1, 2), (2, 16))),
        "basis_a": scatter_about(keys[11], (R, D), D ** -0.5, 0.21875, ((0, 16),)),
        "basis_b": scatter_about(keys[12], (D, R), R ** -0.5, 0.1875, ((0, 2), (1, 16))),
        "norm_gain": jnp.clip(1.0 + 0.1 * jax.random.normal(keys[13], (LAYERS, 2, D), jnp.float32), 0.5, 1.5),
        "norm_bias": scatter_about(keys[14], (LAYERS, 2, D), 0.3, 2.0, (), jnp.float32),
    }


EPSILON = 1e-05
SCORE_SCALE = 0.125
MASKED_SCORE = -1000000000.0
LEARN_RATE = 0.3
WEIGHT_DECAY = 0.01
FIRST_BETA = 0.5
SECOND_BETA = 0.5
ADAM_EPSILON = 1e-08

@jax.custom_vjp
def low(v):
    return lax.optimization_barrier(v.astype(jnp.bfloat16)).astype(jnp.float32)

@jax.custom_vjp
def low_back(v):
    return v

def low_keep(v):
    return (low(v), None)

def low_pass(kept, grad):
    return (grad,)

def back_keep(v):
    return (v, None)

def back_low(kept, grad):
    return (low(grad),)
low.defvjp(low_keep, low_pass)
low_back.defvjp(back_keep, back_low)

def matmul(left, right):
    return jnp.dot(left, right, precision=lax.Precision.HIGHEST, preferred_element_type=jnp.float32)

def normalize(values, gain_row, offset):
    center = values - lax.optimization_barrier(jnp.mean(values, axis=-1, keepdims=True))
    spread = lax.optimization_barrier(jnp.mean(center * center, axis=-1, keepdims=True))
    return center * lax.rsqrt(spread + EPSILON) * gain_row + offset

def segment_ids(doc_sizes):
    doc_ends = jnp.cumsum(doc_sizes)
    places = jnp.arange(ROW, dtype=jnp.int32)
    return lax.optimization_barrier(jnp.sum((doc_ends[None, :] <= places[:, None]).astype(jnp.int32), axis=1))

def encoder_layer(hidden, trained, frozen, same_doc):
    scale_q, scale_v, bias_q, bias_v = trained
    weight_in, weight_out, weight_up, weight_down, basis_a, basis_b, norm_gains, offsets = frozen
    hidden_low = low(hidden)
    projected = matmul(hidden_low, basis_a.T)
    group_width = D // N_TENSOR
    parts_q = []
    parts_v = []
    for group in range(N_TENSOR):
        shared = low_back(projected)
        rows_b = basis_b[group * group_width:(group + 1) * group_width]
        parts_q.append(low_back(matmul(low(scale_q * shared), rows_b.T)))
        parts_v.append(low_back(matmul(low(scale_v * shared), rows_b.T)))
    adapt_q = jnp.concatenate(parts_q, axis=1)
    adapt_v = jnp.concatenate(parts_v, axis=1)
    frozen_qkv = matmul(hidden_low, weight_in.reshape(D, 3 * D)).reshape(ROW, 3, D)
    query_rows = low(low_back(frozen_qkv[:, 0] + bias_q * adapt_q)).reshape(ROW, HEADS, HDIM)
    key_rows = low(low_back(frozen_qkv[:, 1])).reshape(ROW, HEADS, HDIM)
    value_rows = low(low_back(frozen_qkv[:, 2] + bias_v * adapt_v)).reshape(ROW, HEADS, HDIM)
    scores = jnp.einsum('qhe,khe->hqk', query_rows, key_rows, precision=lax.Precision.HIGHEST) * SCORE_SCALE
    scores = low_back(jnp.where(same_doc[None], scores, MASKED_SCORE))
    chances = low(jax.nn.softmax(scores, axis=-1))
    mixed_rows = jnp.einsum('hqk,khe->qhe', chances, value_rows, precision=lax.Precision.HIGHEST).reshape(ROW, D)
    mixed_rows = low(low_back(mixed_rows))
    branch = low_back(matmul(mixed_rows, weight_out))
    middle = normalize(hidden + branch, norm_gains[0], offsets[0])
    before = low_back(matmul(low(middle), weight_up))
    active = low(jax.nn.gelu(before, approximate=False))
    feed = low_back(matmul(active, weight_down))
    return normalize(middle + feed, norm_gains[1], offsets[1])

def reference(inputs, cotangent, lengths, owners, vectors, first_moment, second_moment, weight_in, weight_out, weight_up, weight_down, basis_a, basis_b, norm_gain, norm_bias):
    span_ids = jnp.arange(SPANS, dtype=jnp.int32)
    same_owner = owners[:, None] == owners[None, :]
    earlier = span_ids[None, :] < span_ids[:, None]
    owner_ranks = lax.optimization_barrier(jnp.sum((same_owner & earlier).astype(jnp.int32), axis=1))
    slot_of = (owners * SLOTS + owner_ranks).astype(jnp.int32)
    flat = vectors[slot_of].reshape(LAYERS, 2 * R + 2 * D)
    params = (flat[:, :R], flat[:, R:2 * R], flat[:, 2 * R:2 * R + D], flat[:, 2 * R + D:])
    layer_weights = []
    for layer_index in range(LAYERS):
        layer_weights.append((weight_in[layer_index].astype(jnp.float32), weight_out[layer_index].astype(jnp.float32), weight_up[layer_index].astype(jnp.float32), weight_down[layer_index].astype(jnp.float32), basis_a.astype(jnp.float32), basis_b.astype(jnp.float32), norm_gain[layer_index], norm_bias[layer_index]))
    rows_in = inputs.reshape(MICRO * N_BATCH, ROW, D)
    rows_back = cotangent.reshape(MICRO * N_BATCH, ROW, D)
    rows_len = lengths.reshape(MICRO * N_BATCH, SEGS)

    def one_row(totals, row_data):
        hidden, upstream, doc_sizes = row_data
        doc_ids = segment_ids(doc_sizes)
        same_doc = doc_ids[:, None] == doc_ids[None, :]

        def forward(start_rows, trained):
            values = start_rows
            for layer_index in range(LAYERS):
                values = encoder_layer(values, tuple((part[layer_index] for part in trained)), layer_weights[layer_index], same_doc)
            return values
        result, pullback = jax.vjp(forward, hidden.astype(jnp.float32), params)
        start_grad, trained_grad = pullback(upstream.astype(jnp.float32))
        totals = jax.tree.map(jnp.add, totals, trained_grad)
        return (totals, (result.astype(jnp.bfloat16), start_grad))
    zeros = jax.tree.map(jnp.zeros_like, params)
    totals, (results, start_grads) = lax.scan(one_row, zeros, (rows_in, rows_back, rows_len))
    grads = jnp.concatenate(list(totals), axis=1).reshape(SPANS, SPAN)
    old = vectors[slot_of]
    new_one = FIRST_BETA * first_moment[slot_of] + (1.0 - FIRST_BETA) * grads
    new_two = SECOND_BETA * second_moment[slot_of] + (1.0 - SECOND_BETA) * grads * grads
    fixed_one = new_one / (1.0 - FIRST_BETA ** STEP)
    fixed_two = new_two / (1.0 - SECOND_BETA ** STEP)
    updated = old - LEARN_RATE * (fixed_one / (jnp.sqrt(fixed_two) + ADAM_EPSILON) + WEIGHT_DECAY * old)

    def place(values):
        return jnp.zeros((N_BATCH * SLOTS, SPAN), jnp.float32).at[slot_of].set(values)
    new_vectors = place(updated)
    return (results.reshape(MICRO, N_BATCH * ROW, D), start_grads.reshape(MICRO, N_BATCH * ROW, D), place(grads), place(new_one), place(new_two), new_vectors, new_vectors.astype(jnp.bfloat16))
```

```python
import functools

import jax
import jax.numpy as jnp
from jax import lax
from jax.experimental import pallas as pl
from jax.experimental.pallas import tpu as pltpu
from jax.sharding import PartitionSpec as P

D = 768
HDIM = 64
R = 1024
LAYERS = 2
STEP = 10
HALF = 384
GROUPS = 16
BLOCKS = 24
CHUNKS = 13
LAG = 2

EPSILON = 1e-05
SCORE_SCALE = 0.125
MASKED_SCORE = -1000000000.0
LEARN_RATE = 0.3
WEIGHT_DECAY = 0.01
FIRST_BETA = 0.5
SECOND_BETA = 0.5
ADAM_EPSILON = 1e-08
MESH = pl.DeviceIdType.MESH

ARRIVALS = ["Si", "Sj", "Sf", "Dj", "Df", "Xo", "Xi", "Xj", "Xf", "Yo", "Yi", "Yj", "Yf", "Dxo", "Dxi", "Dyo", "Dyi"]
SLOT = {name: index for index, name in enumerate(ARRIVALS)}
FROM_SIBLING = len(ARRIVALS)
TO_SIBLING, TO_X, TO_Y, TO_IN, TO_OUT, LOCAL = range(6)
DEPTHS = 7


class Gather:
    def __init__(self, sub, pack_wide, pack, wide, full, send_sem, recv_sem):
        self.sub = sub
        self.pack_wide, self.pack, self.wide, self.full = pack_wide, pack, wide, full
        self.send_sem, self.recv_sem = send_sem, recv_sem
        batch = lax.axis_index("batch")
        self.core = lax.axis_index("tensor")
        group = batch // sub
        self.lane = batch % sub
        z, p = group // 4, group % 4
        inward = 1 - 2 * (z // 2)
        self.middle = ((z + 1) // 2) % 2
        plane_i, plane_j = z + inward, z + 2 * inward
        plane_f = 6 - z - plane_i - plane_j
        self.planes = {"o": z, "i": plane_i, "j": plane_j, "f": plane_f}
        col_x, col_y = p + 1 - 2 * (p % 2), p + 2 - 4 * (p // 2)
        self.cols = {"S": p, "X": col_x, "Y": col_y, "D": 3 - p}
        self.sibling = (batch, 1 - self.core)
        self.to_x = self.device(z, col_x)
        self.to_y = self.device(z, col_y)
        self.to_in = self.device(plane_i, p)
        self.to_out = self.device(plane_f, p)

    def device(self, plane, col):
        return ((plane * 4 + col) * self.sub + self.lane, self.core)

    def barrier(self):
        semaphore = pltpu.get_barrier_semaphore()
        for device in (self.sibling, self.to_x, self.to_y, self.to_in):
            pl.semaphore_signal(semaphore, inc=1, device_id=device, device_id_type=MESH)

        @pl.when(self.middle == 1)
        def _():
            pl.semaphore_signal(semaphore, inc=1, device_id=self.to_out, device_id_type=MESH)
            pl.semaphore_wait(semaphore, 5)

        @pl.when(self.middle == 0)
        def _():
            pl.semaphore_wait(semaphore, 4)

    def rows(self, chunk, half, start, count, blocks=(0, 2)):
        ref, size, base = (self.wide, 64, 0) if chunk == 0 else (self.full, 48, 2 * (chunk - 1))
        first = pl.multiple_of(start * size, 16) if not isinstance(start, int) else start * size
        return ref.at[half, pl.ds(base + blocks[0], blocks[1]), pl.ds(first, count * size)]

    def shard(self, chunk, half, col, plane, blocks=(0, 2)):
        return self.rows(chunk, half, self.planes[plane] * 4 + self.cols[col], 1, blocks)

    def copy(self, chunk, source, target, device, send, slot):
        pltpu.make_async_remote_copy(
            src_ref=source,
            dst_ref=target,
            send_sem=self.send_sem.at[chunk, send],
            recv_sem=self.recv_sem.at[chunk, slot],
            device_id=device,
            device_id_type=MESH,
        ).start()

    def push(self, chunk, col, plane, moves, blocks=(0, 2), sibling=True, source=None):
        region = self.shard(chunk, self.core, col, plane, blocks)
        source = region if source is None else source
        for device, send, slot in moves:
            slot = SLOT[slot] if isinstance(slot, str) else slot
            self.copy(chunk, source, region, device, send, slot)
        if sibling:
            self.copy(chunk, source, region, self.sibling, TO_SIBLING, FROM_SIBLING)

    def take(self, chunk, name):
        blocks = {"x": (0, 1), "y": (1, 1)}.get(name[1:-1], (0, 2))
        region = self.shard(chunk, self.core, name[0], name[-1], blocks)
        pltpu.make_async_remote_copy(
            src_ref=region,
            dst_ref=region,
            send_sem=self.send_sem.at[chunk, TO_X],
            recv_sem=self.recv_sem.at[chunk, SLOT[name]],
            device_id=self.to_x,
            device_id_type=MESH,
        ).wait_recv()

    def when_middle(self, action):
        pl.when(self.middle == 1)(action)

    def when_end(self, action):
        pl.when(self.middle == 0)(action)

    def local(self, chunk):
        source = self.pack_wide if chunk == 0 else self.pack.at[pl.ds(2 * (chunk - 1), 2)]
        return pltpu.make_async_copy(
            source, self.shard(chunk, self.core, "S", "o"), self.send_sem.at[chunk, LOCAL]
        )

    def step(self, chunk, depth):
        to_x, to_y = (self.to_x, TO_X), (self.to_y, TO_Y)
        to_in, to_out = (self.to_in, TO_IN), (self.to_out, TO_OUT)
        if depth == 0:
            source = self.pack_wide if chunk == 0 else self.pack.at[pl.ds(2 * (chunk - 1), 2)]
            arrival = self.middle * SLOT["Si"] + (1 - self.middle) * SLOT["Sf"]
            self.push(chunk, "S", "o", [(*to_in, arrival), (*to_x, "Xo"), (*to_y, "Yo")], source=source)

            @self.when_middle
            def _():
                self.push(chunk, "S", "o", [(*to_out, "Si")], sibling=False, source=source)

            self.local(chunk).start()
        elif depth == 1:
            self.take(chunk, "Si")

            @self.when_middle
            def _():
                self.push(chunk, "S", "i", [(*to_out, "Sj")], sibling=False)
                self.take(chunk, "Sf")
                self.push(chunk, "S", "f", [(*to_in, "Sj"), (*to_x, "Xf"), (*to_y, "Yf")])

            self.push(chunk, "S", "i", [(*to_x, "Xi"), (*to_y, "Yi")])
            self.cross(chunk, "o")
        elif depth == 2:
            self.take(chunk, "Sj")

            @self.when_middle
            def _():
                self.push(chunk, "S", "j", [(*to_out, "Sf")], sibling=False)

            self.push(chunk, "S", "j", [(*to_x, "Xj"), (*to_y, "Yj")])
            self.take(chunk, "Dxo")
            self.take(chunk, "Dyo")

            @self.when_end
            def _():
                self.push(chunk, "D", "o", [(*to_in, "Df")], sibling=False)

            self.push(chunk, "D", "o", [])
            self.cross(chunk, "i")

            @self.when_middle
            def _():
                self.land(chunk, "Xf", "Yf")
        elif depth == 3:
            @self.when_end
            def _():
                self.take(chunk, "Sf")
                self.push(chunk, "S", "f", [(*to_x, "Xf"), (*to_y, "Yf")])

            self.take(chunk, "Dxi")
            self.take(chunk, "Dyi")

            @self.when_middle
            def _():
                self.push(chunk, "D", "i", [(*to_out, "Dj")], sibling=False)
                self.take(chunk, "Df")
                self.push(chunk, "D", "f", [(*to_in, "Dj")])

            self.push(chunk, "D", "i", [])
            self.land(chunk, "Xj", "Yj")
        elif depth == 4:
            self.take(chunk, "Dj")

            @self.when_middle
            def _():
                self.push(chunk, "D", "j", [(*to_out, "Df")], sibling=False)

            self.push(chunk, "D", "j", [])

            @self.when_end
            def _():
                self.land(chunk, "Xf", "Yf")
        elif depth == 5:
            @self.when_end
            def _():
                self.land(chunk, "Df")
        else:
            self.local(chunk).wait()
            whole = self.rows(chunk, 1 - self.core, 0, GROUPS)
            pltpu.make_async_remote_copy(
                src_ref=whole,
                dst_ref=whole,
                send_sem=self.send_sem.at[chunk, TO_SIBLING],
                recv_sem=self.recv_sem.at[chunk, FROM_SIBLING],
                device_id=self.sibling,
                device_id_type=MESH,
            ).wait_recv()

    def cross(self, chunk, plane):
        self.take(chunk, "X" + plane)
        self.push(chunk, "X", plane, [(self.to_y, TO_Y, "Dy" + plane)], (1, 1), sibling=False)
        self.push(chunk, "X", plane, [])
        self.take(chunk, "Y" + plane)
        self.push(chunk, "Y", plane, [(self.to_x, TO_X, "Dx" + plane)], (0, 1), sibling=False)
        self.push(chunk, "Y", plane, [])

    def land(self, chunk, *names):
        for name in names:
            self.take(chunk, name)
            self.push(chunk, name[0], name[1], [])

    def sent(self, chunk, send, shards):
        region = self.rows(chunk, self.core, 0, shards)
        pltpu.make_async_remote_copy(
            src_ref=region,
            dst_ref=region,
            send_sem=self.send_sem.at[chunk, send],
            recv_sem=self.recv_sem.at[chunk, FROM_SIBLING],
            device_id=self.sibling,
            device_id_type=MESH,
        ).wait_send()

    def finish(self):
        for chunk in range(CHUNKS):
            self.sent(chunk, TO_SIBLING, GROUPS)
            self.sent(chunk, TO_X, 5)
            self.sent(chunk, TO_Y, 5)

        @self.when_middle
        def _():
            for chunk in range(CHUNKS):
                self.sent(chunk, TO_IN, 3)
                self.sent(chunk, TO_OUT, 5)

        @self.when_end
        def _():
            for chunk in range(CHUNKS):
                self.sent(chunk, TO_IN, 2)

    def tick(self, number):
        for depth in range(DEPTHS):
            chunk, rest = divmod(number - depth, LAG)
            if rest == 0 and 0 <= chunk < CHUNKS:
                self.step(chunk, depth)


TICKS = LAG * (CHUNKS - 1) + DEPTHS


def gather_kernel(sub, pack_wide, pack, wide, full, send_sem, recv_sem):
    gather = Gather(sub, pack_wide, pack, wide, full, send_sem, recv_sem)
    gather.barrier()
    for number in range(TICKS):
        gather.tick(number)
    gather.finish()


def gather_weights(sub, pack_wide, pack):
    return pl.pallas_call(
        functools.partial(gather_kernel, sub),
        out_shape=(
            jax.ShapeDtypeStruct((2, 2, R, HALF), jnp.bfloat16),
            jax.ShapeDtypeStruct((2, BLOCKS, D, HALF), jnp.bfloat16),
        ),
        in_specs=[pl.BlockSpec(memory_space=pl.ANY)] * 2,
        out_specs=[pl.BlockSpec(memory_space=pl.ANY)] * 2,
        scratch_shapes=[
            pltpu.SemaphoreType.DMA((CHUNKS, 6)),
            pltpu.SemaphoreType.DMA((CHUNKS, len(ARRIVALS) + 1)),
        ],
        compiler_params=pltpu.CompilerParams(collective_id=0, has_side_effects=True),
    )(pack_wide, pack)


def pack_weights(sub, weight_in, weight_out, weight_up, weight_down, basis_a, basis_b):
    core = lax.axis_index("tensor")
    rows_in = weight_in.shape[1]
    blocks = []
    for layer in range(LAYERS):
        ins = [weight_in[layer, :, part] for part in range(3)]
        outs = weight_out[layer].T
        ups = weight_up[layer].reshape(rows_in, 4, HALF)
        downs = weight_down[layer].T.reshape(rows_in, 4, HALF)
        blocks += ins + [outs]
        for part in range(4):
            blocks += [ups[:, part], downs[:, part]]
    pack = jnp.stack(blocks)
    pack_wide = jnp.stack([lax.dynamic_slice_in_dim(basis_a, core * HALF, HALF, 1), basis_b.T])
    if sub > 1:
        group = lax.axis_index("batch") // sub
        pack = lax.all_gather(pack, "batch", axis=1, tiled=True)
        pack = lax.dynamic_slice_in_dim(pack, group * (D // GROUPS), D // GROUPS, 1)
        pack_wide = lax.all_gather(pack_wide, "batch", axis=1, tiled=True)
        pack_wide = lax.dynamic_slice_in_dim(pack_wide, group * (R // GROUPS), R // GROUPS, 1)
    return pack_wide, pack


def normalize(values, gain_row, offset):
    center = values - jnp.mean(values, axis=-1, keepdims=True)
    spread = jnp.mean(center * center, axis=-1, keepdims=True)
    return center * lax.rsqrt(spread + EPSILON) * gain_row + offset


def norm_back(values, gain_row, offset, upstream):
    _, pullback = jax.vjp(lambda argument: normalize(argument, gain_row, offset), values)
    return pullback(upstream)[0]


def gelu_back(before, upstream):
    _, pullback = jax.vjp(lambda argument: jax.nn.gelu(argument, approximate=False), before)
    return pullback(upstream)[0]


def product(left, right, form):
    return jnp.einsum(form, left, right, preferred_element_type=jnp.float32)


def low(values):
    return values.astype(jnp.bfloat16)


def segment_ids(doc_sizes, total_rows):
    doc_ends = jnp.cumsum(doc_sizes)
    places = jnp.arange(total_rows, dtype=jnp.int32)
    return jnp.sum((doc_ends[None, :] <= places[:, None]).astype(jnp.int32), axis=1)


def owner_tables(owners, batch_index, slot_count):
    span_count = owners.shape[0]
    span_ids = jnp.arange(span_count, dtype=jnp.int32)
    same_owner = owners[:, None] == owners[None, :]
    earlier = span_ids[None, :] < span_ids[:, None]
    owner_ranks = jnp.sum((same_owner & earlier).astype(jnp.int32), axis=1)
    slot_of = owners * slot_count + owner_ranks
    own_span = owners == batch_index
    slot_ids = jnp.arange(slot_count, dtype=jnp.int32)
    select = ((owner_ranks[None, :] == slot_ids[:, None]) & own_span[None, :]).astype(jnp.float32)
    filled = jnp.sum(select, axis=1, keepdims=True)
    return (slot_of, select, filled)


def scores_of(query, key, same):
    scores = product(query, key, "qhe,khe->hqk") * SCORE_SCALE
    return jnp.where(same[None], scores, MASKED_SCORE)


def layer_forward(rows, trained, blocks, wide, gains, offsets, same):
    scale_q, scale_v, bias_q, bias_v = trained
    rows_low = low(rows)
    total = rows.shape[0]
    projected = sum(
        product(rows_low[:, h * HALF : (h + 1) * HALF], wide[h, 0], "td,rd->tr") for h in range(2)
    )
    u_q, u_v = low(scale_q * projected), low(scale_v * projected)
    adapt_q = jnp.concatenate([product(u_q, wide[h, 1], "tr,rw->tw") for h in range(2)], 1)
    adapt_v = jnp.concatenate([product(u_v, wide[h, 1], "tr,rw->tw") for h in range(2)], 1)
    frozen = [
        jnp.concatenate([product(rows_low, blocks[h, part], "td,dw->tw") for h in range(2)], 1)
        for part in range(3)
    ]
    query = low(frozen[0] + bias_q * adapt_q).reshape(total, -1, HDIM)
    key = low(frozen[1]).reshape(total, -1, HDIM)
    value = low(frozen[2] + bias_v * adapt_v).reshape(total, -1, HDIM)
    chances = jax.nn.softmax(scores_of(query, key, same), axis=-1)
    mixed = low(product(low(chances), value, "hqk,khe->qhe").reshape(total, D))
    first = rows + sum(
        product(mixed[:, h * HALF : (h + 1) * HALF], blocks[h, 3], "tw,dw->td") for h in range(2)
    )
    middle = normalize(first, gains[0], offsets[0])
    middle_low = low(middle)
    before = [
        [product(middle_low, blocks[h, 4 + 2 * j], "td,df->tf") for j in range(4)] for h in range(2)
    ]
    feed = 0.0
    for h in range(2):
        for j in range(4):
            active = low(jax.nn.gelu(before[h][j], approximate=False))
            feed = feed + product(active, blocks[h, 5 + 2 * j], "tf,df->td")
    second = middle + feed
    result = normalize(second, gains[1], offsets[1])
    return result, (projected, adapt_q, adapt_v, query, key, value, first, before, second)


def layer_backward(upstream, kept, trained, blocks, wide, gains, offsets, same):
    scale_q, scale_v, bias_q, bias_v = trained
    projected, adapt_q, adapt_v, query, key, value, first, before, second = kept
    total = first.shape[0]
    second_grad = norm_back(second, gains[1], offsets[1], upstream)
    feed_grad = low(second_grad)
    middle_grad = second_grad
    for h in range(2):
        for j in range(4):
            active_grad = product(feed_grad, blocks[h, 5 + 2 * j], "td,df->tf")
            before_grad = low(gelu_back(before[h][j], active_grad))
            middle_grad = middle_grad + product(before_grad, blocks[h, 4 + 2 * j], "tf,df->td")
    first_grad = norm_back(first, gains[0], offsets[0], middle_grad)
    branch = low(first_grad)
    mixed_grad = jnp.concatenate([product(branch, blocks[h, 3], "td,dw->tw") for h in range(2)], 1)
    mixed_grad = low(mixed_grad).reshape(total, -1, HDIM)
    chances = jax.nn.softmax(scores_of(query, key, same), axis=-1)
    chance_grad = product(mixed_grad, value, "qhe,khe->hqk")
    inner = jnp.sum(chances * chance_grad, axis=-1, keepdims=True)
    score_grad = low(chances * (chance_grad - inner))
    query_grad = low(product(score_grad, key, "hqk,khe->qhe") * SCORE_SCALE).reshape(total, D)
    key_grad = low(product(score_grad, query, "hqk,qhe->khe") * SCORE_SCALE).reshape(total, D)
    value_grad = low(product(low(chances), mixed_grad, "hqk,qhe->khe")).reshape(total, D)
    query_wide, value_wide = query_grad.astype(jnp.float32), value_grad.astype(jnp.float32)
    back_q, back_v = low(bias_q * query_wide), low(bias_v * value_wide)
    sums_q = sums_v = 0.0
    input_grad = first_grad
    from_basis = [0.0, 0.0]
    for h in range(2):
        part = slice(h * HALF, (h + 1) * HALF)
        from_q = product(back_q[:, part], wide[h, 1], "tw,rw->tr")
        from_v = product(back_v[:, part], wide[h, 1], "tw,rw->tr")
        sums_q = sums_q + jnp.sum(projected * from_q, axis=0)
        sums_v = sums_v + jnp.sum(projected * from_v, axis=0)
        projected_grad = low(scale_q * from_q + scale_v * from_v)
        from_basis = [from_basis[k] + jnp.dot(projected_grad, wide[k, 0], preferred_element_type=jnp.float32) for k in range(2)]
        for number, grad in enumerate((query_grad, key_grad, value_grad)):
            input_grad = input_grad + product(grad[:, part], blocks[h, number], "tw,dw->td")
    input_grad = input_grad + jnp.concatenate(from_basis, 1)
    grads = jnp.concatenate(
        [sums_q, sums_v, jnp.sum(query_wide * adapt_q, axis=0), jnp.sum(value_wide * adapt_v, axis=0)]
    )
    return input_grad, grads


def on_device(
    inputs, cotangent, lengths, owners, vectors, first_moment, second_moment,
    weight_in, weight_out, weight_up, weight_down, basis_a, basis_b, norm_gain, norm_bias,
):
    sub = lax.axis_size("batch") // GROUPS
    core = lax.axis_index("tensor")
    batch_index = lax.axis_index("batch")
    slot_count = vectors.shape[0]
    slot_of, select, filled = owner_tables(owners, batch_index, slot_count)
    all_slots = lax.all_gather(vectors, "batch", axis=0, tiled=True)
    flat = jnp.take(all_slots, slot_of, axis=0).reshape(LAYERS, 2 * R + 2 * D)
    trained = [
        (flat[l, :R], flat[l, R : 2 * R], flat[l, 2 * R : 2 * R + D], flat[l, 2 * R + D :])
        for l in range(LAYERS)
    ]
    pack_wide, pack = pack_weights(sub, weight_in, weight_out, weight_up, weight_down, basis_a, basis_b)
    wide, full = gather_weights(sub, pack_wide, pack)
    swap = functools.partial(lax.all_to_all, axis_name="tensor", tiled=True)
    rows = swap(inputs, split_axis=0, concat_axis=1)[0].astype(jnp.float32)
    upstream = swap(cotangent, split_axis=0, concat_axis=1)[0].astype(jnp.float32)
    ids = segment_ids(lax.dynamic_index_in_dim(lengths[:, 0], core, 0, False), rows.shape[0])
    same = ids[:, None] == ids[None, :]
    kept = []
    for l in range(LAYERS):
        rows, saved = layer_forward(
            rows, trained[l], full[:, 12 * l : 12 * (l + 1)], wide, norm_gain[l], norm_bias[l], same
        )
        kept.append(saved)
    grads = [None] * LAYERS
    for l in reversed(range(LAYERS)):
        upstream, grads[l] = layer_backward(
            upstream, kept[l], trained[l], full[:, 12 * l : 12 * (l + 1)], wide, norm_gain[l], norm_bias[l], same
        )
    results = swap(low(rows)[None], split_axis=1, concat_axis=0)
    input_grads = swap(upstream[None], split_axis=1, concat_axis=0)
    full_grad = lax.psum(jnp.concatenate(grads).reshape(slot_of.shape[0], -1), ("batch", "tensor"))
    own_grad = jnp.dot(
        select, full_grad, precision=lax.Precision.HIGHEST, preferred_element_type=jnp.float32
    )
    new_one = (FIRST_BETA * first_moment + (1.0 - FIRST_BETA) * own_grad) * filled
    new_two = (SECOND_BETA * second_moment + (1.0 - SECOND_BETA) * own_grad * own_grad) * filled
    fixed_one = new_one / (1.0 - FIRST_BETA**STEP)
    fixed_two = new_two / (1.0 - SECOND_BETA**STEP)
    updated = (
        vectors
        - LEARN_RATE * (fixed_one / (jnp.sqrt(fixed_two) + ADAM_EPSILON) + WEIGHT_DECAY * vectors)
    ) * filled
    return (results, input_grads, own_grad, new_one, new_two, updated, low(updated))


def solution(mesh):
    rows_spec = P(None, ("batch", "tensor"), None)
    split = P("batch", None)
    return jax.shard_map(
        on_device,
        mesh=mesh,
        in_specs=(
            rows_spec, rows_spec, P(None, "batch", None), P(), split, split, split,
            P(None, "batch", None, "tensor"), P(None, "tensor", "batch"), P(None, "batch", "tensor"),
            P(None, "tensor", "batch"), split, P("tensor", "batch"), P(), P(),
        ),
        out_specs=(rows_spec, rows_spec, split, split, split, split, split),
        check_vma=False,
    )
```

```python
import functools

import jax
import jax.numpy as jnp
from jax import lax
from jax.experimental import pallas as pl
from jax.experimental.pallas import tpu as pltpu
from jax.sharding import PartitionSpec as P

D = 768
HDIM = 64
R = 1024
LAYERS = 2
STEP = 10
HALF = 384
GROUPS = 16
BLOCKS = 24
CHUNKS = 13
LAG = 2

EPSILON = 1e-05
SCORE_SCALE = 0.125
MASKED_SCORE = -1000000000.0
LEARN_RATE = 0.3
WEIGHT_DECAY = 0.01
FIRST_BETA = 0.5
SECOND_BETA = 0.5
ADAM_EPSILON = 1e-08
MESH = pl.DeviceIdType.MESH

ARRIVALS = ["Si", "Sj", "Sf", "Dj", "Df", "Xo", "Xi", "Xj", "Xf", "Yo", "Yi", "Yj", "Yf", "Dxo", "Dxi", "Dyo", "Dyi"]
SLOT = {name: index for index, name in enumerate(ARRIVALS)}
FROM_SIBLING = len(ARRIVALS)
TO_SIBLING, TO_X, TO_Y, TO_IN, TO_OUT, LOCAL = range(6)
DEPTHS = 7


class Gather:
    def __init__(self, sub, pack_wide, pack, pack_vec, wide, full, vecs, send_sem, recv_sem):
        self.sub = sub
        self.owners = GROUPS * sub
        self.pack_wide, self.pack, self.pack_vec = pack_wide, pack, pack_vec
        self.wide, self.full, self.vecs = wide, full, vecs
        self.send_sem, self.recv_sem = send_sem, recv_sem
        batch = lax.axis_index("batch")
        self.core = lax.axis_index("tensor")
        group = batch // sub
        self.lane = batch % sub
        z, p = group // 4, group % 4
        inward = 1 - 2 * (z // 2)
        self.middle = ((z + 1) // 2) % 2
        plane_i, plane_j = z + inward, z + 2 * inward
        plane_f = 6 - z - plane_i - plane_j
        self.planes = {"o": z, "i": plane_i, "j": plane_j, "f": plane_f}
        col_x, col_y = p + 1 - 2 * (p % 2), p + 2 - 4 * (p // 2)
        self.cols = {"S": p, "X": col_x, "Y": col_y, "D": 3 - p}
        self.sibling = (batch, 1 - self.core)
        self.to_x = self.device(z, col_x)
        self.to_y = self.device(z, col_y)
        self.to_in = self.device(plane_i, p)
        self.to_out = self.device(plane_f, p)

    def device(self, plane, col):
        return ((plane * 4 + col) * self.sub + self.lane, self.core)

    def barrier(self):
        semaphore = pltpu.get_barrier_semaphore()
        for device in (self.sibling, self.to_x, self.to_y, self.to_in):
            pl.semaphore_signal(semaphore, inc=1, device_id=device, device_id_type=MESH)

        @pl.when(self.middle == 1)
        def _():
            pl.semaphore_signal(semaphore, inc=1, device_id=self.to_out, device_id_type=MESH)
            pl.semaphore_wait(semaphore, 5)

        @pl.when(self.middle == 0)
        def _():
            pl.semaphore_wait(semaphore, 4)

    def rows(self, chunk, half, start, count, blocks=(0, 2)):
        if chunk == 0:
            ref, size, base = self.wide, R // GROUPS, 0
        elif chunk == CHUNKS:
            ref, size, base = self.vecs, 16, 0
        else:
            ref, size, base = self.full, D // GROUPS, 2 * (chunk - 1)
        first = pl.multiple_of(start * size, 16) if not isinstance(start, int) else start * size
        return ref.at[half, pl.ds(base + blocks[0], blocks[1]), pl.ds(first, count * size)]

    def shard(self, chunk, half, col, plane, blocks=(0, 2)):
        return self.rows(chunk, half, self.planes[plane] * 4 + self.cols[col], 1, blocks)

    def copy(self, chunk, source, target, device, send, slot):
        pltpu.make_async_remote_copy(
            src_ref=source,
            dst_ref=target,
            send_sem=self.send_sem.at[chunk, send],
            recv_sem=self.recv_sem.at[chunk, slot],
            device_id=device,
            device_id_type=MESH,
        ).start()

    def push(self, chunk, col, plane, moves, blocks=(0, 2), sibling=True, source=None):
        region = self.shard(chunk, self.core, col, plane, blocks)
        source = region if source is None else source
        for device, send, slot in moves:
            slot = SLOT[slot] if isinstance(slot, str) else slot
            self.copy(chunk, source, region, device, send, slot)
        if sibling:
            self.copy(chunk, source, region, self.sibling, TO_SIBLING, FROM_SIBLING)

    def take(self, chunk, name):
        blocks = {"x": (0, 1), "y": (1, 1)}.get(name[1:-1], (0, 2))
        region = self.shard(chunk, self.core, name[0], name[-1], blocks)
        pltpu.make_async_remote_copy(
            src_ref=region,
            dst_ref=region,
            send_sem=self.send_sem.at[chunk, TO_X],
            recv_sem=self.recv_sem.at[chunk, SLOT[name]],
            device_id=self.to_x,
            device_id_type=MESH,
        ).wait_recv()

    def when_middle(self, action):
        pl.when(self.middle == 1)(action)

    def when_end(self, action):
        pl.when(self.middle == 0)(action)

    def source(self, chunk):
        if chunk == 0:
            return self.pack_wide
        return self.pack_vec if chunk == CHUNKS else self.pack.at[pl.ds(2 * (chunk - 1), 2)]

    def local(self, chunk):
        return pltpu.make_async_copy(
            self.source(chunk), self.shard(chunk, self.core, "S", "o"), self.send_sem.at[chunk, LOCAL]
        )

    def step(self, chunk, depth):
        to_x, to_y = (self.to_x, TO_X), (self.to_y, TO_Y)
        to_in, to_out = (self.to_in, TO_IN), (self.to_out, TO_OUT)
        if depth == 0:
            source = self.source(chunk)
            arrival = self.middle * SLOT["Si"] + (1 - self.middle) * SLOT["Sf"]
            self.push(chunk, "S", "o", [(*to_in, arrival), (*to_x, "Xo"), (*to_y, "Yo")], source=source)

            @self.when_middle
            def _():
                self.push(chunk, "S", "o", [(*to_out, "Si")], sibling=False, source=source)

            self.local(chunk).start()
        elif depth == 1:
            self.take(chunk, "Si")

            @self.when_middle
            def _():
                self.push(chunk, "S", "i", [(*to_out, "Sj")], sibling=False)
                self.take(chunk, "Sf")
                self.push(chunk, "S", "f", [(*to_in, "Sj"), (*to_x, "Xf"), (*to_y, "Yf")])

            self.push(chunk, "S", "i", [(*to_x, "Xi"), (*to_y, "Yi")])
            self.cross(chunk, "o")
        elif depth == 2:
            self.take(chunk, "Sj")

            @self.when_middle
            def _():
                self.push(chunk, "S", "j", [(*to_out, "Sf")], sibling=False)

            self.push(chunk, "S", "j", [(*to_x, "Xj"), (*to_y, "Yj")])
            self.take(chunk, "Dxo")
            self.take(chunk, "Dyo")

            @self.when_end
            def _():
                self.push(chunk, "D", "o", [(*to_in, "Df")], sibling=False)

            self.push(chunk, "D", "o", [])
            self.cross(chunk, "i")

            @self.when_middle
            def _():
                self.land(chunk, "Xf", "Yf")
        elif depth == 3:
            @self.when_end
            def _():
                self.take(chunk, "Sf")
                self.push(chunk, "S", "f", [(*to_x, "Xf"), (*to_y, "Yf")])

            self.take(chunk, "Dxi")
            self.take(chunk, "Dyi")

            @self.when_middle
            def _():
                self.push(chunk, "D", "i", [(*to_out, "Dj")], sibling=False)
                self.take(chunk, "Df")
                self.push(chunk, "D", "f", [(*to_in, "Dj")])

            self.push(chunk, "D", "i", [])
            self.land(chunk, "Xj", "Yj")
        elif depth == 4:
            self.take(chunk, "Dj")

            @self.when_middle
            def _():
                self.push(chunk, "D", "j", [(*to_out, "Df")], sibling=False)

            self.push(chunk, "D", "j", [])

            @self.when_end
            def _():
                self.land(chunk, "Xf", "Yf")
        elif depth == 5:
            @self.when_end
            def _():
                self.land(chunk, "Df")
        else:
            self.local(chunk).wait()
            whole = self.rows(chunk, 1 - self.core, 0, GROUPS)
            pltpu.make_async_remote_copy(
                src_ref=whole,
                dst_ref=whole,
                send_sem=self.send_sem.at[chunk, TO_SIBLING],
                recv_sem=self.recv_sem.at[chunk, FROM_SIBLING],
                device_id=self.sibling,
                device_id_type=MESH,
            ).wait_recv()

    def cross(self, chunk, plane):
        self.take(chunk, "X" + plane)
        self.push(chunk, "X", plane, [(self.to_y, TO_Y, "Dy" + plane)], (1, 1), sibling=False)
        self.push(chunk, "X", plane, [])
        self.take(chunk, "Y" + plane)
        self.push(chunk, "Y", plane, [(self.to_x, TO_X, "Dx" + plane)], (0, 1), sibling=False)
        self.push(chunk, "Y", plane, [])

    def land(self, chunk, *names):
        for name in names:
            self.take(chunk, name)
            self.push(chunk, name[0], name[1], [])

    def sent(self, chunk, send, shards):
        region = self.rows(chunk, self.core, 0, shards)
        pltpu.make_async_remote_copy(
            src_ref=region,
            dst_ref=region,
            send_sem=self.send_sem.at[chunk, send],
            recv_sem=self.recv_sem.at[chunk, FROM_SIBLING],
            device_id=self.sibling,
            device_id_type=MESH,
        ).wait_send()

    def finish(self):
        for chunk in range(CHUNKS + 1):
            self.sent(chunk, TO_SIBLING, GROUPS)
            self.sent(chunk, TO_X, 5)
            self.sent(chunk, TO_Y, 5)

        @self.when_middle
        def _():
            for chunk in range(CHUNKS + 1):
                self.sent(chunk, TO_IN, 3)
                self.sent(chunk, TO_OUT, 5)

        @self.when_end
        def _():
            for chunk in range(CHUNKS + 1):
                self.sent(chunk, TO_IN, 2)

    def tick(self, number):
        for depth in range(DEPTHS):
            if number == depth:
                self.step(CHUNKS, depth)
            chunk, rest = divmod(number - depth, LAG)
            if rest == 0 and 0 <= chunk < CHUNKS:
                self.step(chunk, depth)


TICKS = LAG * (CHUNKS - 1) + DEPTHS


def pack_weights(sub, vectors, weight_in, weight_out, weight_up, weight_down, basis_a, basis_b):
    core = lax.axis_index("tensor")
    rows_in = weight_in.shape[1]
    blocks = []
    for layer in range(LAYERS):
        ins = [weight_in[layer, :, part] for part in range(3)]
        outs = weight_out[layer].T
        ups = weight_up[layer].reshape(rows_in, 4, HALF)
        downs = weight_down[layer].T.reshape(rows_in, 4, HALF)
        blocks += ins + [outs]
        for part in range(4):
            blocks += [ups[:, part], downs[:, part]]
    pack = jnp.stack(blocks)
    pack_wide = jnp.stack([lax.dynamic_slice_in_dim(basis_a, core * HALF, HALF, 1), basis_b.T])
    pack_vec = jnp.pad(vectors, ((0, 0), (0, 128 - vectors.shape[1])))
    if sub > 1:
        group = lax.axis_index("batch") // sub
        pack = lax.all_gather(pack, "batch", axis=1, tiled=True)
        pack = lax.dynamic_slice_in_dim(pack, group * (D // GROUPS), D // GROUPS, 1)
        pack_wide = lax.all_gather(pack_wide, "batch", axis=1, tiled=True)
        pack_wide = lax.dynamic_slice_in_dim(pack_wide, group * (R // GROUPS), R // GROUPS, 1)
        pack_vec = lax.all_gather(pack_vec, "batch", axis=0, tiled=True)
        pack_vec = lax.dynamic_slice_in_dim(pack_vec, group * 32, 32, 0)
    return pack_wide, pack, pack_vec.reshape(2, 16, 128)


def mm(left, right):
    return jnp.dot(left, right, preferred_element_type=jnp.float32)


def mm_t(left, right):
    return lax.dot_general(left, right, (((1,), (1,)), ((), ())), preferred_element_type=jnp.float32)


def exact(left, right):
    return jnp.dot(left, right, precision=lax.Precision.HIGHEST, preferred_element_type=jnp.float32)


def low(values):
    return values.astype(jnp.bfloat16)


def normalize(values, gain, offset):
    center = values - jnp.mean(values, axis=-1, keepdims=True)
    spread = jnp.mean(center * center, axis=-1, keepdims=True)
    return center * lax.rsqrt(spread + EPSILON) * gain + offset


def norm_back(values, gain, upstream):
    center = values - jnp.mean(values, axis=-1, keepdims=True)
    spread = jnp.mean(center * center, axis=-1, keepdims=True)
    scale = lax.rsqrt(spread + EPSILON)
    unit = center * scale
    scaled = upstream * gain
    first = jnp.mean(scaled, axis=-1, keepdims=True)
    second = jnp.mean(scaled * unit, axis=-1, keepdims=True)
    return scale * (scaled - first - unit * second)


def gelu_and_slope(values):
    bell = jnp.exp(-0.5 * values * values)
    t = 1.0 / (1.0 + 0.23164190 * jnp.abs(values))
    poly = t * (0.127414796 + t * (-0.142248368 + t * (0.7107068705 + t * (-0.7265760135 + t * 0.5307027145))))
    tail = poly * bell
    share = jnp.where(values < 0, tail, 1.0 - tail)
    return values * share, share + values * (0.3989422804 * bell)


def piece_ranks(col, row, axis):
    count = row.shape[1]
    down = lax.broadcasted_iota(jnp.int32, (count, count), 0)
    across = lax.broadcasted_iota(jnp.int32, (count, count), 1)
    earlier = (down < across) if axis == 0 else (across < down)
    return jnp.sum(((col == row) & earlier).astype(jnp.float32), axis=axis, keepdims=True).astype(jnp.int32)


SPAN_LANES = 896


def lay_out(pieces, span, flat):
    lanes = lax.broadcasted_iota(jnp.int32, (8, 128), 1)
    tiles = [jnp.zeros((8, 128), jnp.float32) for _ in range(SPAN_LANES // 128)]
    for i in range(32):
        tile, offset = divmod(span * i, 128)
        rows = pieces[pl.ds(i, 8, stride=32), :]
        rows = pltpu.roll(rows, offset, 1) if offset else rows
        inside = (lanes >= offset) & (lanes < offset + span)
        tiles[tile] = tiles[tile] + jnp.where(inside, rows, 0.0)
        if offset + span > 128:
            tiles[tile + 1] = tiles[tile + 1] + jnp.where(lanes < offset + span - 128, rows, 0.0)
    for tile, values in enumerate(tiles):
        flat[:, 128 * tile : 128 * (tile + 1)] = values


def cut_up(flat, span, pieces):
    lanes = lax.broadcasted_iota(jnp.int32, (8, 128), 1)
    for i in range(32):
        tile, offset = divmod(span * i, 128)
        rows = flat[:, 128 * tile : 128 * (tile + 1)]
        if offset:
            rows = pltpu.roll(rows, 128 - offset, 1)
        if offset + span > 128:
            after = pltpu.roll(flat[:, 128 * (tile + 1) : 128 * (tile + 2)], 128 - offset, 1)
            rows = jnp.where(lanes < 128 - offset, rows, after)
        pieces[pl.ds(i, 8, stride=32), :] = jnp.where(lanes < span, rows, 0.0)


ROW = 512
SAVES = 13
SEND_INPUT, SEND_COTANGENT, SEND_RESULT = range(3)


def forward_kernel(
    sub, span,
    pack_wide, pack, pack_vec, inputs, cotangent, lengths, owner_col, owner_row, gains, offsets,
    wide, full, upstream, qkv, probs, proj, adapt, sums, slopes, trained, results,
    vecs, pieces, flat, rows_low, rows, wide_v, att_v, ffn_v, qkv_v, probs_v, proj_v, proj_low, adapt_v, mixed, feed,
    sums_v, slopes_v, doc_col, doc_row, result_v,
    send_sem, recv_sem, swap_send, swap_recv, own_sem, load_sem, save_sem,
):
    gather = Gather(sub, pack_wide, pack, pack_vec, wide, full, vecs, send_sem, recv_sem)
    core = gather.core
    half_rows = inputs.shape[1]
    mine = pl.ds(pl.multiple_of(core * half_rows, 16), half_rows)
    other = pl.ds(pl.multiple_of((1 - core) * half_rows, 16), half_rows)

    def swap(number, source, target):
        return pltpu.make_async_remote_copy(
            src_ref=source, dst_ref=target, send_sem=swap_send.at[number], recv_sem=swap_recv.at[number],
            device_id=gather.sibling, device_id_type=MESH,
        )

    def own(number, source, target):
        return pltpu.make_async_copy(source, target, own_sem.at[number])

    gather.barrier()
    swap_in = swap(SEND_INPUT, inputs.at[1 - core], rows_low.at[mine])
    swap_cot = swap(SEND_COTANGENT, cotangent.at[1 - core], upstream.at[mine])
    own_in = own(0, inputs.at[core], rows_low.at[mine])
    own_cot = own(1, cotangent.at[core], upstream.at[mine])
    swap_in.start()
    own_in.start()

    def save(layer, number, source, target):
        copy = pltpu.make_async_copy(source, target, save_sem.at[layer, number])
        copy.start()
        saved.append(copy)
        return copy

    saved = []
    probs_saved = {}

    def load_wide():
        return pltpu.make_async_copy(wide, wide_v, load_sem.at[0])

    def load_att(layer, part):
        pair = pl.ds(12 * layer + 2 * part, 2)
        return pltpu.make_async_copy(full.at[:, pair], att_v.at[:, pl.ds(2 * part, 2)], load_sem.at[1 + part])

    def load_ffn(layer, part):
        pair = pl.ds(12 * layer + 4 + 2 * part, 2)
        return pltpu.make_async_copy(full.at[:, pair], ffn_v.at[part % 2], load_sem.at[3 + part % 2])

    def vector(layer, start, size):
        return trained[layer : layer + 1, start : start + size]

    def documents():
        places_col = lax.broadcasted_iota(jnp.int32, (ROW, 128), 0)
        places_row = lax.broadcasted_iota(jnp.int32, (8, ROW), 1)
        ids_col = jnp.zeros((ROW, 128), jnp.int32)
        ids_row = jnp.zeros((8, ROW), jnp.int32)
        end = jnp.int32(0)
        for number in range(lengths.shape[2]):
            end = end + lengths[core, 0, number]
            ids_col = ids_col + (places_col >= end).astype(jnp.int32)
            ids_row = ids_row + (places_row >= end).astype(jnp.int32)
        doc_col[...] = ids_col
        doc_row[...] = ids_row

    def start_rows():
        own_in.wait()
        swap_in.wait()
        rows[...] = rows_low[...].astype(jnp.float32)

    def vectors_in():
        slot = owner_col[...] * (512 // gather.owners) + piece_ranks(owner_col[...], owner_row[...], 1)
        place = ((slot >> 4) & 1) * 256 + (slot >> 5) * 16 + (slot & 15)
        spots = lax.broadcasted_iota(jnp.int32, (slot.shape[0], 512), 1)
        select = (place == spots).astype(jnp.float32)
        pieces[...] = exact(select, vecs[0].reshape(512, 128))
        lay_out(pieces, span, flat)
        for number in range(8):
            layer, part = divmod(number, 4)
            trained[layer : layer + 1, SPAN_LANES * part : SPAN_LANES * (part + 1)] = flat[number : number + 1, :]

    def project(layer):
        if layer == 0:
            load_wide().wait()
        proj_v[...] = mm_t(rows_low[:, :HALF], wide_v[0, 0]) + mm_t(rows_low[:, HALF:], wide_v[1, 0])
        proj_low[layer] = low(proj_v[...])
        save(layer, 0, proj_low.at[layer], proj.at[layer])

    def frozen(layer, part, half):
        if half == 0:
            load_att(layer, part).wait()
        for number in ((0, 1) if part == 0 else (2,)):
            values = mm(rows_low[...], att_v[half, number])
            if number != 1:
                start = (0, None, 1)[number]
                bias = vector(layer, 2 * R + start * D + half * HALF, HALF)
                scale = vector(layer, start * R, R)
                adapted = mm(low(scale * proj_v[...]), wide_v[half, 1])
                adapt_v[layer, start, :, half * HALF : (half + 1) * HALF] = low(adapted)
                values = values + bias * adapted
            values = low(values)
            for third in range(3):
                qkv_v[layer, 3 * half + third, number] = values[:, 128 * third : 128 * (third + 1)]

    def save_rows(layer):
        save(layer, 1, qkv_v.at[layer], qkv.at[layer])
        save(layer, 2, adapt_v.at[layer], adapt.at[layer])

    def attend(layer, pair):
        if layer > 0:
            probs_saved[layer - 1, pair].wait()
        query = qkv_v[layer, pair, 0].astype(jnp.float32) * SCORE_SCALE
        query_t = low(query.T)
        value_t = low(qkv_v[layer, pair, 2].astype(jnp.float32).T)
        key = qkv_v[layer, pair, 1]
        ids_col = doc_col[...]
        same = jnp.concatenate([ids_col] * 4, axis=1) == doc_row[0:1, :]
        zeros = jnp.zeros((HDIM, ROW), jnp.bfloat16)
        mixed_t = []
        for head in range(2):
            part = slice(head * HDIM, (head + 1) * HDIM)
            masked = [query_t[part], zeros] if head == 0 else [zeros, query_t[part]]
            scores = jnp.where(same, mm(key, jnp.concatenate(masked, axis=0)), MASKED_SCORE)
            raised = jnp.exp(scores - jnp.max(scores, axis=0, keepdims=True))
            chances = low(raised * (1.0 / jnp.sum(raised, axis=0, keepdims=True)))
            probs_v[pair, head] = chances
            mixed_t.append(mm(value_t[part], chances))
        mixed[:, 128 * pair : 128 * (pair + 1)] = low(jnp.concatenate(mixed_t, axis=0).T)
        probs_saved[layer, pair] = save(layer, 3 + pair, probs_v.at[pair], probs.at[layer, pair])

    def attention_out(layer):
        total = rows[...] + mm_t(mixed[:, :HALF], att_v[0, 3]) + mm_t(mixed[:, HALF:], att_v[1, 3])
        sums_v[layer, 0] = total
        save(layer, 9, sums_v.at[layer, 0], sums.at[layer, 0])
        middle = normalize(total, gains[2 * layer : 2 * layer + 1, :], offsets[2 * layer : 2 * layer + 1, :])
        rows[...] = middle
        rows_low[...] = low(middle)

    def feed_forward(layer, part, half):
        if half == 0:
            load_ffn(layer, part).wait()
        before = mm(rows_low[...], ffn_v[part % 2, half, 0])
        active, slope = gelu_and_slope(before)
        slopes_v[layer, part, half] = low(slope)
        term = mm_t(low(active), ffn_v[part % 2, half, 1])
        if part == 0 and half == 0:
            feed[...] = term
        else:
            feed[...] += term

    def layer_out(layer):
        save(layer, 10, slopes_v.at[layer], slopes.at[layer])
        total = rows[...] + feed[...]
        sums_v[layer, 1] = total
        save(layer, 11, sums_v.at[layer, 1], sums.at[layer, 1])
        number = 2 * layer + 1
        values = normalize(total, gains[number : number + 1, :], offsets[number : number + 1, :])
        if layer == LAYERS - 1:
            result_v[...] = low(values)
        else:
            rows[...] = values
            rows_low[...] = low(values)

    def ready(chunk):
        return LAG * chunk + DEPTHS - 1

    queue = []

    def add(tick, task, *arguments):
        queue.append((tick, functools.partial(task, *arguments)))

    add(0, documents)
    add(1, start_rows)
    add(ready(0), vectors_in)
    add(ready(0), project, 0)
    for layer in range(LAYERS):
        first = 1 + 6 * layer
        if layer > 0:
            add(0, project, layer)
        for half in range(2):
            add(ready(first), frozen, layer, 0, half)
        for half in range(2):
            add(ready(first + 1), frozen, layer, 1, half)
        add(0, save_rows, layer)
        for pair in range(6):
            add(0, attend, layer, pair)
        add(0, attention_out, layer)
        for part in range(4):
            for half in range(2):
                add(ready(first + 2 + part), feed_forward, layer, part, half)
        add(0, layer_out, layer)

    costs = {"documents": 1, "start_rows": 1, "vectors_in": 4, "project": 1, "frozen": 2, "save_rows": 0, "attend": 2, "attention_out": 2, "feed_forward": 3, "layer_out": 1}

    ffn_order = [(layer, part) for layer in range(LAYERS) for part in range(4)]
    ffn_started = [0]
    ffn_done = [0]
    att_done = [0]

    def start_loads(number):
        while ffn_started[0] < len(ffn_order) and ffn_started[0] < ffn_done[0] + 2:
            layer, part = ffn_order[ffn_started[0]]
            if ready(3 + 6 * layer + part) > number:
                break
            load_ffn(layer, part).start()
            ffn_started[0] += 1
        for layer in range(LAYERS):
            for part in range(2):
                if (layer, part) in att_started or ready(1 + 6 * layer + part) > number or att_done[0] < layer:
                    continue
                load_att(layer, part).start()
                att_started.add((layer, part))

    att_started = set()
    position = 0
    for number in range(TICKS + 1):
        if number < TICKS:
            gather.tick(number)
        if number == 0:
            swap_cot.start()
            own_cot.start()
        if number == ready(0):
            load_wide().start()
        start_loads(number)
        budget = BUDGET if number < TICKS else 10**6
        while position < len(queue) and queue[position][0] <= number and budget > 0:
            _, task = queue[position]
            name = task.func.__name__
            start_loads(number)
            task()
            if name == "feed_forward" and task.args[2] == 1:
                ffn_done[0] += 1
            if name == "attention_out":
                att_done[0] += 1
            start_loads(number)
            budget -= costs[name]
            position += 1
    assert position == len(queue)

    swap_out = swap(SEND_RESULT, result_v.at[other], results.at[core])
    own_out = own(2, result_v.at[mine], results.at[core])
    swap_out.start()
    own_out.start()
    gather.finish()
    own_cot.wait()
    swap_cot.wait()
    own_out.wait()
    swap_out.wait()
    waited = set(id(copy) for (layer, _), copy in probs_saved.items() if layer < LAYERS - 1)
    for copy in saved:
        if id(copy) not in waited:
            copy.wait()


BUDGET = 4


def forward(sub, span, owners, pack_wide, pack, pack_vec, inputs, cotangent, lengths, gains, offsets):
    anywhere = pl.BlockSpec(memory_space=pl.ANY)
    on_chip = pl.BlockSpec(memory_space=pltpu.VMEM)
    scalars = pl.BlockSpec(memory_space=pltpu.SMEM)
    shape = jax.ShapeDtypeStruct
    bf16, f32 = jnp.bfloat16, jnp.float32
    vmem = pltpu.VMEM
    dma = pltpu.SemaphoreType.DMA
    return pl.pallas_call(
        functools.partial(forward_kernel, sub, span),
        out_shape=(
            shape((2, 2, R, HALF), bf16),
            shape((2, BLOCKS, D, HALF), bf16),
            shape((ROW, D), bf16),
            shape((LAYERS, 6, 3, ROW, 128), bf16),
            shape((LAYERS, 6, 2, ROW, ROW), bf16),
            shape((LAYERS, ROW, R), bf16),
            shape((LAYERS, 2, ROW, D), bf16),
            shape((LAYERS, 2, ROW, D), f32),
            shape((LAYERS, 4, 2, ROW, HALF), bf16),
            shape((LAYERS, 4 * SPAN_LANES), f32),
            shape(inputs.shape, bf16),
        ),
        in_specs=[anywhere] * 5 + [scalars] + [on_chip] * 4,
        out_specs=[anywhere] * 9 + [on_chip, anywhere],
        scratch_shapes=[
            vmem((2, 2, 256, 128), f32),
            vmem((256, 128), f32),
            vmem((8, SPAN_LANES), f32),
            vmem((ROW, D), bf16),
            vmem((ROW, D), f32),
            vmem((2, 2, R, HALF), bf16),
            vmem((2, 4, D, HALF), bf16),
            vmem((2, 2, 2, D, HALF), bf16),
            vmem((LAYERS, 6, 3, ROW, 128), bf16),
            vmem((6, 2, ROW, ROW), bf16),
            vmem((ROW, R), f32),
            vmem((LAYERS, ROW, R), bf16),
            vmem((LAYERS, 2, ROW, D), bf16),
            vmem((ROW, D), bf16),
            vmem((ROW, D), f32),
            vmem((LAYERS, 2, ROW, D), f32),
            vmem((LAYERS, 4, 2, ROW, HALF), bf16),
            vmem((ROW, 128), jnp.int32),
            vmem((8, ROW), jnp.int32),
            vmem((ROW, D), bf16),
            dma((CHUNKS + 1, 6)),
            dma((CHUNKS + 1, len(ARRIVALS) + 1)),
            dma((3,)),
            dma((3,)),
            dma((3,)),
            dma((5,)),
            dma((LAYERS, SAVES)),
        ],
        compiler_params=pltpu.CompilerParams(
            collective_id=0, has_side_effects=True, vmem_limit_bytes=62 * 1024 * 1024
        ),
        cost_estimate=pl.CostEstimate(flops=2 * 10**10, bytes_accessed=10**8, transcendentals=10**7),
    )(pack_wide, pack, pack_vec, inputs, cotangent, lengths, owners[:, None], owners[None, :], gains, offsets)


def backward_kernel(
    upstream, full, wide, slopes, sums, qkv, probs, proj, adapt, trained, gains,
    input_grad, grads,
    up_v, ffn_v, slopes_v, sums_v, out_v, in_v, wide_v, qkv_v, probs_v, proj_v, adapt_v,
    second_grad, first_grad, total, mixed_grad, row_grads, load_sem,
):
    flights = {}

    def load(key, source, target, sem):
        flights[key] = pltpu.make_async_copy(source, target, load_sem.at[sem])
        flights[key].start()

    def ready(key):
        flights.pop(key).wait()

    def load_ffn(layer, part):
        if part < 4:
            pair = pl.ds(12 * layer + 4 + 2 * part, 2)
            load(("ffn", layer, part), full.at[:, pair], ffn_v.at[part % 2], part % 2)
            load(("slope", layer, part), slopes.at[layer, part], slopes_v.at[part % 2], 2 + part % 2)

    def load_sums(layer):
        load(("second", layer), sums.at[layer, 1], sums_v.at[1], 4)
        load(("first", layer), sums.at[layer, 0], sums_v.at[0], 5)

    def load_attention(layer):
        load(("out", layer), full.at[:, pl.ds(12 * layer + 3, 1)], out_v, 6)
        load(("qkv", layer), qkv.at[layer], qkv_v, 7)
        for pair in range(6):
            load(("probs", layer, pair), probs.at[layer, pair], probs_v.at[pair], 8 + pair)

    def load_tail(layer):
        load(("proj", layer), proj.at[layer], proj_v, 14)
        load(("adapt", layer), adapt.at[layer], adapt_v, 15)
        load(("in", layer), full.at[:, pl.ds(12 * layer, 3)], in_v, 16)

    def gain(number):
        return gains[number : number + 1, :]

    def vector(layer, start, size):
        return trained[layer : layer + 1, start : start + size]

    def attend_back(layer, pair):
        lanes = slice(128 * pair, 128 * (pair + 1))
        query, key, value = qkv_v[pair, 0], qkv_v[pair, 1], qkv_v[pair, 2]
        outer = mixed_grad[:, lanes]
        outer_t = low(outer.astype(jnp.float32).T)
        key_t = low(key.astype(jnp.float32).T)
        zeros = jnp.zeros((HDIM, ROW), jnp.bfloat16)
        query_t, keys, values = [], [], []
        for head in range(2):
            part = slice(head * HDIM, (head + 1) * HDIM)
            masked = [outer_t[part], zeros] if head == 0 else [zeros, outer_t[part]]
            chances_low = probs_v[pair, head]
            chances = chances_low.astype(jnp.float32)
            chance_grad = mm(value, jnp.concatenate(masked, axis=0))
            inner = jnp.sum(chances * chance_grad, axis=0, keepdims=True)
            score_grad = low(chances * (chance_grad - inner))
            values.append(mm(chances_low, outer))
            keys.append(mm(score_grad, query))
            query_t.append(mm(key_t[part], score_grad))
        left = lax.broadcasted_iota(jnp.int32, (ROW, 128), 1) < HDIM
        row_grads[0, :, lanes] = low(SCORE_SCALE * jnp.concatenate(query_t, axis=0).T)
        row_grads[1, :, lanes] = low(SCORE_SCALE * jnp.where(left, keys[0], keys[1]))
        row_grads[2, :, lanes] = low(jnp.where(left, values[0], values[1]))

    start_v = pltpu.make_async_copy(upstream, up_v, load_sem.at[17])
    start_v.start()
    last = LAYERS - 1
    load_sums(last)
    load_ffn(last, 0)
    load_ffn(last, 1)
    load_attention(last)
    load_tail(last)
    load("wide", wide, wide_v, 18)
    start_v.wait()
    total[...] = up_v[...].astype(jnp.float32)
    for layer in reversed(range(LAYERS)):
        ready(("second", layer))
        values = norm_back(sums_v[1], gain(2 * layer + 1), total[...])
        second_grad[...] = low(values)
        first_grad[...] = values
        for part in range(4):
            ready(("ffn", layer, part))
            ready(("slope", layer, part))
            for half in range(2):
                active = mm(second_grad[...], ffn_v[part % 2, half, 1])
                before = low(active * slopes_v[part % 2, half].astype(jnp.float32))
                first_grad[...] += mm_t(before, ffn_v[part % 2, half, 0])
            load_ffn(layer, part + 2)
        ready(("first", layer))
        values = norm_back(sums_v[0], gain(2 * layer), first_grad[...])
        total[...] = values
        second_grad[...] = low(values)
        if layer > 0:
            load_sums(layer - 1)
            load_ffn(layer - 1, 0)
            load_ffn(layer - 1, 1)
        ready(("out", layer))
        for half in range(2):
            mixed_grad[:, half * HALF : (half + 1) * HALF] = low(mm(second_grad[...], out_v[half, 0]))
        ready(("qkv", layer))
        for pair in range(6):
            ready(("probs", layer, pair))
            attend_back(layer, pair)
        if layer > 0:
            load_attention(layer - 1)
        if layer == last:
            ready("wide")
        ready(("proj", layer))
        ready(("adapt", layer))
        combined = None
        for number, start in ((0, 0), (2, 1)):
            row = row_grads[number].astype(jnp.float32)
            bias = vector(layer, 2 * R + start * D, D)
            scale = vector(layer, start * R, R)
            grads[layer : layer + 1, 2 * R + start * D : 2 * R + (start + 1) * D] = jnp.sum(
                row * adapt_v[start].astype(jnp.float32), axis=0, keepdims=True
            )
            back = low(bias * row)
            source = mm_t(back[:, :HALF], wide_v[0, 1]) + mm_t(back[:, HALF:], wide_v[1, 1])
            grads[layer : layer + 1, start * R : (start + 1) * R] = jnp.sum(
                source * proj_v[...].astype(jnp.float32), axis=0, keepdims=True
            )
            combined = scale * source if combined is None else combined + scale * source
        combined = low(combined)
        for half in range(2):
            total[:, half * HALF : (half + 1) * HALF] += mm(combined, wide_v[half, 0])
        ready(("in", layer))
        for half in range(2):
            part = slice(half * HALF, (half + 1) * HALF)
            total[...] += (
                mm_t(row_grads[0, :, part], in_v[half, 0])
                + mm_t(row_grads[1, :, part], in_v[half, 1])
                + mm_t(row_grads[2, :, part], in_v[half, 2])
            )
        if layer > 0:
            load_tail(layer - 1)
    input_grad[...] = total[...]


def backward(upstream, full, wide, slopes, sums, qkv, probs, proj, adapt, trained, gains):
    anywhere = pl.BlockSpec(memory_space=pl.ANY)
    on_chip = pl.BlockSpec(memory_space=pltpu.VMEM)
    bf16, f32 = jnp.bfloat16, jnp.float32
    vmem = pltpu.VMEM
    return pl.pallas_call(
        backward_kernel,
        out_shape=(
            jax.ShapeDtypeStruct((ROW, D), f32),
            jax.ShapeDtypeStruct((LAYERS, 4 * SPAN_LANES), f32),
        ),
        in_specs=[anywhere] * 9 + [on_chip] * 2,
        out_specs=[on_chip] * 2,
        scratch_shapes=[
            vmem((ROW, D), bf16),
            vmem((2, 2, 2, D, HALF), bf16),
            vmem((2, 2, ROW, HALF), bf16),
            vmem((2, ROW, D), f32),
            vmem((2, 1, D, HALF), bf16),
            vmem((2, 3, D, HALF), bf16),
            vmem((2, 2, R, HALF), bf16),
            vmem((6, 3, ROW, 128), bf16),
            vmem((6, 2, ROW, ROW), bf16),
            vmem((ROW, R), bf16),
            vmem((2, ROW, D), bf16),
            vmem((ROW, D), bf16),
            vmem((ROW, D), f32),
            vmem((ROW, D), f32),
            vmem((ROW, D), bf16),
            vmem((3, ROW, D), bf16),
            pltpu.SemaphoreType.DMA((19,)),
        ],
        compiler_params=pltpu.CompilerParams(vmem_limit_bytes=62 * 1024 * 1024),
        cost_estimate=pl.CostEstimate(flops=2 * 10**10, bytes_accessed=10**8, transcendentals=10**6),
    )(upstream, full, wide, slopes, sums, qkv, probs, proj, adapt, trained, gains)


def ending_kernel(
    span, steps,
    input_grad, grads, owner_col, owner_row, vectors, first_moment, second_moment,
    input_grads, own_grad, new_one, new_two, updated,
    flat, pieces, inbox, send_sem, recv_sem, swap_sem, own_sem,
):
    batch = lax.axis_index("batch")
    core = lax.axis_index("tensor")
    sibling = (batch, 1 - core)
    partners = [sibling]
    for bit in range(steps):
        size = 2**bit
        partners.append((batch + size * (1 - 2 * ((batch // size) % 2)), core))
    semaphore = pltpu.get_barrier_semaphore()
    for device in partners:
        pl.semaphore_signal(semaphore, inc=1, device_id=device, device_id_type=MESH)
    pl.semaphore_wait(semaphore, len(partners))

    half_rows = input_grads.shape[1]
    mine = pl.ds(pl.multiple_of(core * half_rows, 8), half_rows)
    other = pl.ds(pl.multiple_of((1 - core) * half_rows, 8), half_rows)
    swap = pltpu.make_async_remote_copy(
        src_ref=input_grad.at[other], dst_ref=input_grads.at[core], send_sem=swap_sem.at[0],
        recv_sem=swap_sem.at[1], device_id=sibling, device_id_type=MESH,
    )
    own = pltpu.make_async_copy(input_grad.at[mine], input_grads.at[core], own_sem)

    for number in range(8):
        layer, part = divmod(number, 4)
        flat[0, number : number + 1, :] = grads[layer : layer + 1, SPAN_LANES * part : SPAN_LANES * (part + 1)]
    for number, device in enumerate(partners):
        copy = pltpu.make_async_remote_copy(
            src_ref=flat.at[number], dst_ref=inbox.at[number], send_sem=send_sem.at[number],
            recv_sem=recv_sem.at[number], device_id=device, device_id_type=MESH,
        )
        copy.start()
        if number == 0:
            swap.start()
            own.start()
        copy.wait()
        flat[number + 1] = flat[number] + inbox[number]

    cut_up(flat.at[len(partners)], span, pieces)
    slots = vectors.shape[0]
    count = owner_row.shape[1]
    rank = piece_ranks(owner_col[...], owner_row[...], 0)
    numbers = lax.broadcasted_iota(jnp.int32, (slots, count), 0)
    select = ((rank == numbers) & (owner_row[...] == batch)).astype(jnp.float32)
    filled = jnp.sum(select, axis=1, keepdims=True)
    gathered = exact(select, pieces[...])[:, :span]
    one = (FIRST_BETA * first_moment[...] + (1.0 - FIRST_BETA) * gathered) * filled
    two = (SECOND_BETA * second_moment[...] + (1.0 - SECOND_BETA) * gathered * gathered) * filled
    fixed_one = one / (1.0 - FIRST_BETA**STEP)
    fixed_two = two / (1.0 - SECOND_BETA**STEP)
    old = vectors[...]
    own_grad[...] = gathered
    new_one[...] = one
    new_two[...] = two
    updated[...] = (
        old - LEARN_RATE * (fixed_one / (jnp.sqrt(fixed_two) + ADAM_EPSILON) + WEIGHT_DECAY * old)
    ) * filled
    own.wait()
    swap.wait()


def ending(input_grad, grads, owners, vectors, first_moment, second_moment, half_rows):
    anywhere = pl.BlockSpec(memory_space=pl.ANY)
    on_chip = pl.BlockSpec(memory_space=pltpu.VMEM)
    steps = lax.axis_size("batch").bit_length() - 1
    f32 = jnp.float32
    slot = jax.ShapeDtypeStruct(vectors.shape, f32)
    return pl.pallas_call(
        functools.partial(ending_kernel, vectors.shape[1], steps),
        out_shape=(jax.ShapeDtypeStruct((2, half_rows, D), f32), slot, slot, slot, slot),
        in_specs=[anywhere] + [on_chip] * 6,
        out_specs=[anywhere] + [on_chip] * 4,
        scratch_shapes=[
            pltpu.VMEM((steps + 2, 8, SPAN_LANES), f32),
            pltpu.VMEM((256, 128), f32),
            pltpu.VMEM((steps + 1, 8, SPAN_LANES), f32),
            pltpu.SemaphoreType.DMA((steps + 1,)),
            pltpu.SemaphoreType.DMA((steps + 1,)),
            pltpu.SemaphoreType.DMA((2,)),
            pltpu.SemaphoreType.DMA,
        ],
        compiler_params=pltpu.CompilerParams(collective_id=1, has_side_effects=True),
    )(input_grad, grads, owners[:, None], owners[None, :], vectors, first_moment, second_moment)


def on_device(
    inputs, cotangent, lengths, owners, vectors, first_moment, second_moment,
    weight_in, weight_out, weight_up, weight_down, basis_a, basis_b, norm_gain, norm_bias,
):
    sub = lax.axis_size("batch") // GROUPS
    span = vectors.shape[1]
    pack_wide, pack, pack_vec = pack_weights(
        sub, vectors, weight_in, weight_out, weight_up, weight_down, basis_a, basis_b
    )
    gains, offsets = norm_gain.reshape(2 * LAYERS, D), norm_bias.reshape(2 * LAYERS, D)
    wide, full, upstream, qkv, probs, proj, adapt, sums, slopes, trained, results = forward(
        sub, span, owners, pack_wide, pack, pack_vec, inputs, cotangent, lengths, gains, offsets
    )
    input_grad, grads = backward(
        upstream, full, wide, slopes, sums, qkv, probs, proj, adapt, trained, gains
    )
    input_grads, own_grad, new_one, new_two, updated = ending(
        input_grad, grads, owners, vectors, first_moment, second_moment, inputs.shape[1]
    )
    return (results, input_grads, own_grad, new_one, new_two, updated, low(updated))


def solution(mesh):
    rows_spec = P(None, ("batch", "tensor"), None)
    split = P("batch", None)
    return jax.shard_map(
        on_device,
        mesh=mesh,
        in_specs=(
            rows_spec, rows_spec, P(None, "batch", None), P(), split, split, split,
            P(None, "batch", None, "tensor"), P(None, "tensor", "batch"), P(None, "batch", "tensor"),
            P(None, "tensor", "batch"), split, P("tensor", "batch"), P(), P(),
        ),
        out_specs=(rows_spec, rows_spec, split, split, split, split, split),
        check_vma=False,
    )
```

```python
import functools

import jax
import jax.numpy as jnp
from jax import lax
from jax.experimental import pallas as pl
from jax.experimental.pallas import tpu as pltpu
from jax.sharding import PartitionSpec as P

D = 768
HDIM = 64
R = 1024
LAYERS = 2
STEP = 10
HALF = 384
GROUPS = 16
BLOCKS = 24
CHUNKS = 13
LAG = 2
AHEAD = 4
DEEP_FIRST = False

EPSILON = 1e-05
SCORE_SCALE = 0.125
MASKED_SCORE = -1000000000.0
LEARN_RATE = 0.3
WEIGHT_DECAY = 0.01
FIRST_BETA = 0.5
SECOND_BETA = 0.5
ADAM_EPSILON = 1e-08
MESH = pl.DeviceIdType.MESH

ARRIVALS = ["Si", "Sj", "Sf", "Dj", "Df", "Xo", "Xi", "Xj", "Xf", "Yo", "Yi", "Yj", "Yf", "Dxo", "Dxi", "Dyo", "Dyi"]
SLOT = {name: index for index, name in enumerate(ARRIVALS)}
FROM_SIBLING = len(ARRIVALS)
TO_SIBLING, TO_X, TO_Y, TO_IN, TO_OUT, LOCAL = range(6)
DEPTHS = 7


class Gather:
    def __init__(self, sub, pack_wide, pack, pack_vec, wide, full, vecs, send_sem, recv_sem):
        self.sub = sub
        self.owners = GROUPS * sub
        self.pack_wide, self.pack, self.pack_vec = pack_wide, pack, pack_vec
        self.wide, self.full, self.vecs = wide, full, vecs
        self.send_sem, self.recv_sem = send_sem, recv_sem
        batch = lax.axis_index("batch")
        self.batch = batch
        self.core = lax.axis_index("tensor")
        group = batch // sub
        self.lane = batch % sub
        z, p = group // 4, group % 4
        inward = 1 - 2 * (z // 2)
        self.middle = ((z + 1) // 2) % 2
        plane_i, plane_j = z + inward, z + 2 * inward
        plane_f = 6 - z - plane_i - plane_j
        self.z, self.p = z, p
        self.planes = {"o": z, "i": plane_i, "j": plane_j, "f": plane_f}
        col_x, col_y = p + 1 - 2 * (p % 2), p + 2 - 4 * (p // 2)
        self.cols = {"S": p, "X": col_x, "Y": col_y, "D": 3 - p}
        self.sibling = (batch, 1 - self.core)
        self.to_x = self.device(z, col_x)
        self.to_y = self.device(z, col_y)
        self.to_in = self.device(plane_i, p)
        self.to_out = self.device(plane_f, p)

    def device(self, plane, col):
        return ((plane * 4 + col) * self.sub + self.lane, self.core)

    def barrier(self, others):
        semaphore = pltpu.get_barrier_semaphore()
        devices = [self.sibling, self.to_x, self.to_y, self.to_in, self.to_out] + others
        for device in devices:
            pl.semaphore_signal(semaphore, inc=1, device_id=device, device_id_type=MESH)
        pl.semaphore_wait(semaphore, len(devices))

    def rows(self, chunk, half, start, count, blocks=(0, 2)):
        if chunk == 0:
            ref, size, base = self.wide, R // GROUPS, 0
        elif chunk == CHUNKS:
            ref, size, base = self.vecs, 8, 0
        else:
            ref, size, base = self.full, D // GROUPS, 2 * (chunk - 1)
        first = pl.multiple_of(start * size, min(size, 16)) if not isinstance(start, int) else start * size
        return ref.at[half, pl.ds(base + blocks[0], blocks[1]), pl.ds(first, count * size)]

    def shard(self, chunk, half, col, plane, blocks=(0, 2)):
        return self.rows(chunk, half, self.planes[plane] * 4 + self.cols[col], 1, blocks)

    def copy(self, chunk, source, target, device, send, slot):
        pltpu.make_async_remote_copy(
            src_ref=source,
            dst_ref=target,
            send_sem=self.send_sem.at[chunk, send],
            recv_sem=self.recv_sem.at[chunk, slot],
            device_id=device,
            device_id_type=MESH,
        ).start()

    def push(self, chunk, col, plane, moves, blocks=(0, 2), sibling=True, source=None):
        region = self.shard(chunk, self.core, col, plane, blocks)
        source = region if source is None else source
        for device, send, slot in moves:
            slot = SLOT[slot] if isinstance(slot, str) else slot
            self.copy(chunk, source, region, device, send, slot)
        if sibling:
            self.copy(chunk, source, region, self.sibling, TO_SIBLING, FROM_SIBLING)

    def take(self, chunk, name):
        blocks = {"x": (0, 1), "y": (1, 1)}.get(name[1:-1], (0, 2))
        region = self.shard(chunk, self.core, name[0], name[-1], blocks)
        pltpu.make_async_remote_copy(
            src_ref=region,
            dst_ref=region,
            send_sem=self.send_sem.at[chunk, TO_X],
            recv_sem=self.recv_sem.at[chunk, SLOT[name]],
            device_id=self.to_x,
            device_id_type=MESH,
        ).wait_recv()

    def when_middle(self, action):
        pl.when(self.middle == 1)(action)

    def when_end(self, action):
        pl.when(self.middle == 0)(action)

    def source(self, chunk):
        if chunk == 0:
            return self.pack_wide
        return self.pack_vec if chunk == CHUNKS else self.pack.at[pl.ds(2 * (chunk - 1), 2)]

    def local(self, chunk):
        return pltpu.make_async_copy(
            self.source(chunk), self.shard(chunk, self.core, "S", "o"), self.send_sem.at[chunk, LOCAL]
        )

    def step(self, chunk, depth):
        to_x, to_y = (self.to_x, TO_X), (self.to_y, TO_Y)
        to_in, to_out = (self.to_in, TO_IN), (self.to_out, TO_OUT)
        if depth == 0:
            source = self.source(chunk)
            arrival = self.middle * SLOT["Si"] + (1 - self.middle) * SLOT["Sf"]
            self.push(chunk, "S", "o", [(*to_in, arrival), (*to_x, "Xo"), (*to_y, "Yo")], source=source)

            @self.when_middle
            def _():
                self.push(chunk, "S", "o", [(*to_out, "Si")], sibling=False, source=source)

            self.local(chunk).start()
        elif depth == 1:
            self.take(chunk, "Si")

            @self.when_middle
            def _():
                self.push(chunk, "S", "i", [(*to_out, "Sj")], sibling=False)
                self.take(chunk, "Sf")
                self.push(chunk, "S", "f", [(*to_in, "Sj"), (*to_x, "Xf"), (*to_y, "Yf")])

            self.push(chunk, "S", "i", [(*to_x, "Xi"), (*to_y, "Yi")])
            self.cross(chunk, "o")
        elif depth == 2:
            self.take(chunk, "Sj")

            @self.when_middle
            def _():
                self.push(chunk, "S", "j", [(*to_out, "Sf")], sibling=False)

            self.push(chunk, "S", "j", [(*to_x, "Xj"), (*to_y, "Yj")])
            self.take(chunk, "Dxo")
            self.take(chunk, "Dyo")

            @self.when_end
            def _():
                self.push(chunk, "D", "o", [(*to_in, "Df")], sibling=False)

            self.push(chunk, "D", "o", [])
            self.cross(chunk, "i")

            @self.when_middle
            def _():
                self.land(chunk, "Xf", "Yf")
        elif depth == 3:
            @self.when_end
            def _():
                self.take(chunk, "Sf")
                self.push(chunk, "S", "f", [(*to_x, "Xf"), (*to_y, "Yf")])

            self.take(chunk, "Dxi")
            self.take(chunk, "Dyi")

            @self.when_middle
            def _():
                self.push(chunk, "D", "i", [(*to_out, "Dj")], sibling=False)
                self.take(chunk, "Df")
                self.push(chunk, "D", "f", [(*to_in, "Dj")])

            self.push(chunk, "D", "i", [])
            self.land(chunk, "Xj", "Yj")
        elif depth == 4:
            self.take(chunk, "Dj")

            @self.when_middle
            def _():
                self.push(chunk, "D", "j", [(*to_out, "Df")], sibling=False)

            self.push(chunk, "D", "j", [])

            @self.when_end
            def _():
                self.land(chunk, "Xf", "Yf")
        elif depth == 5:
            @self.when_end
            def _():
                self.land(chunk, "Df")
        else:
            self.local(chunk).wait()
            whole = self.rows(chunk, 1 - self.core, 0, GROUPS)
            pltpu.make_async_remote_copy(
                src_ref=whole,
                dst_ref=whole,
                send_sem=self.send_sem.at[chunk, TO_SIBLING],
                recv_sem=self.recv_sem.at[chunk, FROM_SIBLING],
                device_id=self.sibling,
                device_id_type=MESH,
            ).wait_recv()

    def cross(self, chunk, plane):
        self.take(chunk, "X" + plane)
        self.push(chunk, "X", plane, [(self.to_y, TO_Y, "Dy" + plane)], (1, 1), sibling=False)
        self.push(chunk, "X", plane, [])
        self.take(chunk, "Y" + plane)
        self.push(chunk, "Y", plane, [(self.to_x, TO_X, "Dx" + plane)], (0, 1), sibling=False)
        self.push(chunk, "Y", plane, [])

    def land(self, chunk, *names):
        for name in names:
            self.take(chunk, name)
            self.push(chunk, name[0], name[1], [])

    def sent(self, chunk, send, shards):
        region = self.rows(chunk, self.core, 0, shards)
        pltpu.make_async_remote_copy(
            src_ref=region,
            dst_ref=region,
            send_sem=self.send_sem.at[chunk, send],
            recv_sem=self.recv_sem.at[chunk, FROM_SIBLING],
            device_id=self.sibling,
            device_id_type=MESH,
        ).wait_send()

    def finish(self):
        for chunk in range(CHUNKS + 1):
            self.sent(chunk, TO_SIBLING, GROUPS)
            self.sent(chunk, TO_X, 5)
            self.sent(chunk, TO_Y, 5)

        @self.when_middle
        def _():
            for chunk in range(CHUNKS + 1):
                self.sent(chunk, TO_IN, 3)
                self.sent(chunk, TO_OUT, 5)

        @self.when_end
        def _():
            for chunk in range(CHUNKS + 1):
                self.sent(chunk, TO_IN, 2)

    def tick(self, number):
        for chunk, depth in TIMES.get(number, ()):
            self.step(chunk, depth)


def timetable():
    times = {}
    for chunk in range(CHUNKS + 1):
        for depth in range(DEPTHS):
            tick = LAG * (chunk % CHUNKS) + depth
            if depth == 0:
                tick = max(0, tick - AHEAD)
            times.setdefault(tick, []).append((depth, chunk % CHUNKS, chunk))
    return {tick: [(chunk, depth) for depth, _, chunk in sorted(events, reverse=DEEP_FIRST)] for tick, events in times.items()}


TIMES = timetable()
TICKS = LAG * (CHUNKS - 1) + DEPTHS


def group_rows(values, axis, size, sub):
    if sub == 1:
        return values
    group = lax.axis_index("batch") // sub
    values = lax.all_gather(values, "batch", axis=axis, tiled=True)
    return lax.dynamic_slice_in_dim(values, group * size, size, axis)


def mm(left, right):
    return jnp.dot(left, right, preferred_element_type=jnp.float32)


def mm_t(left, right):
    return lax.dot_general(left, right, (((1,), (1,)), ((), ())), preferred_element_type=jnp.float32)


def exact(left, right):
    return jnp.dot(left, right, precision=lax.Precision.HIGHEST, preferred_element_type=jnp.float32)


def low(values):
    return values.astype(jnp.bfloat16)


def normalize(values, gain, offset):
    center = values - jnp.mean(values, axis=-1, keepdims=True)
    spread = jnp.mean(center * center, axis=-1, keepdims=True)
    return center * lax.rsqrt(spread + EPSILON) * gain + offset


def norm_back(values, gain, upstream):
    center = values - jnp.mean(values, axis=-1, keepdims=True)
    spread = jnp.mean(center * center, axis=-1, keepdims=True)
    scale = lax.rsqrt(spread + EPSILON)
    unit = center * scale
    scaled = upstream * gain
    first = jnp.mean(scaled, axis=-1, keepdims=True)
    second = jnp.mean(scaled * unit, axis=-1, keepdims=True)
    return scale * (scaled - first - unit * second)


def gelu_and_slope(values):
    bell = jnp.exp(-0.5 * values * values)
    t = 1.0 / (1.0 + 0.23164190 * jnp.abs(values))
    poly = t * (0.127414796 + t * (-0.142248368 + t * (0.7107068705 + t * (-0.7265760135 + t * 0.5307027145))))
    tail = poly * bell
    share = jnp.where(values < 0, tail, 1.0 - tail)
    return values * share, share + values * (0.3989422804 * bell)


def piece_ranks(col, row, axis):
    count = row.shape[1]
    down = lax.broadcasted_iota(jnp.int32, (count, count), 0)
    across = lax.broadcasted_iota(jnp.int32, (count, count), 1)
    earlier = (down < across) if axis == 0 else (across < down)
    return jnp.sum(((col == row) & earlier).astype(jnp.float32), axis=axis, keepdims=True).astype(jnp.int32)


SPAN_LANES = 896


def lay_out(pieces, span, flat):
    lanes = lax.broadcasted_iota(jnp.int32, (8, 128), 1)
    tiles = [jnp.zeros((8, 128), jnp.float32) for _ in range(SPAN_LANES // 128)]
    for i in range(32):
        tile, offset = divmod(span * i, 128)
        rows = pieces[pl.ds(i, 8, stride=32), :]
        rows = pltpu.roll(rows, offset, 1) if offset else rows
        inside = (lanes >= offset) & (lanes < offset + span)
        tiles[tile] = tiles[tile] + jnp.where(inside, rows, 0.0)
        if offset + span > 128:
            tiles[tile + 1] = tiles[tile + 1] + jnp.where(lanes < offset + span - 128, rows, 0.0)
    for tile, values in enumerate(tiles):
        flat[:, 128 * tile : 128 * (tile + 1)] = values


def cut_up(flat, span, pieces):
    lanes = lax.broadcasted_iota(jnp.int32, (4, 128), 1)
    for layer in range(LAYERS):
        for i in range(32):
            tile, offset = divmod(span * i, 128)
            rows = flat[layer, pl.ds(tile, 4, stride=7), :]
            if offset:
                rows = pltpu.roll(rows, 128 - offset, 1)
            if offset + span > 128:
                after = pltpu.roll(flat[layer, pl.ds(tile + 1, 4, stride=7), :], 128 - offset, 1)
                rows = jnp.where(lanes < 128 - offset, rows, after)
            pieces[pl.ds(128 * layer + i, 4, stride=32), :] = jnp.where(lanes < span, rows, 0.0)


def as_column(row):
    count = row.shape[1]
    down = lax.broadcasted_iota(jnp.int32, (count, count), 0)
    across = lax.broadcasted_iota(jnp.int32, (count, count), 1)
    return jnp.sum(jnp.where(down == across, row, 0).astype(jnp.float32), axis=1, keepdims=True).astype(jnp.int32)


ROW = 512
SEND_INPUT, SEND_COTANGENT, SEND_RESULT, SEND_GRAD = range(4)
BUDGET = 4
COSTS = {
    "documents": 1, "start_rows": 1, "vectors_in": 4, "project": 1, "frozen": 2, "attend": 2, "attention_out": 2,
    "feed_forward": 3, "layer_out": 1,
}


class Sums:
    def __init__(self, gather, inbox, send_sem, recv_sem):
        self.gather, self.inbox, self.send_sem, self.recv_sem = gather, inbox, send_sem, recv_sem
        z, p = gather.z, gather.p
        cols = [gather.cols[name] for name in ("X", "Y", "D")]
        planes = [gather.planes[name] for name in ("i", "j", "f")]
        self.phases = [
            [(gather.sibling, 0, 0)],
            [(gather.device(z, col), 1 + p, 1 + col) for col in cols],
            [(gather.device(plane, p), 5 + z, 5 + plane) for plane in planes],
        ]
        self.own_slots = [None, 1 + p, 5 + z]
        self.ranges = [None, (1, 4), (5, 4)]
        size, slot = 1, 9
        while size < gather.sub:
            partner = gather.batch + size * (1 - 2 * ((gather.lane // size) % 2))
            self.phases.append([((partner, gather.core), slot, slot)])
            self.own_slots.append(None)
            self.ranges.append(None)
            size, slot = 2 * size, slot + 1

    def others(self):
        gather = self.gather
        found = [gather.device(gather.z, gather.cols["D"]), gather.device(gather.planes["j"], gather.p)]
        for phase in self.phases[3:]:
            found.append(phase[0][0])
        return found

    def copies(self, layer, phase, values):
        base = sum(len(moves) for moves in self.phases[:phase])
        return [
            pltpu.make_async_remote_copy(
                src_ref=values, dst_ref=self.inbox.at[layer, there], send_sem=self.send_sem.at[layer, base + number],
                recv_sem=self.recv_sem.at[layer, there], device_id=device, device_id_type=MESH,
            )
            for number, (device, there, _) in enumerate(self.phases[phase])
        ]

    def start(self, layer, phase, values):
        if self.own_slots[phase] is not None:
            self.inbox[layer, self.own_slots[phase]] = values[...]
        for copy in self.copies(layer, phase, values):
            copy.start()

    def finish(self, layer, phase, values):
        for copy, (device, _, here) in zip(self.copies(layer, phase, values), self.phases[phase]):
            copy.wait_send()
            pltpu.make_async_remote_copy(
                src_ref=values, dst_ref=self.inbox.at[layer, here], send_sem=self.send_sem.at[layer, 0],
                recv_sem=self.recv_sem.at[layer, here], device_id=device, device_id_type=MESH,
            ).wait_recv()
        if self.ranges[phase] is None:
            values[...] = values[...] + self.inbox[layer, self.phases[phase][0][2]]
        else:
            first, count = self.ranges[phase]
            values[...] = sum(self.inbox[layer, first + number] for number in range(1, count)) + self.inbox[layer, first]


def train_kernel(
    sub, span,
    weight_in, weight_out, weight_up, weight_down, basis_a, basis_b, vectors, owner_row, gains, offsets, lengths, inputs, cotangent,
    wide, full, probs, grads, grad_own, grad_swap, result_own, result_swap,
    pack, wide_pack, vec_pack, vecs, pieces, flat, trained,
    rows_low, rows, wide_v, att_v, ffn_v, qkv_v, probs_v, proj_v, proj_low, adapt_v, mixed, feed, sums_v, slopes_v,
    doc_col, doc_row, result_v, up_v, row_grads, inbox,
    send_sem, recv_sem, swap_send, swap_recv, own_sem, load_sem, save_sem, sums_send, sums_recv,
):
    gather = Gather(sub, wide_pack, pack, vec_pack, wide, full, vecs, send_sem, recv_sem)
    sums = Sums(gather, inbox, sums_send, sums_recv)
    core = gather.core
    half_rows = inputs.shape[1]
    mine = pl.ds(pl.multiple_of(core * half_rows, 16), half_rows)
    other = pl.ds(pl.multiple_of((1 - core) * half_rows, 16), half_rows)

    def swap(number, source, target):
        return pltpu.make_async_remote_copy(
            src_ref=source, dst_ref=target, send_sem=swap_send.at[number], recv_sem=swap_recv.at[number],
            device_id=gather.sibling, device_id_type=MESH,
        )

    def own(number, source, target):
        return pltpu.make_async_copy(source, target, own_sem.at[number])

    def gain(number):
        return gains[number // 2, number % 2 : number % 2 + 1, :]

    def offset(number):
        return offsets[number // 2, number % 2 : number % 2 + 1, :]

    def vector(layer, start, size):
        return trained[layer : layer + 1, start : start + size]

    wide_pack[0] = jnp.where(core == 0, basis_a[:, :HALF], basis_a[:, HALF:])
    wide_pack[1] = basis_b[...]
    padded = jnp.concatenate([vectors[...], jnp.zeros((32, 128 - span), jnp.float32)], axis=1)
    vec_pack[...] = jnp.where(core == 0, padded[:16], padded[16:]).reshape(2, 8, 128)

    for layer in range(LAYERS):
        for part in range(3):
            pack[12 * layer + part] = weight_in[layer, part]
        pack[12 * layer + 3] = weight_out[layer]
        for part in range(4):
            columns = slice(part * HALF, (part + 1) * HALF)
            pack[12 * layer + 4 + 2 * part] = weight_up[layer, :, columns]
            pack[12 * layer + 5 + 2 * part] = weight_down[layer, :, columns]

    gather.barrier(sums.others())
    swap_in = swap(SEND_INPUT, inputs.at[1 - core], rows_low.at[mine])
    swap_cot = swap(SEND_COTANGENT, cotangent.at[1 - core], up_v.at[mine])
    own_in = own(0, inputs.at[core], rows_low.at[mine])
    own_cot = own(1, cotangent.at[core], up_v.at[mine])
    swap_in.start()
    own_in.start()

    def load_wide():
        return pltpu.make_async_copy(wide, wide_v, load_sem.at[0])

    def load_att(layer, part):
        pair = pl.ds(12 * layer + 2 * part, 2)
        return pltpu.make_async_copy(full.at[:, pair], att_v.at[:, pl.ds(2 * part, 2)], load_sem.at[1 + part])

    def load_ffn(layer, part):
        pair = pl.ds(12 * layer + 4 + 2 * part, 2)
        return pltpu.make_async_copy(full.at[:, pair], ffn_v.at[part % 2], load_sem.at[3 + part % 2])

    def save_probs(pair):
        return pltpu.make_async_copy(probs_v.at[pair], probs.at[pair], save_sem.at[pair])

    def load_probs(pair):
        return pltpu.make_async_copy(probs.at[pair], probs_v.at[pair], save_sem.at[pair])

    def documents():
        places_col = lax.broadcasted_iota(jnp.int32, (ROW, 128), 0)
        places_row = lax.broadcasted_iota(jnp.int32, (8, ROW), 1)
        ids_col = jnp.zeros((ROW, 128), jnp.int32)
        ids_row = jnp.zeros((8, ROW), jnp.int32)
        end = jnp.int32(0)
        for number in range(lengths.shape[2]):
            end = end + lengths[core, 0, number]
            ids_col = ids_col + (places_col >= end).astype(jnp.int32)
            ids_row = ids_row + (places_row >= end).astype(jnp.int32)
        doc_col[...] = ids_col
        doc_row[...] = ids_row

    def start_rows():
        own_in.wait()
        swap_in.wait()
        rows[...] = rows_low[...].astype(jnp.float32)

    def vectors_in():
        owner_col = as_column(owner_row[...])
        slot = owner_col * (512 // gather.owners) + piece_ranks(owner_col, owner_row[...], 1)
        place = ((slot >> 3) & 3) * 128 + (slot >> 5) * 8 + (slot & 7)
        spots = lax.broadcasted_iota(jnp.int32, (slot.shape[0], 512), 1)
        select = (place == spots).astype(jnp.float32)
        pieces[...] = exact(select, vecs[...].reshape(512, 128))
        lay_out(pieces, span, flat)
        for number in range(8):
            layer, part = divmod(number, 4)
            trained[layer : layer + 1, SPAN_LANES * part : SPAN_LANES * (part + 1)] = flat[number : number + 1, :]

    def project(layer):
        if layer == 0:
            load_wide().wait()
        proj_v[...] = mm_t(rows_low[:, :HALF], wide_v[0, 0]) + mm_t(rows_low[:, HALF:], wide_v[1, 0])
        proj_low[layer] = low(proj_v[...])

    def frozen(layer, part, half):
        if half == 0:
            load_att(layer, part).wait()
        for number in ((0, 1) if part == 0 else (2,)):
            values = mm(rows_low[...], att_v[half, number])
            if number != 1:
                start = (0, None, 1)[number]
                bias = vector(layer, 2 * R + start * D + half * HALF, HALF)
                scale = vector(layer, start * R, R)
                adapted = mm(low(scale * proj_v[...]), wide_v[half, 1])
                adapt_v[layer, start, :, half * HALF : (half + 1) * HALF] = low(adapted)
                values = values + bias * adapted
            values = low(values)
            for third in range(3):
                qkv_v[layer, 3 * half + third, number] = values[:, 128 * third : 128 * (third + 1)]

    def attend(layer, pair):
        if layer > 0:
            save_probs(pair).wait()
        query = qkv_v[layer, pair, 0].astype(jnp.float32) * SCORE_SCALE
        query_t = low(query.T)
        value_t = low(qkv_v[layer, pair, 2].astype(jnp.float32).T)
        key = qkv_v[layer, pair, 1]
        ids_col = doc_col[...]
        same = jnp.concatenate([ids_col] * 4, axis=1) == doc_row[0:1, :]
        zeros = jnp.zeros((HDIM, ROW), jnp.bfloat16)
        mixed_t = []
        for head in range(2):
            part = slice(head * HDIM, (head + 1) * HDIM)
            masked = [query_t[part], zeros] if head == 0 else [zeros, query_t[part]]
            scores = jnp.where(same, mm(key, jnp.concatenate(masked, axis=0)), MASKED_SCORE)
            raised = jnp.exp(scores - jnp.max(scores, axis=0, keepdims=True))
            chances = low(raised * (1.0 / jnp.sum(raised, axis=0, keepdims=True)))
            probs_v[pair, head] = chances
            mixed_t.append(mm(value_t[part], chances))
        mixed[:, 128 * pair : 128 * (pair + 1)] = low(jnp.concatenate(mixed_t, axis=0).T)
        if layer < LAYERS - 1:
            save_probs(pair).start()

    def attention_out(layer):
        total = rows[...] + mm_t(mixed[:, :HALF], att_v[0, 3]) + mm_t(mixed[:, HALF:], att_v[1, 3])
        sums_v[layer, 0] = total
        middle = normalize(total, gain(2 * layer), offset(2 * layer))
        rows[...] = middle
        rows_low[...] = low(middle)

    def feed_forward(layer, part, half):
        if half == 0:
            load_ffn(layer, part).wait()
        before = mm(rows_low[...], ffn_v[part % 2, half, 0])
        active, slope = gelu_and_slope(before)
        slopes_v[layer, part, half] = low(slope)
        term = mm_t(low(active), ffn_v[part % 2, half, 1])
        if part == 0 and half == 0:
            feed[...] = term
        else:
            feed[...] += term

    def layer_out(layer):
        total = rows[...] + feed[...]
        sums_v[layer, 1] = total
        values = normalize(total, gain(2 * layer + 1), offset(2 * layer + 1))
        if layer == LAYERS - 1:
            result_v[...] = low(values)
        else:
            rows[...] = values
            rows_low[...] = low(values)

    def ready(chunk):
        return LAG * chunk + DEPTHS - 1

    queue = []

    def add(tick, task, *arguments):
        queue.append((tick, functools.partial(task, *arguments)))

    add(0, documents)
    add(1, start_rows)
    add(ready(0), vectors_in)
    add(ready(0), project, 0)
    for layer in range(LAYERS):
        first = 1 + 6 * layer
        if layer > 0:
            add(0, project, layer)
        for part in range(2):
            for half in range(2):
                add(ready(first + part), frozen, layer, part, half)
        for pair in range(6):
            add(0, attend, layer, pair)
        add(0, attention_out, layer)
        for part in range(4):
            for half in range(2):
                add(ready(first + 2 + part), feed_forward, layer, part, half)
        add(0, layer_out, layer)

    ffn_order = [(layer, part) for layer in range(LAYERS) for part in range(4)]
    counts = {"ffn_started": 0, "ffn_done": 0, "att_done": 0}
    att_started = set()

    def start_loads(number):
        while counts["ffn_started"] < min(len(ffn_order), counts["ffn_done"] + 2):
            layer, part = ffn_order[counts["ffn_started"]]
            if ready(3 + 6 * layer + part) > number:
                break
            load_ffn(layer, part).start()
            counts["ffn_started"] += 1
        for layer in range(LAYERS):
            for part in range(2):
                if (layer, part) in att_started or ready(1 + 6 * layer + part) > number or counts["att_done"] < layer:
                    continue
                load_att(layer, part).start()
                att_started.add((layer, part))

    position = 0
    for number in range(TICKS):
        gather.tick(number)
        if number == 0:
            swap_cot.start()
            own_cot.start()
        if number == ready(0):
            load_wide().start()
        start_loads(number)
        budget = BUDGET if number < TICKS - 1 else 10**6
        while position < len(queue) and queue[position][0] <= number and budget > 0:
            task = queue[position][1]
            name = task.func.__name__
            task()
            counts["ffn_done"] += name == "feed_forward" and task.args[2] == 1
            counts["att_done"] += name == "attention_out"
            start_loads(number)
            budget -= COSTS[name]
            position += 1
    assert position == len(queue)

    swap_out = swap(SEND_RESULT, result_v.at[other], result_swap)
    own_out = own(2, result_v.at[mine], result_own)
    swap_out.start()
    own_out.start()

    def feed_back(layer, part):
        if (layer, part) not in resident:
            load_ffn(layer, part).wait()
        for half in range(2):
            active = mm(rows_low[...], ffn_v[part % 2, half, 1])
            before = low(active * slopes_v[layer, part, half].astype(jnp.float32))
            feed[...] += mm_t(before, ffn_v[part % 2, half, 0])

    def attend_back(layer, pair):
        lanes = slice(128 * pair, 128 * (pair + 1))
        query, key, value = qkv_v[layer, pair, 0], qkv_v[layer, pair, 1], qkv_v[layer, pair, 2]
        outer = mixed[:, lanes]
        outer_t = low(outer.astype(jnp.float32).T)
        key_t = low(key.astype(jnp.float32).T)
        zeros = jnp.zeros((HDIM, ROW), jnp.bfloat16)
        query_t, keys, values = [], [], []
        for head in range(2):
            part = slice(head * HDIM, (head + 1) * HDIM)
            masked = [outer_t[part], zeros] if head == 0 else [zeros, outer_t[part]]
            chances_low = probs_v[pair, head]
            chances = chances_low.astype(jnp.float32)
            chance_grad = mm(value, jnp.concatenate(masked, axis=0))
            inner = jnp.sum(chances * chance_grad, axis=0, keepdims=True)
            score_grad = low(chances * (chance_grad - inner))
            values.append(mm(chances_low, outer))
            keys.append(mm(score_grad, query))
            query_t.append(mm(key_t[part], score_grad))
        left = lax.broadcasted_iota(jnp.int32, (ROW, 128), 1) < HDIM
        row_grads[0, :, lanes] = low(SCORE_SCALE * jnp.concatenate(query_t, axis=0).T)
        row_grads[1, :, lanes] = low(SCORE_SCALE * jnp.where(left, keys[0], keys[1]))
        row_grads[2, :, lanes] = low(jnp.where(left, values[0], values[1]))

    def vector_back(layer):
        found = {}
        combined = None
        for number, start in ((0, 0), (2, 1)):
            row = row_grads[number].astype(jnp.float32)
            bias = vector(layer, 2 * R + start * D, D)
            scale = vector(layer, start * R, R)
            found[2 + start] = jnp.sum(row * adapt_v[layer, start].astype(jnp.float32), axis=0, keepdims=True)
            back = low(bias * row)
            source = mm_t(back[:, :HALF], wide_v[0, 1]) + mm_t(back[:, HALF:], wide_v[1, 1])
            found[start] = jnp.sum(source * proj_low[layer].astype(jnp.float32), axis=0, keepdims=True)
            combined = scale * source if combined is None else combined + scale * source
        proj_low[layer] = low(combined)
        number = 0
        for start in range(4):
            for tile in range(found[start].shape[1] // 128):
                grads[layer, number : number + 1, :] = found[start][:, 128 * tile : 128 * (tile + 1)]
                number += 1
        grads[layer, number:, :] = jnp.zeros((32 - number, 128), jnp.float32)

    def input_back(layer, which):
        for half in range(2):
            part = slice(half * HALF, (half + 1) * HALF)
            rows[which, part] += mm(proj_low[layer, which], wide_v[half, 0])
        total = rows[which, :]
        for half in range(2):
            part = slice(half * HALF, (half + 1) * HALF)
            for number in range(3):
                total = total + mm_t(row_grads[number, which, part], att_v[half, number])
        rows[which, :] = total

    last = LAYERS - 1
    order = [(layer, part) for layer in reversed(range(LAYERS)) for part in reversed(range(4))]
    resident = {(last, 3), (last, 2)}
    own_cot.wait()
    swap_cot.wait()
    rows[...] = up_v[...].astype(jnp.float32)
    phases = len(sums.phases)
    pending = []
    for layer in reversed(range(LAYERS)):
        values = norm_back(sums_v[layer, 1], gain(2 * layer + 1), rows[...])
        rows_low[...] = low(values)
        feed[...] = values
        for part in reversed(range(4)):
            feed_back(layer, part)
            following = order.index((layer, part)) + 2
            if following < len(order):
                load_ffn(*order[following]).start()
            if pending:
                pending.pop(0)()
        values = norm_back(sums_v[layer, 0], gain(2 * layer), feed[...])
        rows[...] = values
        rows_low[...] = low(values)
        if layer < last:
            for part in range(2):
                load_att(layer, part).wait()
        for half in range(2):
            mixed[:, half * HALF : (half + 1) * HALF] = low(mm(rows_low[...], att_v[half, 3]))
        for pair in range(6):
            if layer < last:
                load_probs(pair).wait()
            attend_back(layer, pair)
            if layer > 0:
                load_probs(pair).start()
            if pending:
                pending.pop(0)()
        vector_back(layer)
        values = grads.at[layer]
        sums.start(layer, 0, values)

        def advance(layer, phase, values):
            sums.finish(layer, phase, values)
            if phase + 1 < phases:
                sums.start(layer, phase + 1, values)

        steps = [functools.partial(advance, layer, phase, values) for phase in range(phases)]
        if layer > 0:
            input_back(layer, slice(None))
            for part in range(2):
                load_att(layer - 1, part).start()
            pending = steps
        else:
            while pending:
                pending.pop(0)()
            input_back(layer, other)
            swap_grad = swap(SEND_GRAD, rows.at[other], grad_swap)
            swap_grad.start()
            steps.pop(0)()
            input_back(layer, mine)
            own_grad = own(3, rows.at[mine], grad_own)
            own_grad.start()
            for step in steps:
                step()

    gather.finish()
    own_out.wait()
    swap_out.wait()
    own_grad.wait()
    swap_grad.wait()


def train(sub, span, shards, owner_row, gains, offsets, lengths, inputs, cotangent):
    anywhere = pl.BlockSpec(memory_space=pl.ANY)
    on_chip = pl.BlockSpec(memory_space=pltpu.VMEM)
    scalars = pl.BlockSpec(memory_space=pltpu.SMEM)
    shape = jax.ShapeDtypeStruct
    bf16, f32 = jnp.bfloat16, jnp.float32
    vmem = pltpu.VMEM
    dma = pltpu.SemaphoreType.DMA
    half_rows = inputs.shape[1]
    slots = 9 + (sub.bit_length() - 1)
    return pl.pallas_call(
        functools.partial(train_kernel, sub, span),
        out_shape=(
            shape((2, 2, R, HALF), bf16),
            shape((2, BLOCKS, D, HALF), bf16),
            shape((6, 2, ROW, ROW), bf16),
            shape((LAYERS, 32, 128), f32),
            shape((half_rows, D), f32),
            shape((half_rows, D), f32),
            shape((half_rows, D), bf16),
            shape((half_rows, D), bf16),
        ),
        in_specs=[on_chip] * 10 + [scalars] + [anywhere] * 2,
        out_specs=[anywhere] * 3 + [on_chip] + [anywhere] * 4,
        scratch_shapes=[
            vmem((BLOCKS, D // GROUPS, HALF), bf16),
            vmem((2, 64, HALF), bf16),
            vmem((2, 8, 128), f32),
            vmem((2, 2, 128, 128), f32),
            vmem((256, 128), f32),
            vmem((8, SPAN_LANES), f32),
            vmem((LAYERS, 4 * SPAN_LANES), f32),
            vmem((ROW, D), bf16),
            vmem((ROW, D), f32),
            vmem((2, 2, R, HALF), bf16),
            vmem((2, 4, D, HALF), bf16),
            vmem((2, 2, 2, D, HALF), bf16),
            vmem((LAYERS, 6, 3, ROW, 128), bf16),
            vmem((6, 2, ROW, ROW), bf16),
            vmem((ROW, R), f32),
            vmem((LAYERS, ROW, R), bf16),
            vmem((LAYERS, 2, ROW, D), bf16),
            vmem((ROW, D), bf16),
            vmem((ROW, D), f32),
            vmem((LAYERS, 2, ROW, D), f32),
            vmem((LAYERS, 4, 2, ROW, HALF), bf16),
            vmem((ROW, 128), jnp.int32),
            vmem((8, ROW), jnp.int32),
            vmem((ROW, D), bf16),
            vmem((ROW, D), bf16),
            vmem((3, ROW, D), bf16),
            vmem((LAYERS, slots, 32, 128), f32),
            dma((CHUNKS + 1, 6)),
            dma((CHUNKS + 1, len(ARRIVALS) + 1)),
            dma((4,)),
            dma((4,)),
            dma((4,)),
            dma((5,)),
            dma((6,)),
            dma((LAYERS, slots)),
            dma((LAYERS, slots)),
        ],
        compiler_params=pltpu.CompilerParams(
            collective_id=0, has_side_effects=True, vmem_limit_bytes=63 * 1024 * 1024
        ),
        cost_estimate=pl.CostEstimate(flops=4 * 10**10, bytes_accessed=10**8, transcendentals=10**7),
    )(*shards, owner_row, gains, offsets, lengths, inputs, cotangent)


def update_kernel(
    span,
    grads, owner_row, vectors, first_moment, second_moment, grad_own, grad_swap, result_own, result_swap,
    results, input_grads, own_grad, new_one, new_two, updated, updated_low,
    pieces, sem,
):
    core = lax.axis_index("tensor")
    batch = lax.axis_index("batch")
    moves = [
        pltpu.make_async_copy(source, target, sem.at[number])
        for number, (source, target) in enumerate(
            (
                (grad_own, input_grads.at[core]),
                (grad_swap, input_grads.at[1 - core]),
                (result_own, results.at[core]),
                (result_swap, results.at[1 - core]),
            )
        )
    ]
    for move in moves:
        move.start()
    cut_up(grads, span, pieces)
    slots = vectors.shape[0]
    count = owner_row.shape[1]
    owner_col = as_column(owner_row[...])
    rank = piece_ranks(owner_col, owner_row[...], 0)
    numbers = lax.broadcasted_iota(jnp.int32, (slots, count), 0)
    select = ((rank == numbers) & (owner_row[...] == batch)).astype(jnp.float32)
    filled = jnp.sum(select, axis=1, keepdims=True)
    gathered = exact(select, pieces[...])[:, :span]
    one = (FIRST_BETA * first_moment[...] + (1.0 - FIRST_BETA) * gathered) * filled
    two = (SECOND_BETA * second_moment[...] + (1.0 - SECOND_BETA) * gathered * gathered) * filled
    fixed_one = one / (1.0 - FIRST_BETA**STEP)
    fixed_two = two / (1.0 - SECOND_BETA**STEP)
    old = vectors[...]
    new = (
        old - LEARN_RATE * (fixed_one / (jnp.sqrt(fixed_two) + ADAM_EPSILON) + WEIGHT_DECAY * old)
    ) * filled
    own_grad[...] = gathered
    new_one[...] = one
    new_two[...] = two
    updated[...] = new
    updated_low[...] = low(new)
    for move in moves:
        move.wait()


def update(grads, owner_row, vectors, first_moment, second_moment, grad_own, grad_swap, result_own, result_swap):
    anywhere = pl.BlockSpec(memory_space=pl.ANY)
    on_chip = pl.BlockSpec(memory_space=pltpu.VMEM)
    half_rows = grad_own.shape[0]
    slot = jax.ShapeDtypeStruct(vectors.shape, jnp.float32)
    return pl.pallas_call(
        functools.partial(update_kernel, vectors.shape[1]),
        out_shape=(
            jax.ShapeDtypeStruct((2, half_rows, D), jnp.bfloat16),
            jax.ShapeDtypeStruct((2, half_rows, D), jnp.float32),
            slot, slot, slot, slot, jax.ShapeDtypeStruct(vectors.shape, jnp.bfloat16),
        ),
        in_specs=[on_chip] * 5 + [anywhere] * 4,
        out_specs=[on_chip] * 7,
        scratch_shapes=[pltpu.VMEM((256, 128), jnp.float32), pltpu.SemaphoreType.DMA((4,))],
    )(grads, owner_row, vectors, first_moment, second_moment, grad_own, grad_swap, result_own, result_swap)


def on_device(
    inputs, cotangent, lengths, owners, vectors, first_moment, second_moment,
    weight_in, weight_out, weight_up, weight_down, basis_a, basis_b, norm_gain, norm_bias,
):
    sub = lax.axis_size("batch") // GROUPS
    span = vectors.shape[1]
    owner_row = owners[None, :]
    shards = (
        group_rows(jnp.swapaxes(weight_in, 1, 2), 2, D // GROUPS, sub),
        group_rows(jnp.swapaxes(weight_out, 1, 2), 1, D // GROUPS, sub),
        group_rows(weight_up, 1, D // GROUPS, sub),
        group_rows(jnp.swapaxes(weight_down, 1, 2), 1, D // GROUPS, sub),
        group_rows(basis_a, 0, R // GROUPS, sub),
        group_rows(basis_b.T, 0, R // GROUPS, sub),
        group_rows(vectors, 0, 512 // GROUPS, sub),
    )
    _, _, _, grads, grad_own, grad_swap, result_own, result_swap = train(
        sub, span, shards, owner_row, norm_gain, norm_bias, lengths, inputs, cotangent
    )
    return update(
        grads, owner_row, vectors, first_moment, second_moment, grad_own, grad_swap, result_own, result_swap
    )


def solution(mesh):
    rows_spec = P(None, ("batch", "tensor"), None)
    split = P("batch", None)
    return jax.shard_map(
        on_device,
        mesh=mesh,
        in_specs=(
            rows_spec, rows_spec, P(None, "batch", None), P(), split, split, split,
            P(None, "batch", None, "tensor"), P(None, "tensor", "batch"), P(None, "batch", "tensor"),
            P(None, "tensor", "batch"), split, P("tensor", "batch"), P(), P(),
        ),
        out_specs=(rows_spec, rows_spec, split, split, split, split, split),
        check_vma=False,
    )
```

```python
import functools

import jax
import jax.numpy as jnp
from jax import lax
from jax.experimental import pallas as pl
from jax.experimental.pallas import tpu as pltpu
from jax.sharding import PartitionSpec as P

D = 768
HDIM = 64
R = 1024
LAYERS = 2
STEP = 10
HALF = 384
GROUPS = 16
BLOCKS = 24
CHUNKS = 13
LAG = 3
STRIDE = 2
AHEAD = 6
DEEP_FIRST = False

EPSILON = 1e-05
SCORE_SCALE = 0.125
MASKED_SCORE = -1000000000.0
LEARN_RATE = 0.3
WEIGHT_DECAY = 0.01
FIRST_BETA = 0.5
SECOND_BETA = 0.5
ADAM_EPSILON = 1e-08
MESH = pl.DeviceIdType.MESH

ARRIVALS = ["Si", "Sj", "Sf", "Dj", "Df", "Xo", "Xi", "Xj", "Xf", "Yo", "Yi", "Yj", "Yf", "Dxo", "Dxi", "Dyo", "Dyi"]
SLOT = {name: index for index, name in enumerate(ARRIVALS)}
FROM_SIBLING = len(ARRIVALS)
TO_SIBLING, TO_X, TO_Y, TO_IN, TO_OUT, LOCAL = range(6)
DEPTHS = 7


class Gather:
    def __init__(self, sub, pack_wide, pack, pack_vec, wide, full, vecs, send_sem, recv_sem):
        self.sub = sub
        self.owners = GROUPS * sub
        self.pack_wide, self.pack, self.pack_vec = pack_wide, pack, pack_vec
        self.wide, self.full, self.vecs = wide, full, vecs
        self.send_sem, self.recv_sem = send_sem, recv_sem
        batch = lax.axis_index("batch")
        self.batch = batch
        self.core = lax.axis_index("tensor")
        group = batch // sub
        self.lane = batch % sub
        z, p = group // 4, group % 4
        inward = 1 - 2 * (z // 2)
        self.middle = ((z + 1) // 2) % 2
        plane_i, plane_j = z + inward, z + 2 * inward
        plane_f = 6 - z - plane_i - plane_j
        self.z, self.p = z, p
        self.planes = {"o": z, "i": plane_i, "j": plane_j, "f": plane_f}
        col_x, col_y = p + 1 - 2 * (p % 2), p + 2 - 4 * (p // 2)
        self.cols = {"S": p, "X": col_x, "Y": col_y, "D": 3 - p}
        self.sibling = (batch, 1 - self.core)
        self.to_x = self.device(z, col_x)
        self.to_y = self.device(z, col_y)
        self.to_in = self.device(plane_i, p)
        self.to_out = self.device(plane_f, p)

    def device(self, plane, col):
        return ((plane * 4 + col) * self.sub + self.lane, self.core)

    def barrier(self, others):
        semaphore = pltpu.get_barrier_semaphore()
        devices = [self.sibling, self.to_x, self.to_y, self.to_in, self.to_out] + others
        for device in devices:
            pl.semaphore_signal(semaphore, inc=1, device_id=device, device_id_type=MESH)
        pl.semaphore_wait(semaphore, len(devices))

    def rows(self, chunk, half, start, count, blocks=(0, 2)):
        if chunk == 0:
            ref, size, base = self.wide, R // GROUPS, 0
        elif chunk == CHUNKS:
            ref, size, base = self.vecs, 8, 0
        else:
            ref, size, base = self.full, D // GROUPS, 2 * (chunk - 1)
        first = pl.multiple_of(start * size, min(size, 16)) if not isinstance(start, int) else start * size
        return ref.at[half, pl.ds(base + blocks[0], blocks[1]), pl.ds(first, count * size)]

    def shard(self, chunk, half, col, plane, blocks=(0, 2)):
        return self.rows(chunk, half, self.planes[plane] * 4 + self.cols[col], 1, blocks)

    def copy(self, chunk, source, target, device, send, slot):
        pltpu.make_async_remote_copy(
            src_ref=source,
            dst_ref=target,
            send_sem=self.send_sem.at[chunk, send],
            recv_sem=self.recv_sem.at[chunk, slot],
            device_id=device,
            device_id_type=MESH,
        ).start()

    def push(self, chunk, col, plane, moves, blocks=(0, 2), sibling=True, source=None):
        region = self.shard(chunk, self.core, col, plane, blocks)
        source = region if source is None else source
        for device, send, slot in moves:
            slot = SLOT[slot] if isinstance(slot, str) else slot
            self.copy(chunk, source, region, device, send, slot)
        if sibling:
            self.copy(chunk, source, region, self.sibling, TO_SIBLING, FROM_SIBLING)

    def take(self, chunk, name):
        blocks = {"x": (0, 1), "y": (1, 1)}.get(name[1:-1], (0, 2))
        region = self.shard(chunk, self.core, name[0], name[-1], blocks)
        pltpu.make_async_remote_copy(
            src_ref=region,
            dst_ref=region,
            send_sem=self.send_sem.at[chunk, TO_X],
            recv_sem=self.recv_sem.at[chunk, SLOT[name]],
            device_id=self.to_x,
            device_id_type=MESH,
        ).wait_recv()

    def when_middle(self, action):
        pl.when(self.middle == 1)(action)

    def when_end(self, action):
        pl.when(self.middle == 0)(action)

    def source(self, chunk):
        if chunk == 0:
            return self.pack_wide
        return self.pack_vec if chunk == CHUNKS else self.pack.at[pl.ds(2 * (chunk - 1), 2)]

    def local(self, chunk):
        return pltpu.make_async_copy(
            self.source(chunk), self.shard(chunk, self.core, "S", "o"), self.send_sem.at[chunk, LOCAL]
        )

    def step(self, chunk, depth):
        to_x, to_y = (self.to_x, TO_X), (self.to_y, TO_Y)
        to_in, to_out = (self.to_in, TO_IN), (self.to_out, TO_OUT)
        if depth == 0:
            source = self.source(chunk)
            arrival = self.middle * SLOT["Si"] + (1 - self.middle) * SLOT["Sf"]
            self.push(chunk, "S", "o", [(*to_in, arrival), (*to_x, "Xo"), (*to_y, "Yo")], source=source)

            @self.when_middle
            def _():
                self.push(chunk, "S", "o", [(*to_out, "Si")], sibling=False, source=source)

            self.local(chunk).start()
        elif depth == 1:
            self.take(chunk, "Si")

            @self.when_middle
            def _():
                self.push(chunk, "S", "i", [(*to_out, "Sj")], sibling=False)

            self.push(chunk, "S", "i", [(*to_x, "Xi"), (*to_y, "Yi")])
            yield

            @self.when_middle
            def _():
                self.take(chunk, "Sf")
                self.push(chunk, "S", "f", [(*to_in, "Sj"), (*to_x, "Xf"), (*to_y, "Yf")])

            yield
            yield from self.cross(chunk, "o")
        elif depth == 2:
            self.take(chunk, "Sj")

            @self.when_middle
            def _():
                self.push(chunk, "S", "j", [(*to_out, "Sf")], sibling=False)

            self.push(chunk, "S", "j", [(*to_x, "Xj"), (*to_y, "Yj")])
            yield
            self.take(chunk, "Dxo")
            self.take(chunk, "Dyo")

            @self.when_end
            def _():
                self.push(chunk, "D", "o", [(*to_in, "Df")], sibling=False)

            self.push(chunk, "D", "o", [])
            yield
            yield from self.cross(chunk, "i")

            @self.when_middle
            def _():
                self.land(chunk, "Xf", "Yf")
        elif depth == 3:
            @self.when_end
            def _():
                self.take(chunk, "Sf")
                self.push(chunk, "S", "f", [(*to_x, "Xf"), (*to_y, "Yf")])

            yield
            self.take(chunk, "Dxi")
            self.take(chunk, "Dyi")

            @self.when_middle
            def _():
                self.push(chunk, "D", "i", [(*to_out, "Dj")], sibling=False)
                self.take(chunk, "Df")
                self.push(chunk, "D", "f", [(*to_in, "Dj")])

            self.push(chunk, "D", "i", [])
            yield
            self.land(chunk, "Xj", "Yj")
        elif depth == 4:
            self.take(chunk, "Dj")

            @self.when_middle
            def _():
                self.push(chunk, "D", "j", [(*to_out, "Df")], sibling=False)

            self.push(chunk, "D", "j", [])
            yield

            @self.when_end
            def _():
                self.land(chunk, "Xf", "Yf")
        elif depth == 5:
            @self.when_end
            def _():
                self.land(chunk, "Df")
        else:
            self.local(chunk).wait()
            whole = self.rows(chunk, 1 - self.core, 0, GROUPS)
            pltpu.make_async_remote_copy(
                src_ref=whole,
                dst_ref=whole,
                send_sem=self.send_sem.at[chunk, TO_SIBLING],
                recv_sem=self.recv_sem.at[chunk, FROM_SIBLING],
                device_id=self.sibling,
                device_id_type=MESH,
            ).wait_recv()
        yield

    def cross(self, chunk, plane):
        self.take(chunk, "X" + plane)
        self.push(chunk, "X", plane, [(self.to_y, TO_Y, "Dy" + plane)], (1, 1), sibling=False)
        self.push(chunk, "X", plane, [])
        yield
        self.take(chunk, "Y" + plane)
        self.push(chunk, "Y", plane, [(self.to_x, TO_X, "Dx" + plane)], (0, 1), sibling=False)
        self.push(chunk, "Y", plane, [])
        yield

    def land(self, chunk, *names):
        for name in names:
            self.take(chunk, name)
            self.push(chunk, name[0], name[1], [])

    def sent(self, chunk, send, shards):
        region = self.rows(chunk, self.core, 0, shards)
        pltpu.make_async_remote_copy(
            src_ref=region,
            dst_ref=region,
            send_sem=self.send_sem.at[chunk, send],
            recv_sem=self.recv_sem.at[chunk, FROM_SIBLING],
            device_id=self.sibling,
            device_id_type=MESH,
        ).wait_send()

    def finish(self):
        for chunk in range(CHUNKS + 1):
            self.sent(chunk, TO_SIBLING, GROUPS)
            self.sent(chunk, TO_X, 5)
            self.sent(chunk, TO_Y, 5)

        @self.when_middle
        def _():
            for chunk in range(CHUNKS + 1):
                self.sent(chunk, TO_IN, 3)
                self.sent(chunk, TO_OUT, 5)

        @self.when_end
        def _():
            for chunk in range(CHUNKS + 1):
                self.sent(chunk, TO_IN, 2)

    def tick(self, number):
        for chunk, depth in TIMES.get(number, ()):
            yield from self.step(chunk, depth)


def timetable():
    times = {}
    for chunk in range(CHUNKS + 1):
        for depth in range(DEPTHS):
            tick = LAG * (chunk % CHUNKS) + STRIDE * depth
            if depth == 0:
                tick = max(0, tick - AHEAD)
            times.setdefault(tick, []).append((depth, chunk % CHUNKS, chunk))
    return {tick: [(chunk, depth) for depth, _, chunk in sorted(events, reverse=DEEP_FIRST)] for tick, events in times.items()}


TIMES = timetable()
TICKS = LAG * (CHUNKS - 1) + STRIDE * (DEPTHS - 1) + 1


def group_rows(values, axis, size, sub):
    if sub == 1:
        return values
    group = lax.axis_index("batch") // sub
    values = lax.all_gather(values, "batch", axis=axis, tiled=True)
    return lax.dynamic_slice_in_dim(values, group * size, size, axis)


def mm(left, right):
    return jnp.dot(left, right, preferred_element_type=jnp.float32)


def mm_t(left, right):
    return lax.dot_general(left, right, (((1,), (1,)), ((), ())), preferred_element_type=jnp.float32)


def exact(left, right):
    return jnp.dot(left, right, precision=lax.Precision.HIGHEST, preferred_element_type=jnp.float32)


def low(values):
    return values.astype(jnp.bfloat16)


def normalize(values, gain, offset):
    center = values - jnp.mean(values, axis=-1, keepdims=True)
    spread = jnp.mean(center * center, axis=-1, keepdims=True)
    return center * lax.rsqrt(spread + EPSILON) * gain + offset


def norm_back(values, gain, upstream):
    center = values - jnp.mean(values, axis=-1, keepdims=True)
    spread = jnp.mean(center * center, axis=-1, keepdims=True)
    scale = lax.rsqrt(spread + EPSILON)
    unit = center * scale
    scaled = upstream * gain
    first = jnp.mean(scaled, axis=-1, keepdims=True)
    second = jnp.mean(scaled * unit, axis=-1, keepdims=True)
    return scale * (scaled - first - unit * second)


def gelu_and_slope(values):
    bell = jnp.exp(-0.5 * values * values)
    t = 1.0 / (1.0 + 0.23164190 * jnp.abs(values))
    poly = t * (0.127414796 + t * (-0.142248368 + t * (0.7107068705 + t * (-0.7265760135 + t * 0.5307027145))))
    tail = poly * bell
    share = jnp.where(values < 0, tail, 1.0 - tail)
    return values * share, share + values * (0.3989422804 * bell)


def piece_ranks(col, row, axis):
    count = row.shape[1]
    down = lax.broadcasted_iota(jnp.int32, (count, count), 0)
    across = lax.broadcasted_iota(jnp.int32, (count, count), 1)
    earlier = (down < across) if axis == 0 else (across < down)
    return jnp.sum(((col == row) & earlier).astype(jnp.float32), axis=axis, keepdims=True).astype(jnp.int32)


SPAN_LANES = 896


def lay_out(pieces, span, flat):
    lanes = lax.broadcasted_iota(jnp.int32, (8, 128), 1)
    tiles = [jnp.zeros((8, 128), jnp.float32) for _ in range(SPAN_LANES // 128)]
    for i in range(32):
        tile, offset = divmod(span * i, 128)
        rows = pieces[pl.ds(i, 8, stride=32), :]
        rows = pltpu.roll(rows, offset, 1) if offset else rows
        inside = (lanes >= offset) & (lanes < offset + span)
        tiles[tile] = tiles[tile] + jnp.where(inside, rows, 0.0)
        if offset + span > 128:
            tiles[tile + 1] = tiles[tile + 1] + jnp.where(lanes < offset + span - 128, rows, 0.0)
    for tile, values in enumerate(tiles):
        flat[:, 128 * tile : 128 * (tile + 1)] = values


def cut_up(flat, span, pieces):
    lanes = lax.broadcasted_iota(jnp.int32, (8, 128), 1)
    for i in range(32):
        tile, offset = divmod(span * i, 128)
        rows = flat[pl.ds(tile, 8, stride=7), :]
        if offset:
            rows = pltpu.roll(rows, 128 - offset, 1)
        if offset + span > 128:
            after = pltpu.roll(flat[pl.ds(tile + 1, 8, stride=7), :], 128 - offset, 1)
            rows = jnp.where(lanes < 128 - offset, rows, after)
        pieces[pl.ds(i, 8, stride=32), :] = jnp.where(lanes < span, rows, 0.0)


def as_column(row):
    count = row.shape[1]
    down = lax.broadcasted_iota(jnp.int32, (count, count), 0)
    across = lax.broadcasted_iota(jnp.int32, (count, count), 1)
    return jnp.sum(jnp.where(down == across, row, 0).astype(jnp.float32), axis=1, keepdims=True).astype(jnp.int32)


ROW = 512
SEND_INPUT, SEND_COTANGENT, SEND_RESULT, SEND_GRAD = range(4)
FFN_SLOTS = 4
RATE = 0.3
COSTS = {
    "documents": 0.5, "start_rows": 0.5, "vectors_in": 2.0, "project": 1.0, "frozen": 1.5, "attend": 1.0,
    "attention_out": 1.0, "feed_forward": 2.0, "layer_out": 0.7,
}


class Sums:
    def __init__(self, gather, inbox, send_sem, recv_sem):
        self.gather, self.inbox, self.send_sem, self.recv_sem = gather, inbox, send_sem, recv_sem
        z, p = gather.z, gather.p
        cols = [gather.cols[name] for name in ("X", "Y", "D")]
        planes = [gather.planes[name] for name in ("i", "j", "f")]
        self.phases = [
            [(gather.sibling, 0, 0)],
            [(gather.device(z, col), 1 + p, 1 + col) for col in cols],
            [(gather.device(plane, p), 5 + z, 5 + plane) for plane in planes],
        ]
        self.own_slots = [None, 1 + p, 5 + z]
        self.ranges = [None, (1, 4), (5, 4)]
        size, slot = 1, 9
        while size < gather.sub:
            partner = gather.batch + size * (1 - 2 * ((gather.lane // size) % 2))
            self.phases.append([((partner, gather.core), slot, slot)])
            self.own_slots.append(None)
            self.ranges.append(None)
            size, slot = 2 * size, slot + 1

    def others(self):
        gather = self.gather
        found = [gather.device(gather.z, gather.cols["D"]), gather.device(gather.planes["j"], gather.p)]
        for phase in self.phases[3:]:
            found.append(phase[0][0])
        return found

    def copies(self, layer, phase, values):
        base = sum(len(moves) for moves in self.phases[:phase])
        return [
            pltpu.make_async_remote_copy(
                src_ref=values, dst_ref=self.inbox.at[layer, there], send_sem=self.send_sem.at[layer, base + number],
                recv_sem=self.recv_sem.at[layer, there], device_id=device, device_id_type=MESH,
            )
            for number, (device, there, _) in enumerate(self.phases[phase])
        ]

    def start(self, layer, phase, values):
        if self.own_slots[phase] is not None:
            self.inbox[layer, self.own_slots[phase]] = values[...]
        for copy in self.copies(layer, phase, values):
            copy.start()

    def finish(self, layer, phase, values):
        for copy, (device, _, here) in zip(self.copies(layer, phase, values), self.phases[phase]):
            copy.wait_send()
            pltpu.make_async_remote_copy(
                src_ref=values, dst_ref=self.inbox.at[layer, here], send_sem=self.send_sem.at[layer, 0],
                recv_sem=self.recv_sem.at[layer, here], device_id=device, device_id_type=MESH,
            ).wait_recv()
        if self.ranges[phase] is None:
            values[...] = values[...] + self.inbox[layer, self.phases[phase][0][2]]
        else:
            first, count = self.ranges[phase]
            values[...] = sum(self.inbox[layer, first + number] for number in range(1, count)) + self.inbox[layer, first]


def train_kernel(
    sub, span,
    weight_in, weight_out, weight_up, weight_down, basis_a, basis_b, vectors, owner_row, gains, offsets, lengths, inputs, cotangent,
    wide, full, probs, grads, grad_own, grad_swap, result_own, result_swap,
    pack, wide_pack, vec_pack, vecs, pieces, flat, trained,
    rows_low, rows, wide_v, att_v, ffn_v, qkv_v, probs_v, proj_v, proj_low, adapt_v, mixed, feed, sums_v, slopes_v,
    doc_col, doc_row, result_v, up_v, row_grads, inbox,
    send_sem, recv_sem, swap_send, swap_recv, own_sem, load_sem, save_sem, sums_send, sums_recv,
):
    gather = Gather(sub, wide_pack, pack, vec_pack, wide, full, vecs, send_sem, recv_sem)
    sums = Sums(gather, inbox, sums_send, sums_recv)
    core = gather.core
    half_rows = inputs.shape[1]
    mine = pl.ds(pl.multiple_of(core * half_rows, 16), half_rows)
    other = pl.ds(pl.multiple_of((1 - core) * half_rows, 16), half_rows)

    def swap(number, source, target):
        return pltpu.make_async_remote_copy(
            src_ref=source, dst_ref=target, send_sem=swap_send.at[number], recv_sem=swap_recv.at[number],
            device_id=gather.sibling, device_id_type=MESH,
        )

    def own(number, source, target):
        return pltpu.make_async_copy(source, target, own_sem.at[number])

    def gain(number):
        return gains[number // 2, number % 2 : number % 2 + 1, :]

    def offset(number):
        return offsets[number // 2, number % 2 : number % 2 + 1, :]

    def vector(layer, start, size):
        return trained[layer : layer + 1, start : start + size]

    wide_pack[0] = jnp.where(core == 0, basis_a[:, :HALF], basis_a[:, HALF:])
    wide_pack[1] = basis_b[...]
    padded = jnp.concatenate([vectors[...], jnp.zeros((32, 128 - span), jnp.float32)], axis=1)
    vec_pack[...] = jnp.where(core == 0, padded[:16], padded[16:]).reshape(2, 8, 128)

    for layer in range(LAYERS):
        for part in range(3):
            pack[12 * layer + part] = weight_in[layer, part]
        pack[12 * layer + 3] = weight_out[layer]
        for part in range(4):
            columns = slice(part * HALF, (part + 1) * HALF)
            pack[12 * layer + 4 + 2 * part] = weight_up[layer, :, columns]
            pack[12 * layer + 5 + 2 * part] = weight_down[layer, :, columns]

    gather.barrier(sums.others())
    swap_in = swap(SEND_INPUT, inputs.at[1 - core], rows_low.at[mine])
    swap_cot = swap(SEND_COTANGENT, cotangent.at[1 - core], up_v.at[mine])
    own_in = own(0, inputs.at[core], rows_low.at[mine])
    own_cot = own(1, cotangent.at[core], up_v.at[mine])
    swap_in.start()
    own_in.start()

    def load_wide():
        return pltpu.make_async_copy(wide, wide_v, load_sem.at[0])

    def load_att(layer, part):
        pair = pl.ds(12 * layer + 2 * part, 2)
        return pltpu.make_async_copy(full.at[:, pair], att_v.at[:, pl.ds(2 * part, 2)], load_sem.at[1 + part])

    def load_ffn(layer, part):
        pair = pl.ds(12 * layer + 4 + 2 * part, 2)
        return pltpu.make_async_copy(full.at[:, pair], ffn_v.at[part], load_sem.at[3 + part])

    def save_probs(pair):
        return pltpu.make_async_copy(probs_v.at[pair], probs.at[pair], save_sem.at[pair])

    def load_probs(pair):
        return pltpu.make_async_copy(probs.at[pair], probs_v.at[pair], save_sem.at[pair])

    def documents():
        places_col = lax.broadcasted_iota(jnp.int32, (ROW, 128), 0)
        places_row = lax.broadcasted_iota(jnp.int32, (8, ROW), 1)
        ids_col = jnp.zeros((ROW, 128), jnp.int32)
        ids_row = jnp.zeros((8, ROW), jnp.int32)
        end = jnp.int32(0)
        for number in range(lengths.shape[2]):
            end = end + lengths[core, 0, number]
            ids_col = ids_col + (places_col >= end).astype(jnp.int32)
            ids_row = ids_row + (places_row >= end).astype(jnp.int32)
        doc_col[...] = ids_col
        doc_row[...] = ids_row

    def start_rows():
        own_in.wait()
        swap_in.wait()
        rows[...] = rows_low[...].astype(jnp.float32)

    def vectors_in():
        owner_col = as_column(owner_row[...])
        slot = owner_col * (512 // gather.owners) + piece_ranks(owner_col, owner_row[...], 1)
        place = ((slot >> 3) & 3) * 128 + (slot >> 5) * 8 + (slot & 7)
        spots = lax.broadcasted_iota(jnp.int32, (slot.shape[0], 512), 1)
        select = (place == spots).astype(jnp.float32)
        pieces[...] = exact(select, vecs[...].reshape(512, 128))
        lay_out(pieces, span, flat)
        for number in range(8):
            layer, part = divmod(number, 4)
            trained[layer : layer + 1, SPAN_LANES * part : SPAN_LANES * (part + 1)] = flat[number : number + 1, :]

    def project(layer):
        if layer == 0:
            load_wide().wait()
        proj_v[...] = mm_t(rows_low[:, :HALF], wide_v[0, 0]) + mm_t(rows_low[:, HALF:], wide_v[1, 0])
        proj_low[layer] = low(proj_v[...])

    def frozen(layer, part, half):
        if half == 0:
            load_att(layer, part).wait()
        for number in ((0, 1) if part == 0 else (2,)):
            values = mm(rows_low[...], att_v[half, number])
            if number != 1:
                start = (0, None, 1)[number]
                bias = vector(layer, 2 * R + start * D + half * HALF, HALF)
                scale = vector(layer, start * R, R)
                adapted = mm(low(scale * proj_v[...]), wide_v[half, 1])
                adapt_v[layer, start, :, half * HALF : (half + 1) * HALF] = low(adapted)
                values = values + bias * adapted
            values = low(values)
            for third in range(3):
                qkv_v[layer, 3 * half + third, number] = values[:, 128 * third : 128 * (third + 1)]

    def attend(layer, pair):
        if layer > 0:
            save_probs(pair).wait()
        query = qkv_v[layer, pair, 0].astype(jnp.float32) * SCORE_SCALE
        query_t = low(query.T)
        value_t = low(qkv_v[layer, pair, 2].astype(jnp.float32).T)
        key = qkv_v[layer, pair, 1]
        ids_col = doc_col[...]
        same = jnp.concatenate([ids_col] * 4, axis=1) == doc_row[0:1, :]
        zeros = jnp.zeros((HDIM, ROW), jnp.bfloat16)
        masked = ([query_t[:HDIM], zeros], [zeros, query_t[HDIM:]])
        products = [mm(key, jnp.concatenate(parts, axis=0)) for parts in masked]
        chances = []
        for head in range(2):
            scores = jnp.where(same, products[head], MASKED_SCORE)
            raised = jnp.exp(scores - jnp.max(scores, axis=0, keepdims=True))
            chances.append(low(raised * (1.0 / jnp.sum(raised, axis=0, keepdims=True))))
            probs_v[pair, head] = chances[head]
        mixed_t = [mm(value_t[head * HDIM : (head + 1) * HDIM], chances[head]) for head in range(2)]
        mixed[:, 128 * pair : 128 * (pair + 1)] = low(jnp.concatenate(mixed_t, axis=0).T)
        if layer < LAYERS - 1:
            save_probs(pair).start()

    def attention_out(layer):
        total = rows[...] + mm_t(mixed[:, :HALF], att_v[0, 3]) + mm_t(mixed[:, HALF:], att_v[1, 3])
        sums_v[layer, 0] = total
        middle = normalize(total, gain(2 * layer), offset(2 * layer))
        rows[...] = middle
        rows_low[...] = low(middle)

    def feed_forward(layer, part):
        load_ffn(layer, part).wait()
        before = [mm(rows_low[...], ffn_v[part, half, 0]) for half in range(2)]
        active = []
        for half in range(2):
            values, slope = gelu_and_slope(before[half])
            slopes_v[layer, part, half] = low(slope)
            active.append(low(values))
        term = mm_t(active[0], ffn_v[part, 0, 1]) + mm_t(active[1], ffn_v[part, 1, 1])
        if part == 0:
            feed[...] = term
        else:
            feed[...] += term

    def layer_out(layer):
        total = rows[...] + feed[...]
        sums_v[layer, 1] = total
        values = normalize(total, gain(2 * layer + 1), offset(2 * layer + 1))
        if layer == LAYERS - 1:
            result_v[...] = low(values)
        else:
            rows[...] = values
            rows_low[...] = low(values)

    def ready(chunk):
        return LAG * chunk + STRIDE * (DEPTHS - 1)

    queue = []

    def add(tick, task, *arguments):
        queue.append((tick, functools.partial(task, *arguments)))

    add(0, documents)
    add(1, start_rows)
    add(ready(0), vectors_in)
    add(ready(0), project, 0)
    for layer in range(LAYERS):
        first = 1 + 6 * layer
        if layer > 0:
            add(0, project, layer)
        for part in range(2):
            for half in range(2):
                add(ready(first + part), frozen, layer, part, half)
        for pair in range(6):
            add(0, attend, layer, pair)
        add(0, attention_out, layer)
        for part in range(4):
            add(ready(first + 2 + part), feed_forward, layer, part)
        add(0, layer_out, layer)

    ffn_order = [(layer, part) for layer in range(LAYERS) for part in range(4)]
    counts = {"ffn_started": 0, "ffn_done": 0, "att_done": 0}
    att_started = set()

    def start_loads(number):
        while counts["ffn_started"] < min(len(ffn_order), counts["ffn_done"] + FFN_SLOTS):
            layer, part = ffn_order[counts["ffn_started"]]
            if ready(3 + 6 * layer + part) > number:
                break
            load_ffn(layer, part).start()
            counts["ffn_started"] += 1
        for layer in range(LAYERS):
            for part in range(2):
                if (layer, part) in att_started or ready(1 + 6 * layer + part) > number or counts["att_done"] < layer:
                    continue
                load_att(layer, part).start()
                att_started.add((layer, part))

    def run(position, number):
        task = queue[position][1]
        name = task.func.__name__
        task()
        counts["ffn_done"] += name == "feed_forward"
        counts["att_done"] += name == "attention_out"
        start_loads(number)
        return COSTS[name]

    state = {"credit": 0.0, "position": 0}

    def work(number):
        while state["position"] < len(queue) and queue[state["position"]][0] < number and state["credit"] > 0:
            state["credit"] -= run(state["position"], number - 1)
            state["position"] += 1

    for number in range(TICKS):
        for _ in gather.tick(number):
            state["credit"] = min(state["credit"] + RATE, 1.0)
            work(number)
        if number == 0:
            swap_cot.start()
            own_cot.start()
        if number == ready(0):
            load_wide().start()
        start_loads(number)
    while state["position"] < len(queue):
        run(state["position"], TICKS - 1)
        state["position"] += 1

    swap_out = swap(SEND_RESULT, result_v.at[other], result_swap)
    own_out = own(2, result_v.at[mine], result_own)
    swap_out.start()
    own_out.start()

    def feed_back(layer, part):
        if (layer, part) not in resident:
            load_ffn(layer, part).wait()
        active = [mm(rows_low[...], ffn_v[part, half, 1]) for half in range(2)]
        before = [low(active[half] * slopes_v[layer, part, half].astype(jnp.float32)) for half in range(2)]
        feed[...] += mm_t(before[0], ffn_v[part, 0, 0]) + mm_t(before[1], ffn_v[part, 1, 0])

    def attend_back(layer, pair):
        lanes = slice(128 * pair, 128 * (pair + 1))
        query, key, value = qkv_v[layer, pair, 0], qkv_v[layer, pair, 1], qkv_v[layer, pair, 2]
        outer = mixed[:, lanes]
        outer_t = low(outer.astype(jnp.float32).T)
        key_t = low(key.astype(jnp.float32).T)
        zeros = jnp.zeros((HDIM, ROW), jnp.bfloat16)
        query_t, keys, values = [], [], []
        for head in range(2):
            part = slice(head * HDIM, (head + 1) * HDIM)
            masked = [outer_t[part], zeros] if head == 0 else [zeros, outer_t[part]]
            chances_low = probs_v[pair, head]
            chances = chances_low.astype(jnp.float32)
            chance_grad = mm(value, jnp.concatenate(masked, axis=0))
            inner = jnp.sum(chances * chance_grad, axis=0, keepdims=True)
            score_grad = low(chances * (chance_grad - inner))
            values.append(mm(chances_low, outer))
            keys.append(mm(score_grad, query))
            query_t.append(mm(key_t[part], score_grad))
        left = lax.broadcasted_iota(jnp.int32, (ROW, 128), 1) < HDIM
        row_grads[0, :, lanes] = low(SCORE_SCALE * jnp.concatenate(query_t, axis=0).T)
        row_grads[1, :, lanes] = low(SCORE_SCALE * jnp.where(left, keys[0], keys[1]))
        row_grads[2, :, lanes] = low(jnp.where(left, values[0], values[1]))

    def vector_back(layer):
        found = {}
        combined = None
        for number, start in ((0, 0), (2, 1)):
            row = row_grads[number].astype(jnp.float32)
            bias = vector(layer, 2 * R + start * D, D)
            scale = vector(layer, start * R, R)
            found[2 + start] = jnp.sum(row * adapt_v[layer, start].astype(jnp.float32), axis=0, keepdims=True)
            back = low(bias * row)
            source = mm_t(back[:, :HALF], wide_v[0, 1]) + mm_t(back[:, HALF:], wide_v[1, 1])
            found[start] = jnp.sum(source * proj_low[layer].astype(jnp.float32), axis=0, keepdims=True)
            combined = scale * source if combined is None else combined + scale * source
        proj_low[layer] = low(combined)
        number = 0
        for start in range(4):
            for tile in range(found[start].shape[1] // 128):
                grads[layer, number : number + 1, :] = found[start][:, 128 * tile : 128 * (tile + 1)]
                number += 1
        grads[layer, number:, :] = jnp.zeros((32 - number, 128), jnp.float32)

    def input_back(layer, which):
        for half in range(2):
            part = slice(half * HALF, (half + 1) * HALF)
            rows[which, part] += mm(proj_low[layer, which], wide_v[half, 0])
        total = rows[which, :]
        for half in range(2):
            part = slice(half * HALF, (half + 1) * HALF)
            for number in range(3):
                total = total + mm_t(row_grads[number, which, part], att_v[half, number])
        rows[which, :] = total

    last = LAYERS - 1
    resident = {(last, part) for part in range(4)}
    own_cot.wait()
    swap_cot.wait()
    rows[...] = up_v[...].astype(jnp.float32)
    phases = len(sums.phases)
    pending = []
    for layer in reversed(range(LAYERS)):
        values = norm_back(sums_v[layer, 1], gain(2 * layer + 1), rows[...])
        rows_low[...] = low(values)
        feed[...] = values
        for part in reversed(range(4)):
            feed_back(layer, part)
            if layer > 0:
                load_ffn(layer - 1, part).start()
            if pending:
                pending.pop(0)()
        values = norm_back(sums_v[layer, 0], gain(2 * layer), feed[...])
        rows[...] = values
        rows_low[...] = low(values)
        if layer < last:
            for part in range(2):
                load_att(layer, part).wait()
        for half in range(2):
            mixed[:, half * HALF : (half + 1) * HALF] = low(mm(rows_low[...], att_v[half, 3]))
        for pair in range(6):
            if layer < last:
                load_probs(pair).wait()
            attend_back(layer, pair)
            if layer > 0:
                load_probs(pair).start()
            if pending:
                pending.pop(0)()
        vector_back(layer)
        values = grads.at[layer]
        sums.start(layer, 0, values)

        def advance(layer, phase, values):
            sums.finish(layer, phase, values)
            if phase + 1 < phases:
                sums.start(layer, phase + 1, values)

        steps = [functools.partial(advance, layer, phase, values) for phase in range(phases)]
        if layer > 0:
            input_back(layer, slice(None))
            for part in range(2):
                load_att(layer - 1, part).start()
            pending = steps
        else:
            while pending:
                pending.pop(0)()
            gather.finish()
            input_back(layer, other)
            swap_grad = swap(SEND_GRAD, rows.at[other], grad_swap)
            swap_grad.start()
            steps.pop(0)()
            input_back(layer, mine)
            own_grad = own(3, rows.at[mine], grad_own)
            own_grad.start()
            for step in steps:
                step()

    own_out.wait()
    swap_out.wait()
    own_grad.wait()
    swap_grad.wait()


def train(sub, span, shards, owner_row, gains, offsets, lengths, inputs, cotangent):
    anywhere = pl.BlockSpec(memory_space=pl.ANY)
    on_chip = pl.BlockSpec(memory_space=pltpu.VMEM)
    scalars = pl.BlockSpec(memory_space=pltpu.SMEM)
    shape = jax.ShapeDtypeStruct
    bf16, f32 = jnp.bfloat16, jnp.float32
    vmem = pltpu.VMEM
    dma = pltpu.SemaphoreType.DMA
    half_rows = inputs.shape[1]
    slots = 9 + (sub.bit_length() - 1)
    return pl.pallas_call(
        functools.partial(train_kernel, sub, span),
        out_shape=(
            shape((2, 2, R, HALF), bf16),
            shape((2, BLOCKS, D, HALF), bf16),
            shape((6, 2, ROW, ROW), bf16),
            shape((LAYERS, 32, 128), f32),
            shape((half_rows, D), f32),
            shape((half_rows, D), f32),
            shape((half_rows, D), bf16),
            shape((half_rows, D), bf16),
        ),
        in_specs=[on_chip] * 10 + [scalars] + [anywhere] * 2,
        out_specs=[anywhere] * 3 + [on_chip] + [anywhere] * 4,
        scratch_shapes=[
            vmem((BLOCKS, D // GROUPS, HALF), bf16),
            vmem((2, 64, HALF), bf16),
            vmem((2, 8, 128), f32),
            vmem((2, 2, 128, 128), f32),
            vmem((256, 128), f32),
            vmem((8, SPAN_LANES), f32),
            vmem((LAYERS, 4 * SPAN_LANES), f32),
            vmem((ROW, D), bf16),
            vmem((ROW, D), f32),
            vmem((2, 2, R, HALF), bf16),
            vmem((2, 4, D, HALF), bf16),
            vmem((4, 2, 2, D, HALF), bf16),
            vmem((LAYERS, 6, 3, ROW, 128), bf16),
            vmem((6, 2, ROW, ROW), bf16),
            vmem((ROW, R), f32),
            vmem((LAYERS, ROW, R), bf16),
            vmem((LAYERS, 2, ROW, D), bf16),
            vmem((ROW, D), bf16),
            vmem((ROW, D), f32),
            vmem((LAYERS, 2, ROW, D), f32),
            vmem((LAYERS, 4, 2, ROW, HALF), bf16),
            vmem((ROW, 128), jnp.int32),
            vmem((8, ROW), jnp.int32),
            vmem((ROW, D), bf16),
            vmem((ROW, D), bf16),
            vmem((3, ROW, D), bf16),
            vmem((LAYERS, slots, 32, 128), f32),
            dma((CHUNKS + 1, 6)),
            dma((CHUNKS + 1, len(ARRIVALS) + 1)),
            dma((4,)),
            dma((4,)),
            dma((4,)),
            dma((7,)),
            dma((6,)),
            dma((LAYERS, slots)),
            dma((LAYERS, slots)),
        ],
        compiler_params=pltpu.CompilerParams(
            collective_id=0, has_side_effects=True, vmem_limit_bytes=63 * 1024 * 1024
        ),
        cost_estimate=pl.CostEstimate(flops=4 * 10**10, bytes_accessed=10**8, transcendentals=10**7),
    )(*shards, owner_row, gains, offsets, lengths, inputs, cotangent)


def update_kernel(
    span,
    grads, owner_row, vectors, first_moment, second_moment, grad_own, grad_swap, result_own, result_swap,
    results, input_grads, own_grad, new_one, new_two, updated, updated_low,
    flat, pieces, grad_rows, result_rows, load_sem, store_sem,
):
    core = lax.axis_index("tensor")
    batch = lax.axis_index("batch")
    half = grad_own.shape[0] // 2
    loads, stores = [], []
    for source, staged, target, place in (
        (grad_own, grad_rows, input_grads, core),
        (grad_swap, grad_rows, input_grads, 1 - core),
        (result_own, result_rows, results, core),
        (result_swap, result_rows, results, 1 - core),
    ):
        for start in (0, half):
            rows, number = pl.ds(start, half), len(loads)
            there = staged.at[number // 2 % 2, rows]
            loads.append(pltpu.make_async_copy(source.at[rows], there, load_sem.at[number]))
            stores.append(pltpu.make_async_copy(there, target.at[place, rows], store_sem.at[number]))
    for load in loads:
        load.start()
    flat[0:28, :] = grads[0, 0:28, :]
    flat[28:56, :] = grads[1, 0:28, :]
    cut_up(flat, span, pieces)
    for load, store in zip(loads, stores):
        load.wait()
        store.start()
    slots = vectors.shape[0]
    count = owner_row.shape[1]
    owner_col = as_column(owner_row[...])
    rank = piece_ranks(owner_col, owner_row[...], 0)
    numbers = lax.broadcasted_iota(jnp.int32, (slots, count), 0)
    select = ((rank == numbers) & (owner_row[...] == batch)).astype(jnp.float32)
    filled = jnp.sum(select, axis=1, keepdims=True)
    gathered = exact(select, pieces[...])[:, :span]
    one = (FIRST_BETA * first_moment[...] + (1.0 - FIRST_BETA) * gathered) * filled
    two = (SECOND_BETA * second_moment[...] + (1.0 - SECOND_BETA) * gathered * gathered) * filled
    fixed_one = one / (1.0 - FIRST_BETA**STEP)
    fixed_two = two / (1.0 - SECOND_BETA**STEP)
    old = vectors[...]
    new = (
        old - LEARN_RATE * (fixed_one / (jnp.sqrt(fixed_two) + ADAM_EPSILON) + WEIGHT_DECAY * old)
    ) * filled
    own_grad[...] = gathered
    new_one[...] = one
    new_two[...] = two
    updated[...] = new
    updated_low[...] = low(new)
    for store in stores:
        store.wait()


def update(grads, owner_row, vectors, first_moment, second_moment, grad_own, grad_swap, result_own, result_swap):
    anywhere = pl.BlockSpec(memory_space=pl.ANY)
    on_chip = pl.BlockSpec(memory_space=pltpu.VMEM)
    half_rows = grad_own.shape[0]
    slot = jax.ShapeDtypeStruct(vectors.shape, jnp.float32)
    return pl.pallas_call(
        functools.partial(update_kernel, vectors.shape[1]),
        out_shape=(
            jax.ShapeDtypeStruct((2, half_rows, D), jnp.bfloat16),
            jax.ShapeDtypeStruct((2, half_rows, D), jnp.float32),
            slot, slot, slot, slot, jax.ShapeDtypeStruct(vectors.shape, jnp.bfloat16),
        ),
        in_specs=[on_chip] * 5 + [anywhere] * 4,
        out_specs=[anywhere] * 2 + [on_chip] * 5,
        scratch_shapes=[
            pltpu.VMEM((56, 128), jnp.float32),
            pltpu.VMEM((256, 128), jnp.float32),
            pltpu.VMEM((2, half_rows, D), jnp.float32),
            pltpu.VMEM((2, half_rows, D), jnp.bfloat16),
            pltpu.SemaphoreType.DMA((8,)),
            pltpu.SemaphoreType.DMA((8,)),
        ],
    )(grads, owner_row, vectors, first_moment, second_moment, grad_own, grad_swap, result_own, result_swap)


def on_device(
    inputs, cotangent, lengths, owners, vectors, first_moment, second_moment,
    weight_in, weight_out, weight_up, weight_down, basis_a, basis_b, norm_gain, norm_bias,
):
    sub = lax.axis_size("batch") // GROUPS
    span = vectors.shape[1]
    owner_row = owners[None, :]
    shards = (
        group_rows(jnp.swapaxes(weight_in, 1, 2), 2, D // GROUPS, sub),
        group_rows(jnp.swapaxes(weight_out, 1, 2), 1, D // GROUPS, sub),
        group_rows(weight_up, 1, D // GROUPS, sub),
        group_rows(jnp.swapaxes(weight_down, 1, 2), 1, D // GROUPS, sub),
        group_rows(basis_a, 0, R // GROUPS, sub),
        group_rows(basis_b.T, 0, R // GROUPS, sub),
        group_rows(vectors, 0, 512 // GROUPS, sub),
    )
    _, _, _, grads, grad_own, grad_swap, result_own, result_swap = train(
        sub, span, shards, owner_row, norm_gain, norm_bias, lengths, inputs, cotangent
    )
    return update(
        grads, owner_row, vectors, first_moment, second_moment, grad_own, grad_swap, result_own, result_swap
    )


def solution(mesh):
    rows_spec = P(None, ("batch", "tensor"), None)
    split = P("batch", None)
    return jax.shard_map(
        on_device,
        mesh=mesh,
        in_specs=(
            rows_spec, rows_spec, P(None, "batch", None), P(), split, split, split,
            P(None, "batch", None, "tensor"), P(None, "tensor", "batch"), P(None, "batch", "tensor"),
            P(None, "tensor", "batch"), split, P("tensor", "batch"), P(), P(),
        ),
        out_specs=(rows_spec, rows_spec, split, split, split, split, split),
        check_vma=False,
    )
```

```python
import functools

import jax
import jax.numpy as jnp
from jax import lax
from jax.experimental import pallas as pl
from jax.experimental.pallas import tpu as pltpu
from jax.sharding import PartitionSpec as P

D = 768
HDIM = 64
R = 1024
LAYERS = 2
STEP = 10
HALF = 384
GROUPS = 16
BLOCKS = 24
CHUNKS = 13
LAG = 3
STRIDE = 2
AHEAD = 6
DEEP_FIRST = False

EPSILON = 1e-05
SCORE_SCALE = 0.125
MASKED_SCORE = -1000000000.0
LEARN_RATE = 0.3
WEIGHT_DECAY = 0.01
FIRST_BETA = 0.5
SECOND_BETA = 0.5
ADAM_EPSILON = 1e-08
MESH = pl.DeviceIdType.MESH

ARRIVALS = ["Si", "Sj", "Sf", "Dj", "Df", "Xo", "Xi", "Xj", "Xf", "Yo", "Yi", "Yj", "Yf", "Dxo", "Dxi", "Dyo", "Dyi"]
SLOT = {name: index for index, name in enumerate(ARRIVALS)}
FROM_SIBLING = len(ARRIVALS)
TO_SIBLING, TO_X, TO_Y, TO_IN, TO_OUT, LOCAL = range(6)
DEPTHS = 7


class Gather:
    def __init__(self, sub, pack_wide, pack, pack_vec, wide, full, vecs, send_sem, recv_sem):
        self.sub = sub
        self.owners = GROUPS * sub
        self.pack_wide, self.pack, self.pack_vec = pack_wide, pack, pack_vec
        self.wide, self.full, self.vecs = wide, full, vecs
        self.send_sem, self.recv_sem = send_sem, recv_sem
        batch = lax.axis_index("batch")
        self.batch = batch
        self.core = lax.axis_index("tensor")
        group = batch // sub
        self.lane = batch % sub
        z, p = group // 4, group % 4
        inward = 1 - 2 * (z // 2)
        self.middle = ((z + 1) // 2) % 2
        plane_i, plane_j = z + inward, z + 2 * inward
        plane_f = 6 - z - plane_i - plane_j
        self.z, self.p = z, p
        self.planes = {"o": z, "i": plane_i, "j": plane_j, "f": plane_f}
        col_x, col_y = p + 1 - 2 * (p % 2), p + 2 - 4 * (p // 2)
        self.cols = {"S": p, "X": col_x, "Y": col_y, "D": 3 - p}
        self.sibling = (batch, 1 - self.core)
        self.to_x = self.device(z, col_x)
        self.to_y = self.device(z, col_y)
        self.to_in = self.device(plane_i, p)
        self.to_out = self.device(plane_f, p)

    def device(self, plane, col):
        return ((plane * 4 + col) * self.sub + self.lane, self.core)

    def greet(self, others):
        devices = [self.sibling, self.to_x, self.to_y, self.to_in, self.to_out] + others
        for device in devices:
            pl.semaphore_signal(pltpu.get_barrier_semaphore(), inc=1, device_id=device, device_id_type=MESH)
        return len(devices)

    def rows(self, chunk, half, start, count, blocks=(0, 2)):
        if chunk == 0:
            ref, size, base = self.wide, R // GROUPS, 0
        elif chunk == CHUNKS:
            ref, size, base = self.vecs, 8, 0
        else:
            ref, size, base = self.full, D // GROUPS, 2 * (chunk - 1)
        first = pl.multiple_of(start * size, min(size, 16)) if not isinstance(start, int) else start * size
        return ref.at[half, pl.ds(base + blocks[0], blocks[1]), pl.ds(first, count * size)]

    def shard(self, chunk, half, col, plane, blocks=(0, 2)):
        return self.rows(chunk, half, self.planes[plane] * 4 + self.cols[col], 1, blocks)

    def copy(self, chunk, source, target, device, send, slot):
        pltpu.make_async_remote_copy(
            src_ref=source,
            dst_ref=target,
            send_sem=self.send_sem.at[chunk, send],
            recv_sem=self.recv_sem.at[chunk, slot],
            device_id=device,
            device_id_type=MESH,
        ).start()

    def push(self, chunk, col, plane, moves, blocks=(0, 2), sibling=True, source=None):
        region = self.shard(chunk, self.core, col, plane, blocks)
        source = region if source is None else source
        for device, send, slot in moves:
            slot = SLOT[slot] if isinstance(slot, str) else slot
            self.copy(chunk, source, region, device, send, slot)
        if sibling:
            self.copy(chunk, source, region, self.sibling, TO_SIBLING, FROM_SIBLING)

    def take(self, chunk, name):
        blocks = {"x": (0, 1), "y": (1, 1)}.get(name[1:-1], (0, 2))
        region = self.shard(chunk, self.core, name[0], name[-1], blocks)
        pltpu.make_async_remote_copy(
            src_ref=region,
            dst_ref=region,
            send_sem=self.send_sem.at[chunk, TO_X],
            recv_sem=self.recv_sem.at[chunk, SLOT[name]],
            device_id=self.to_x,
            device_id_type=MESH,
        ).wait_recv()

    def when_middle(self, action):
        pl.when(self.middle == 1)(action)

    def when_end(self, action):
        pl.when(self.middle == 0)(action)

    def source(self, chunk):
        if chunk == 0:
            return self.pack_wide
        return self.pack_vec if chunk == CHUNKS else self.pack.at[pl.ds(2 * (chunk - 1), 2)]

    def local(self, chunk):
        return pltpu.make_async_copy(
            self.source(chunk), self.shard(chunk, self.core, "S", "o"), self.send_sem.at[chunk, LOCAL]
        )

    def step(self, chunk, depth):
        to_x, to_y = (self.to_x, TO_X), (self.to_y, TO_Y)
        to_in, to_out = (self.to_in, TO_IN), (self.to_out, TO_OUT)
        if depth == 0:
            source = self.source(chunk)
            arrival = self.middle * SLOT["Si"] + (1 - self.middle) * SLOT["Sf"]
            self.push(chunk, "S", "o", [(*to_in, arrival), (*to_x, "Xo"), (*to_y, "Yo")], source=source)

            @self.when_middle
            def _():
                self.push(chunk, "S", "o", [(*to_out, "Si")], sibling=False, source=source)

            self.local(chunk).start()
        elif depth == 1:
            self.take(chunk, "Si")

            @self.when_middle
            def _():
                self.push(chunk, "S", "i", [(*to_out, "Sj")], sibling=False)

            self.push(chunk, "S", "i", [(*to_x, "Xi"), (*to_y, "Yi")])
            yield

            @self.when_middle
            def _():
                self.take(chunk, "Sf")
                self.push(chunk, "S", "f", [(*to_in, "Sj"), (*to_x, "Xf"), (*to_y, "Yf")])

            yield
            yield from self.cross(chunk, "o")
        elif depth == 2:
            self.take(chunk, "Sj")

            @self.when_middle
            def _():
                self.push(chunk, "S", "j", [(*to_out, "Sf")], sibling=False)

            self.push(chunk, "S", "j", [(*to_x, "Xj"), (*to_y, "Yj")])
            yield
            self.take(chunk, "Dxo")
            self.take(chunk, "Dyo")

            @self.when_end
            def _():
                self.push(chunk, "D", "o", [(*to_in, "Df")], sibling=False)

            self.push(chunk, "D", "o", [])
            yield
            yield from self.cross(chunk, "i")

            @self.when_middle
            def _():
                self.land(chunk, "Xf", "Yf")
        elif depth == 3:
            @self.when_end
            def _():
                self.take(chunk, "Sf")
                self.push(chunk, "S", "f", [(*to_x, "Xf"), (*to_y, "Yf")])

            yield
            self.take(chunk, "Dxi")
            self.take(chunk, "Dyi")

            @self.when_middle
            def _():
                self.push(chunk, "D", "i", [(*to_out, "Dj")], sibling=False)
                self.take(chunk, "Df")
                self.push(chunk, "D", "f", [(*to_in, "Dj")])

            self.push(chunk, "D", "i", [])
            yield
            self.land(chunk, "Xj", "Yj")
        elif depth == 4:
            self.take(chunk, "Dj")

            @self.when_middle
            def _():
                self.push(chunk, "D", "j", [(*to_out, "Df")], sibling=False)

            self.push(chunk, "D", "j", [])
            yield

            @self.when_end
            def _():
                self.land(chunk, "Xf", "Yf")
        elif depth == 5:
            @self.when_end
            def _():
                self.land(chunk, "Df")
        else:
            self.local(chunk).wait()
            whole = self.rows(chunk, 1 - self.core, 0, GROUPS)
            pltpu.make_async_remote_copy(
                src_ref=whole,
                dst_ref=whole,
                send_sem=self.send_sem.at[chunk, TO_SIBLING],
                recv_sem=self.recv_sem.at[chunk, FROM_SIBLING],
                device_id=self.sibling,
                device_id_type=MESH,
            ).wait_recv()
        yield

    def cross(self, chunk, plane):
        self.take(chunk, "X" + plane)
        self.push(chunk, "X", plane, [(self.to_y, TO_Y, "Dy" + plane)], (1, 1), sibling=False)
        self.push(chunk, "X", plane, [])
        yield
        self.take(chunk, "Y" + plane)
        self.push(chunk, "Y", plane, [(self.to_x, TO_X, "Dx" + plane)], (0, 1), sibling=False)
        self.push(chunk, "Y", plane, [])
        yield

    def land(self, chunk, *names):
        for name in names:
            self.take(chunk, name)
            self.push(chunk, name[0], name[1], [])

    def sent(self, chunk, send, shards):
        region = self.rows(chunk, self.core, 0, shards)
        pltpu.make_async_remote_copy(
            src_ref=region,
            dst_ref=region,
            send_sem=self.send_sem.at[chunk, send],
            recv_sem=self.recv_sem.at[chunk, FROM_SIBLING],
            device_id=self.sibling,
            device_id_type=MESH,
        ).wait_send()

    def finish(self):
        for chunk in range(CHUNKS + 1):
            self.sent(chunk, TO_SIBLING, GROUPS)
            self.sent(chunk, TO_X, 5)
            self.sent(chunk, TO_Y, 5)

        @self.when_middle
        def _():
            for chunk in range(CHUNKS + 1):
                self.sent(chunk, TO_IN, 3)
                self.sent(chunk, TO_OUT, 5)

        @self.when_end
        def _():
            for chunk in range(CHUNKS + 1):
                self.sent(chunk, TO_IN, 2)

    def tick(self, number):
        for chunk, depth in TIMES.get(number, ()):
            yield from self.step(chunk, depth)


def timetable():
    times = {}
    for chunk in range(CHUNKS + 1):
        for depth in range(DEPTHS):
            tick = LAG * (chunk % CHUNKS) + STRIDE * depth
            if depth == 0:
                tick = max(0, tick - AHEAD)
            times.setdefault(tick, []).append((depth, chunk % CHUNKS, chunk))
    return {tick: [(chunk, depth) for depth, _, chunk in sorted(events, reverse=DEEP_FIRST)] for tick, events in times.items()}


TIMES = timetable()
TICKS = LAG * (CHUNKS - 1) + STRIDE * (DEPTHS - 1) + 1


def group_rows(values, axis, size, sub):
    if sub == 1:
        return values
    group = lax.axis_index("batch") // sub
    values = lax.all_gather(values, "batch", axis=axis, tiled=True)
    return lax.dynamic_slice_in_dim(values, group * size, size, axis)


def mm(left, right):
    return jnp.dot(left, right, preferred_element_type=jnp.float32)


def mm_t(left, right):
    return lax.dot_general(left, right, (((1,), (1,)), ((), ())), preferred_element_type=jnp.float32)


def beside(left, right):
    return jnp.concatenate([left, right], axis=1)


def exact(left, right):
    return jnp.dot(left, right, precision=lax.Precision.HIGHEST, preferred_element_type=jnp.float32)


def low(values):
    return values.astype(jnp.bfloat16)


def normalize(values, gain, offset):
    center = values - jnp.mean(values, axis=-1, keepdims=True)
    spread = jnp.mean(center * center, axis=-1, keepdims=True)
    return center * lax.rsqrt(spread + EPSILON) * gain + offset


def norm_back(values, gain, upstream):
    center = values - jnp.mean(values, axis=-1, keepdims=True)
    spread = jnp.mean(center * center, axis=-1, keepdims=True)
    scale = lax.rsqrt(spread + EPSILON)
    unit = center * scale
    scaled = upstream * gain
    first = jnp.mean(scaled, axis=-1, keepdims=True)
    second = jnp.mean(scaled * unit, axis=-1, keepdims=True)
    return scale * (scaled - first - unit * second)


def gelu_and_slope(values):
    bell = jnp.exp(-0.5 * values * values)
    t = 1.0 / (1.0 + 0.23164190 * jnp.abs(values))
    poly = t * (0.127414796 + t * (-0.142248368 + t * (0.7107068705 + t * (-0.7265760135 + t * 0.5307027145))))
    tail = poly * bell
    share = jnp.where(values < 0, tail, 1.0 - tail)
    return values * share, share + values * (0.3989422804 * bell)


def piece_ranks(col, row, axis):
    count = row.shape[1]
    down = lax.broadcasted_iota(jnp.int32, (count, count), 0)
    across = lax.broadcasted_iota(jnp.int32, (count, count), 1)
    earlier = (down < across) if axis == 0 else (across < down)
    return jnp.sum(((col == row) & earlier).astype(jnp.float32), axis=axis, keepdims=True).astype(jnp.int32)


SPAN_LANES = 896


def lay_out(pieces, span, flat):
    lanes = lax.broadcasted_iota(jnp.int32, (8, 128), 1)
    tiles = [jnp.zeros((8, 128), jnp.float32) for _ in range(SPAN_LANES // 128)]
    for i in range(32):
        tile, offset = divmod(span * i, 128)
        rows = pieces[pl.ds(i, 8, stride=32), :]
        rows = pltpu.roll(rows, offset, 1) if offset else rows
        inside = (lanes >= offset) & (lanes < offset + span)
        tiles[tile] = tiles[tile] + jnp.where(inside, rows, 0.0)
        if offset + span > 128:
            tiles[tile + 1] = tiles[tile + 1] + jnp.where(lanes < offset + span - 128, rows, 0.0)
    for tile, values in enumerate(tiles):
        flat[:, 128 * tile : 128 * (tile + 1)] = values


def cut_up(flat, span, pieces):
    lanes = lax.broadcasted_iota(jnp.int32, (8, 128), 1)
    for i in range(32):
        tile, offset = divmod(span * i, 128)
        rows = flat[pl.ds(tile, 8, stride=7), :]
        if offset:
            rows = pltpu.roll(rows, 128 - offset, 1)
        if offset + span > 128:
            after = pltpu.roll(flat[pl.ds(tile + 1, 8, stride=7), :], 128 - offset, 1)
            rows = jnp.where(lanes < 128 - offset, rows, after)
        pieces[pl.ds(i, 8, stride=32), :] = jnp.where(lanes < span, rows, 0.0)


def as_column(row):
    count = row.shape[1]
    down = lax.broadcasted_iota(jnp.int32, (count, count), 0)
    across = lax.broadcasted_iota(jnp.int32, (count, count), 1)
    return jnp.sum(jnp.where(down == across, row, 0).astype(jnp.float32), axis=1, keepdims=True).astype(jnp.int32)


ROW = 512
SEND_INPUT, SEND_COTANGENT, SEND_RESULT, SEND_GRAD = range(4)
FFN_SLOTS = 4
RATE = 0.3
COSTS = {
    "documents": 0.5, "start_rows": 0.5, "vectors_in": 2.0, "project": 1.0, "frozen": 1.2, "attend": 1.0,
    "attention_out": 1.0, "feed_forward": 2.0, "layer_out": 0.7,
}


class Sums:
    def __init__(self, gather, inbox, send_sem, recv_sem):
        self.gather, self.inbox, self.send_sem, self.recv_sem = gather, inbox, send_sem, recv_sem
        z, p = gather.z, gather.p
        cols = [gather.cols[name] for name in ("X", "Y", "D")]
        planes = [gather.planes[name] for name in ("i", "j", "f")]
        self.phases = [
            [(gather.sibling, 0, 0)],
            [(gather.device(z, col), 1 + p, 1 + col) for col in cols],
            [(gather.device(plane, p), 5 + z, 5 + plane) for plane in planes],
        ]
        self.own_slots = [None, 1 + p, 5 + z]
        self.ranges = [None, (1, 4), (5, 4)]
        size, slot = 1, 9
        while size < gather.sub:
            partner = gather.batch + size * (1 - 2 * ((gather.lane // size) % 2))
            self.phases.append([((partner, gather.core), slot, slot)])
            self.own_slots.append(None)
            self.ranges.append(None)
            size, slot = 2 * size, slot + 1

    def others(self):
        gather = self.gather
        found = [gather.device(gather.z, gather.cols["D"]), gather.device(gather.planes["j"], gather.p)]
        for phase in self.phases[3:]:
            found.append(phase[0][0])
        return found

    def copies(self, layer, phase, values):
        base = sum(len(moves) for moves in self.phases[:phase])
        return [
            pltpu.make_async_remote_copy(
                src_ref=values, dst_ref=self.inbox.at[layer, there], send_sem=self.send_sem.at[layer, base + number],
                recv_sem=self.recv_sem.at[layer, there], device_id=device, device_id_type=MESH,
            )
            for number, (device, there, _) in enumerate(self.phases[phase])
        ]

    def start(self, layer, phase, values):
        if self.own_slots[phase] is not None:
            self.inbox[layer, self.own_slots[phase]] = values[...]
        for copy in self.copies(layer, phase, values):
            copy.start()

    def finish(self, layer, phase, values):
        for copy, (device, _, here) in zip(self.copies(layer, phase, values), self.phases[phase]):
            copy.wait_send()
            pltpu.make_async_remote_copy(
                src_ref=values, dst_ref=self.inbox.at[layer, here], send_sem=self.send_sem.at[layer, 0],
                recv_sem=self.recv_sem.at[layer, here], device_id=device, device_id_type=MESH,
            ).wait_recv()
        if self.ranges[phase] is None:
            values[...] = values[...] + self.inbox[layer, self.phases[phase][0][2]]
        else:
            first, count = self.ranges[phase]
            values[...] = sum(self.inbox[layer, first + number] for number in range(1, count)) + self.inbox[layer, first]


def train_kernel(
    sub, span,
    weight_in, weight_out, weight_up, weight_down, basis_a, basis_b, vectors, owner_row, gains, offsets, lengths, inputs, cotangent,
    wide, full, probs, grads, grad_own, grad_swap, result_own, result_swap,
    pack, wide_pack, vec_pack, vecs, pieces, flat, trained,
    rows_low, rows, wide_v, att_v, ffn_v, qkv_v, probs_v, proj_v, proj_low, adapt_v, mixed, feed, sums_v, slopes_v,
    doc_col, doc_row, result_v, up_v, row_grads, inbox,
    send_sem, recv_sem, swap_send, swap_recv, own_sem, load_sem, save_sem, sums_send, sums_recv,
):
    gather = Gather(sub, wide_pack, pack, vec_pack, wide, full, vecs, send_sem, recv_sem)
    sums = Sums(gather, inbox, sums_send, sums_recv)
    core = gather.core
    half_rows = inputs.shape[1]
    mine = pl.ds(pl.multiple_of(core * half_rows, 16), half_rows)
    other = pl.ds(pl.multiple_of((1 - core) * half_rows, 16), half_rows)

    def swap(number, source, target):
        return pltpu.make_async_remote_copy(
            src_ref=source, dst_ref=target, send_sem=swap_send.at[number], recv_sem=swap_recv.at[number],
            device_id=gather.sibling, device_id_type=MESH,
        )

    def own(number, source, target):
        return pltpu.make_async_copy(source, target, own_sem.at[number])

    def gain(number):
        return gains[number // 2, number % 2 : number % 2 + 1, :]

    def offset(number):
        return offsets[number // 2, number % 2 : number % 2 + 1, :]

    def vector(layer, start, size):
        return trained[layer : layer + 1, start : start + size]

    greeted = gather.greet(sums.others())
    wide_pack[0] = jnp.where(core == 0, basis_a[:, :HALF], basis_a[:, HALF:])
    wide_pack[1] = basis_b[...]
    padded = jnp.concatenate([vectors[...], jnp.zeros((32, 128 - span), jnp.float32)], axis=1)
    vec_pack[...] = jnp.where(core == 0, padded[:16], padded[16:]).reshape(2, 8, 128)

    for layer in range(LAYERS):
        for part in range(3):
            pack[12 * layer + part] = weight_in[layer, part]
        pack[12 * layer + 3] = weight_out[layer]
        for part in range(4):
            columns = slice(part * HALF, (part + 1) * HALF)
            pack[12 * layer + 4 + 2 * part] = weight_up[layer, :, columns]
            pack[12 * layer + 5 + 2 * part] = weight_down[layer, :, columns]

    pl.semaphore_wait(pltpu.get_barrier_semaphore(), greeted)
    swap_in = swap(SEND_INPUT, inputs.at[1 - core], rows_low.at[mine])
    swap_cot = swap(SEND_COTANGENT, cotangent.at[1 - core], up_v.at[mine])
    own_in = own(0, inputs.at[core], rows_low.at[mine])
    own_cot = own(1, cotangent.at[core], up_v.at[mine])
    swap_in.start()
    own_in.start()

    def load_wide():
        return pltpu.make_async_copy(wide, wide_v, load_sem.at[0])

    def load_att(layer, part):
        pair = pl.ds(12 * layer + 2 * part, 2)
        return pltpu.make_async_copy(full.at[:, pair], att_v.at[:, pl.ds(2 * part, 2)], load_sem.at[1 + part])

    def load_ffn(layer, part):
        pair = pl.ds(12 * layer + 4 + 2 * part, 2)
        return pltpu.make_async_copy(full.at[:, pair], ffn_v.at[part], load_sem.at[3 + part])

    def save_probs(pair):
        return pltpu.make_async_copy(probs_v.at[pair], probs.at[pair], save_sem.at[pair])

    def load_probs(pair):
        return pltpu.make_async_copy(probs.at[pair], probs_v.at[pair], save_sem.at[pair])

    def documents():
        places_col = lax.broadcasted_iota(jnp.int32, (ROW, 128), 0)
        places_row = lax.broadcasted_iota(jnp.int32, (8, ROW), 1)
        ids_col = jnp.zeros((ROW, 128), jnp.int32)
        ids_row = jnp.zeros((8, ROW), jnp.int32)
        end = jnp.int32(0)
        for number in range(lengths.shape[2]):
            end = end + lengths[core, 0, number]
            ids_col = ids_col + (places_col >= end).astype(jnp.int32)
            ids_row = ids_row + (places_row >= end).astype(jnp.int32)
        doc_col[...] = ids_col
        doc_row[...] = ids_row

    def start_rows():
        own_in.wait()
        swap_in.wait()
        rows[...] = rows_low[...].astype(jnp.float32)

    def vectors_in():
        owner_col = as_column(owner_row[...])
        slot = owner_col * (512 // gather.owners) + piece_ranks(owner_col, owner_row[...], 1)
        place = ((slot >> 3) & 3) * 128 + (slot >> 5) * 8 + (slot & 7)
        spots = lax.broadcasted_iota(jnp.int32, (slot.shape[0], 512), 1)
        select = (place == spots).astype(jnp.float32)
        pieces[0:256, :] = exact(select, vecs[...].reshape(512, 128))
        lay_out(pieces, span, flat)
        for number in range(8):
            layer, part = divmod(number, 4)
            trained[layer : layer + 1, SPAN_LANES * part : SPAN_LANES * (part + 1)] = flat[number : number + 1, :]

    def project(layer):
        if layer == 0:
            load_wide().wait()
        proj_v[...] = mm_t(rows_low[...], beside(wide_v[0, 0], wide_v[1, 0]))
        proj_low[layer] = low(proj_v[...])

    def frozen(layer, number):
        if number != 1:
            load_att(layer, number // 2).wait()
        values = mm(rows_low[...], beside(att_v[0, number], att_v[1, number]))
        if number != 1:
            start = number // 2
            bias = vector(layer, 2 * R + start * D, D)
            scale = vector(layer, start * R, R)
            adapted = mm(low(scale * proj_v[...]), beside(wide_v[0, 1], wide_v[1, 1]))
            adapt_v[layer, start] = low(adapted)
            values = values + bias * adapted
        values = low(values)
        for pair in range(6):
            qkv_v[layer, pair, number] = values[:, 128 * pair : 128 * (pair + 1)]

    def attend(layer, pair):
        if layer > 0:
            save_probs(pair).wait()
        query = qkv_v[layer, pair, 0].astype(jnp.float32) * SCORE_SCALE
        query_t = low(query.T)
        value_t = low(qkv_v[layer, pair, 2].astype(jnp.float32).T)
        key = qkv_v[layer, pair, 1]
        ids_col = doc_col[...]
        same = jnp.concatenate([ids_col] * 4, axis=1) == doc_row[0:1, :]
        zeros = jnp.zeros((HDIM, ROW), jnp.bfloat16)
        masked = ([query_t[:HDIM], zeros], [zeros, query_t[HDIM:]])
        products = [mm(key, jnp.concatenate(parts, axis=0)) for parts in masked]
        chances = []
        for head in range(2):
            scores = jnp.where(same, products[head], MASKED_SCORE)
            raised = jnp.exp(scores - jnp.max(scores, axis=0, keepdims=True))
            chances.append(low(raised * (1.0 / jnp.sum(raised, axis=0, keepdims=True))))
            probs_v[pair, head] = chances[head]
        mixed_t = [mm(value_t[head * HDIM : (head + 1) * HDIM], chances[head]) for head in range(2)]
        mixed[:, 128 * pair : 128 * (pair + 1)] = low(jnp.concatenate(mixed_t, axis=0).T)
        if layer < LAYERS - 1:
            save_probs(pair).start()

    def attention_out(layer):
        total = rows[...] + mm_t(mixed[...], beside(att_v[0, 3], att_v[1, 3]))
        sums_v[layer, 0] = total
        middle = normalize(total, gain(2 * layer), offset(2 * layer))
        rows[...] = middle
        rows_low[...] = low(middle)

    def feed_forward(layer, part):
        load_ffn(layer, part).wait()
        before = mm(rows_low[...], beside(ffn_v[part, 0, 0], ffn_v[part, 1, 0]))
        active = []
        for half in range(2):
            values, slope = gelu_and_slope(before[:, half * HALF : (half + 1) * HALF])
            slopes_v[layer, part, half] = low(slope)
            active.append(low(values))
        term = mm_t(beside(*active), beside(ffn_v[part, 0, 1], ffn_v[part, 1, 1]))
        if part == 0:
            feed[...] = term
        else:
            feed[...] += term

    def layer_out(layer):
        total = rows[...] + feed[...]
        sums_v[layer, 1] = total
        values = normalize(total, gain(2 * layer + 1), offset(2 * layer + 1))
        if layer == LAYERS - 1:
            result_v[...] = low(values)
        else:
            rows[...] = values
            rows_low[...] = low(values)

    def ready(chunk):
        return LAG * chunk + STRIDE * (DEPTHS - 1)

    queue = []

    def add(tick, task, *arguments):
        queue.append((tick, functools.partial(task, *arguments)))

    add(0, documents)
    add(1, start_rows)
    add(ready(0), vectors_in)
    add(ready(0), project, 0)
    for layer in range(LAYERS):
        first = 1 + 6 * layer
        if layer > 0:
            add(0, project, layer)
        for number in range(3):
            add(ready(first + number // 2), frozen, layer, number)
        for pair in range(6):
            add(0, attend, layer, pair)
        add(0, attention_out, layer)
        for part in range(4):
            add(ready(first + 2 + part), feed_forward, layer, part)
        add(0, layer_out, layer)

    ffn_order = [(layer, part) for layer in range(LAYERS) for part in range(4)]
    counts = {"ffn_started": 0, "ffn_done": 0, "att_done": 0}
    att_started = set()

    def start_loads(number):
        while counts["ffn_started"] < min(len(ffn_order), counts["ffn_done"] + FFN_SLOTS):
            layer, part = ffn_order[counts["ffn_started"]]
            if ready(3 + 6 * layer + part) > number:
                break
            load_ffn(layer, part).start()
            counts["ffn_started"] += 1
        for layer in range(LAYERS):
            for part in range(2):
                if (layer, part) in att_started or ready(1 + 6 * layer + part) > number or counts["att_done"] < layer:
                    continue
                load_att(layer, part).start()
                att_started.add((layer, part))

    def run(position, number):
        task = queue[position][1]
        name = task.func.__name__
        task()
        counts["ffn_done"] += name == "feed_forward"
        counts["att_done"] += name == "attention_out"
        start_loads(number)
        return COSTS[name]

    state = {"credit": 0.0, "position": 0}

    def work(number):
        while state["position"] < len(queue) and queue[state["position"]][0] < number and state["credit"] > 0:
            state["credit"] -= run(state["position"], number - 1)
            state["position"] += 1

    for number in range(TICKS):
        for _ in gather.tick(number):
            state["credit"] = min(state["credit"] + RATE, 1.0)
            work(number)
        if number == 0:
            swap_cot.start()
            own_cot.start()
        if number == ready(0):
            load_wide().start()
        start_loads(number)
    while state["position"] < len(queue):
        run(state["position"], TICKS - 1)
        state["position"] += 1

    swap_out = swap(SEND_RESULT, result_v.at[other], result_swap)
    own_out = own(2, result_v.at[mine], result_own)
    swap_out.start()
    own_out.start()

    def feed_back(layer, part):
        if (layer, part) not in resident:
            load_ffn(layer, part).wait()
        active = mm(rows_low[...], beside(ffn_v[part, 0, 1], ffn_v[part, 1, 1]))
        slope = beside(slopes_v[layer, part, 0], slopes_v[layer, part, 1]).astype(jnp.float32)
        feed[...] += mm_t(low(active * slope), beside(ffn_v[part, 0, 0], ffn_v[part, 1, 0]))

    def attend_back(layer, pair):
        lanes = slice(128 * pair, 128 * (pair + 1))
        query, key, value = qkv_v[layer, pair, 0], qkv_v[layer, pair, 1], qkv_v[layer, pair, 2]
        outer = mixed[:, lanes]
        outer_t = low(outer.astype(jnp.float32).T)
        key_t = low(key.astype(jnp.float32).T)
        zeros = jnp.zeros((HDIM, ROW), jnp.bfloat16)
        query_t, keys, values = [], [], []
        for head in range(2):
            part = slice(head * HDIM, (head + 1) * HDIM)
            masked = [outer_t[part], zeros] if head == 0 else [zeros, outer_t[part]]
            chances_low = probs_v[pair, head]
            chances = chances_low.astype(jnp.float32)
            chance_grad = mm(value, jnp.concatenate(masked, axis=0))
            inner = jnp.sum(chances * chance_grad, axis=0, keepdims=True)
            score_grad = low(chances * (chance_grad - inner))
            values.append(mm(chances_low, outer))
            keys.append(mm(score_grad, query))
            query_t.append(mm(key_t[part], score_grad))
        left = lax.broadcasted_iota(jnp.int32, (ROW, 128), 1) < HDIM
        row_grads[0, :, lanes] = low(SCORE_SCALE * jnp.concatenate(query_t, axis=0).T)
        row_grads[1, :, lanes] = low(SCORE_SCALE * jnp.where(left, keys[0], keys[1]))
        row_grads[2, :, lanes] = low(jnp.where(left, values[0], values[1]))

    def vector_back(layer):
        found, sources = {}, []
        basis = beside(wide_v[0, 1], wide_v[1, 1])
        for start in range(2):
            row = row_grads[2 * start].astype(jnp.float32)
            sources.append(mm_t(low(vector(layer, 2 * R + start * D, D) * row), basis))
            found[2 + start] = jnp.sum(row * adapt_v[layer, start].astype(jnp.float32), axis=0, keepdims=True)
            found[start] = jnp.sum(sources[start] * proj_low[layer].astype(jnp.float32), axis=0, keepdims=True)
        number = 0
        for start in range(4):
            for tile in range(found[start].shape[1] // 128):
                grads[layer, number : number + 1, :] = found[start][:, 128 * tile : 128 * (tile + 1)]
                number += 1
        grads[layer, number:, :] = jnp.zeros((32 - number, 128), jnp.float32)
        sums.start(layer, 0, grads.at[layer])
        proj_low[layer] = low(vector(layer, 0, R) * sources[0] + vector(layer, R, R) * sources[1])

    def input_back(layer, which):
        total = rows[which, :] + mm(proj_low[layer, which], beside(wide_v[0, 0], wide_v[1, 0]))
        for number in range(3):
            total = total + mm_t(row_grads[number, which, :], beside(att_v[0, number], att_v[1, number]))
        rows[which, :] = total

    last = LAYERS - 1
    resident = {(last, part) for part in range(4)}
    own_cot.wait()
    swap_cot.wait()
    rows[...] = up_v[...].astype(jnp.float32)
    phases = len(sums.phases)
    pending = []
    for layer in reversed(range(LAYERS)):
        values = norm_back(sums_v[layer, 1], gain(2 * layer + 1), rows[...])
        rows_low[...] = low(values)
        feed[...] = values
        for part in reversed(range(4)):
            feed_back(layer, part)
            if layer > 0:
                load_ffn(layer - 1, part).start()
            if pending:
                pending.pop(0)()
        values = norm_back(sums_v[layer, 0], gain(2 * layer), feed[...])
        rows[...] = values
        rows_low[...] = low(values)
        if layer < last:
            for part in range(2):
                load_att(layer, part).wait()
        mixed[...] = low(mm(rows_low[...], beside(att_v[0, 3], att_v[1, 3])))
        for pair in range(6):
            if layer < last:
                load_probs(pair).wait()
            attend_back(layer, pair)
            if layer > 0:
                load_probs(pair).start()
            if pending:
                pending.pop(0)()
        vector_back(layer)
        values = grads.at[layer]

        def advance(layer, phase, values):
            sums.finish(layer, phase, values)
            if phase + 1 < phases:
                sums.start(layer, phase + 1, values)

        steps = [functools.partial(advance, layer, phase, values) for phase in range(phases)]
        if layer > 0:
            input_back(layer, slice(None))
            for part in range(2):
                load_att(layer - 1, part).start()
            pending = steps
        else:
            while pending:
                pending.pop(0)()
            gather.finish()
            input_back(layer, other)
            swap_grad = swap(SEND_GRAD, rows.at[other], grad_swap)
            swap_grad.start()
            steps.pop(0)()
            input_back(layer, mine)
            own_grad = own(3, rows.at[mine], grad_own)
            own_grad.start()
            for step in steps:
                step()

    own_out.wait()
    swap_out.wait()
    own_grad.wait()
    swap_grad.wait()


def train(sub, span, shards, owner_row, gains, offsets, lengths, inputs, cotangent):
    anywhere = pl.BlockSpec(memory_space=pl.ANY)
    on_chip = pl.BlockSpec(memory_space=pltpu.VMEM)
    scalars = pl.BlockSpec(memory_space=pltpu.SMEM)
    shape = jax.ShapeDtypeStruct
    bf16, f32 = jnp.bfloat16, jnp.float32
    vmem = pltpu.VMEM
    dma = pltpu.SemaphoreType.DMA
    half_rows = inputs.shape[1]
    slots = 9 + (sub.bit_length() - 1)
    return pl.pallas_call(
        functools.partial(train_kernel, sub, span),
        out_shape=(
            shape((2, 2, R, HALF), bf16),
            shape((2, BLOCKS, D, HALF), bf16),
            shape((6, 2, ROW, ROW), bf16),
            shape((LAYERS, 32, 128), f32),
            shape((half_rows, D), f32),
            shape((half_rows, D), f32),
            shape((half_rows, D), bf16),
            shape((half_rows, D), bf16),
        ),
        in_specs=[on_chip] * 10 + [scalars] + [anywhere] * 2,
        out_specs=[anywhere] * 3 + [on_chip] + [anywhere] * 4,
        scratch_shapes=[
            vmem((BLOCKS, D // GROUPS, HALF), bf16),
            vmem((2, 64, HALF), bf16),
            vmem((2, 8, 128), f32),
            vmem((2, 2, 128, 128), f32),
            vmem((288, 128), f32),
            vmem((8, SPAN_LANES), f32),
            vmem((LAYERS, 4 * SPAN_LANES), f32),
            vmem((ROW, D), bf16),
            vmem((ROW, D), f32),
            vmem((2, 2, R, HALF), bf16),
            vmem((2, 4, D, HALF), bf16),
            vmem((4, 2, 2, D, HALF), bf16),
            vmem((LAYERS, 6, 3, ROW, 128), bf16),
            vmem((6, 2, ROW, ROW), bf16),
            vmem((ROW, R), f32),
            vmem((LAYERS, ROW, R), bf16),
            vmem((LAYERS, 2, ROW, D), bf16),
            vmem((ROW, D), bf16),
            vmem((ROW, D), f32),
            vmem((LAYERS, 2, ROW, D), f32),
            vmem((LAYERS, 4, 2, ROW, HALF), bf16),
            vmem((ROW, 128), jnp.int32),
            vmem((8, ROW), jnp.int32),
            vmem((ROW, D), bf16),
            vmem((ROW, D), bf16),
            vmem((3, ROW, D), bf16),
            vmem((LAYERS, slots, 32, 128), f32),
            dma((CHUNKS + 1, 6)),
            dma((CHUNKS + 1, len(ARRIVALS) + 1)),
            dma((4,)),
            dma((4,)),
            dma((4,)),
            dma((7,)),
            dma((6,)),
            dma((LAYERS, slots)),
            dma((LAYERS, slots)),
        ],
        compiler_params=pltpu.CompilerParams(
            collective_id=0, has_side_effects=True, vmem_limit_bytes=63 * 1024 * 1024
        ),
        cost_estimate=pl.CostEstimate(flops=4 * 10**10, bytes_accessed=10**8, transcendentals=10**7),
    )(*shards, owner_row, gains, offsets, lengths, inputs, cotangent)


def update_kernel(
    span,
    grads, owner_row, vectors, first_moment, second_moment, grad_own, grad_swap, result_own, result_swap,
    results, input_grads, own_grad, new_one, new_two, updated, updated_low,
    flat, pieces, grad_rows, result_rows, load_sem, store_sem,
):
    core = lax.axis_index("tensor")
    batch = lax.axis_index("batch")
    half = grad_own.shape[0] // 2
    loads, stores = [], []
    for source, staged, target, place in (
        (grad_own, grad_rows, input_grads, core),
        (grad_swap, grad_rows, input_grads, 1 - core),
        (result_own, result_rows, results, core),
        (result_swap, result_rows, results, 1 - core),
    ):
        for start in (0, half):
            rows, number = pl.ds(start, half), len(loads)
            there = staged.at[number // 2 % 2, rows]
            loads.append(pltpu.make_async_copy(source.at[rows], there, load_sem.at[number]))
            stores.append(pltpu.make_async_copy(there, target.at[place, rows], store_sem.at[number]))
    for load in loads:
        load.start()
    flat[0:28, :] = grads[0, 0:28, :]
    flat[28:56, :] = grads[1, 0:28, :]
    cut_up(flat, span, pieces)
    for load, store in zip(loads, stores):
        load.wait()
        store.start()
    slots = vectors.shape[0]
    count = owner_row.shape[1]
    owner_col = as_column(owner_row[...])
    rank = piece_ranks(owner_col, owner_row[...], 0)
    numbers = lax.broadcasted_iota(jnp.int32, (slots, count), 0)
    select = ((rank == numbers) & (owner_row[...] == batch)).astype(jnp.float32)
    filled = jnp.sum(select, axis=1, keepdims=True)
    gathered = exact(select, pieces[0:256, :])[:, :span]
    one = (FIRST_BETA * first_moment[...] + (1.0 - FIRST_BETA) * gathered) * filled
    two = (SECOND_BETA * second_moment[...] + (1.0 - SECOND_BETA) * gathered * gathered) * filled
    fixed_one = one / (1.0 - FIRST_BETA**STEP)
    fixed_two = two / (1.0 - SECOND_BETA**STEP)
    old = vectors[...]
    new = (
        old - LEARN_RATE * (fixed_one / (jnp.sqrt(fixed_two) + ADAM_EPSILON) + WEIGHT_DECAY * old)
    ) * filled
    own_grad[...] = gathered
    new_one[...] = one
    new_two[...] = two
    updated[...] = new
    updated_low[...] = low(new)
    for store in stores:
        store.wait()


def update(grads, owner_row, vectors, first_moment, second_moment, grad_own, grad_swap, result_own, result_swap):
    anywhere = pl.BlockSpec(memory_space=pl.ANY)
    on_chip = pl.BlockSpec(memory_space=pltpu.VMEM)
    half_rows = grad_own.shape[0]
    slot = jax.ShapeDtypeStruct(vectors.shape, jnp.float32)
    return pl.pallas_call(
        functools.partial(update_kernel, vectors.shape[1]),
        out_shape=(
            jax.ShapeDtypeStruct((2, half_rows, D), jnp.bfloat16),
            jax.ShapeDtypeStruct((2, half_rows, D), jnp.float32),
            slot, slot, slot, slot, jax.ShapeDtypeStruct(vectors.shape, jnp.bfloat16),
        ),
        in_specs=[on_chip] * 5 + [anywhere] * 4,
        out_specs=[anywhere] * 2 + [on_chip] * 5,
        scratch_shapes=[
            pltpu.VMEM((64, 128), jnp.float32),
            pltpu.VMEM((288, 128), jnp.float32),
            pltpu.VMEM((2, half_rows, D), jnp.float32),
            pltpu.VMEM((2, half_rows, D), jnp.bfloat16),
            pltpu.SemaphoreType.DMA((8,)),
            pltpu.SemaphoreType.DMA((8,)),
        ],
    )(grads, owner_row, vectors, first_moment, second_moment, grad_own, grad_swap, result_own, result_swap)


def on_device(
    inputs, cotangent, lengths, owners, vectors, first_moment, second_moment,
    weight_in, weight_out, weight_up, weight_down, basis_a, basis_b, norm_gain, norm_bias,
):
    sub = lax.axis_size("batch") // GROUPS
    span = vectors.shape[1]
    owner_row = owners[None, :]
    shards = (
        group_rows(jnp.swapaxes(weight_in, 1, 2), 2, D // GROUPS, sub),
        group_rows(jnp.swapaxes(weight_out, 1, 2), 1, D // GROUPS, sub),
        group_rows(weight_up, 1, D // GROUPS, sub),
        group_rows(jnp.swapaxes(weight_down, 1, 2), 1, D // GROUPS, sub),
        group_rows(basis_a, 0, R // GROUPS, sub),
        group_rows(basis_b.T, 0, R // GROUPS, sub),
        group_rows(vectors, 0, 512 // GROUPS, sub),
    )
    _, _, _, grads, grad_own, grad_swap, result_own, result_swap = train(
        sub, span, shards, owner_row, norm_gain, norm_bias, lengths, inputs, cotangent
    )
    return update(
        grads, owner_row, vectors, first_moment, second_moment, grad_own, grad_swap, result_own, result_swap
    )


def solution(mesh):
    rows_spec = P(None, ("batch", "tensor"), None)
    split = P("batch", None)
    return jax.shard_map(
        on_device,
        mesh=mesh,
        in_specs=(
            rows_spec, rows_spec, P(None, "batch", None), P(), split, split, split,
            P(None, "batch", None, "tensor"), P(None, "tensor", "batch"), P(None, "batch", "tensor"),
            P(None, "tensor", "batch"), split, P("tensor", "batch"), P(), P(),
        ),
        out_specs=(rows_spec, rows_spec, split, split, split, split, split),
        check_vma=False,
    )
```
